32 devices in a mesh: panel: 2 (over x), rad: 2 (over y), ang: 8 (over z, core).
Axes of the slice: x: 2, y: 2, z: 4, core: 2. Of those that a mesh axis runs over, the one named last changes fastest.
Arguments:
- adj_final: float32 [2, 7, 2, 64, 1536], P('panel', None, 'rad', 'ang'), may hold values from -6 to 6
- cond: float32 [2, 2, 64, 1536], P('panel', 'rad', 'ang'), may hold values from 0.5 to 1.5
- diffus: float32 [7], replicated, may hold values from 0.02 to 0.1
- couple: float32 [7, 7], replicated, may hold values from -0.1 to 0.1
- ghost_row: int32 [2, 4, 64], replicated, may hold values from 0 to 63
- ghost_col: int32 [2, 4, 64], replicated, may hold values from 0 to 1535
- ghost_wt: float32 [2, 4, 64], replicated, may hold values from 0.5 to 1.5
- obs_dest: int32 [2, 2, 2048, 1], P('panel', 'rad', 'ang'), may hold values from 0 to 7; in each aligned block of 256 rows (0 to 255, 256 to 511, ..., all dimensions but the last counted through in order) at most 64 rows name the same one
- obs_cell: int32 [2, 2, 4, 2048], P('panel', 'rad', None, 'ang'), may hold values from 0 to 12287
- obs_wt: float32 [2, 2, 4, 2048], P('panel', 'rad', None, 'ang'), may hold values from 0.2 to 1
- misfit: float32 [2, 2, 2, 2048], P('panel', 'rad', None, 'ang'), may hold values from -6 to 6
Outputs:
- adj_start: float32 [2, 7, 2, 64, 1536], P('panel', None, 'rad', 'ang')
The draws below stay inside these ranges and needn't reach their ends.
Inputs may be any that keep to these rules, and one draw needn't show every extreme that they name: `obs_dest`: owner tile, within the observation's own panel, whose outermost layer holds it; among the 256 observations of one device at most 64 name one owner. `obs_cell`: row within the owner's tile times 1536 plus column.
All inputs are finite; a program needn't handle non-finite values.
Results may differ from the reference program's by a relative error of at most 0.000088.
Values sent between devices are 32-bit elements; how exact they have to be, the bound alone decides.
No kernel may reach another device: no remote copies, remote signals or barrier semaphores. Data moves between devices by JAX's collectives and lax.ppermute only.
A program may use at most 64 MiB of HBM per device.

```python
import math
import jax
import jax.numpy as jnp
import numpy as np
from jax import lax

FIELDS = 7
TH_DEV = 8
PH = 1536
OBS_DEV = 256
TILES = 8
RGROUPS = 2
NR = 2
NT = 64
NOBS = 2048
CAP = 64


def touch_ends(drawn, stream_key, smallest, high):
    longest = drawn.shape.index(max(drawn.shape))
    spots = []
    for shift in (0, 1):
        where = [jax.random.randint(jax.random.fold_in(stream_key, axis), (), 0, length) for axis, length in enumerate(drawn.shape)]
        where[longest] = (where[longest] + shift) % drawn.shape[longest]
        spots.append(tuple(where))
    return drawn.at[spots[0]].set(smallest).at[spots[1]].set(high)


def block_levels(key, dims, shards, smallest, high):
    factor_of = 1.0
    for position, parts in shards:
        steps = jax.random.uniform(jax.random.fold_in(jax.random.fold_in(key, 6), position), (parts,), jnp.float32, smallest / len(shards), high / len(shards))
        factor_of = factor_of * jnp.repeat(jnp.exp(steps), dims[position] // parts).reshape((-1,) + (1,) * (len(dims) - 1 - position))
    return factor_of


def routed_block(rng, own, number, rows, count, top, limit, slope):
    sequence = jax.random.permutation(rng, count)
    packed, usual = portions_of(count, rows * top, limit, slope, True), portions_of(count, rows * top, limit, slope, False)
    places = jnp.arange(count)

    def named(tallies, rotation):
        used = int((tallies > 0).sum())
        fixed = max(1, used // 4)
        moved = fixed + (places - fixed + rotation * (used - fixed)) % max(1, count - fixed)
        return jnp.zeros((count,), jnp.int32).at[sequence[jnp.where(places < fixed, places, moved)]].set(jnp.asarray(tallies, jnp.int32))

    tallies = jnp.where(number % 4 == 0, named(packed, number // 4), named(usual, number - number // 4 - 1))
    mixed = jax.random.permutation(jax.random.fold_in(own, 3), count)
    giver, sink = mixed[0:count // 2 * 2:2], mixed[1:count // 2 * 2:2]
    margin = jnp.minimum(tallies[giver] - 1, limit - tallies[sink]) // 2
    margin = jnp.where((giver == sequence[0]) | (sink == sequence[0]) | (tallies[sink] == 0), 0, jnp.maximum(margin, 0))
    moved = jax.random.randint(jax.random.fold_in(own, 4), (count // 2,), 0, 1 << 20) % (margin + 1)
    tallies = tallies.at[giver].add(-moved).at[sink].add(moved)
    labels = jnp.searchsorted(jnp.cumsum(tallies), jnp.arange(rows * top), side="right").astype(jnp.int32)
    grid = labels.reshape(top, rows).T
    grid = grid[jax.random.permutation(jax.random.fold_in(own, 1), rows)]
    rotation = jax.random.randint(jax.random.fold_in(own, 2), (rows, 1), 0, top)
    return jnp.take_along_axis(grid, (jnp.arange(top)[None, :] + rotation) % top, axis=1)


def portions_of(amount, total, reach, skew, full):
    portions = [(1 << 20) // math.isqrt(standing ** skew) + 1 for standing in range(1, amount + 1)]
    largest = reach if full else min(reach, max(-(-total // amount), total * portions[0] // sum(portions)))
    least = 1 if total - largest >= amount - 1 else 0
    holding, rest = [largest] + [least] * (amount - 1), total - largest - least * (amount - 1)
    while rest > 0:
        free = [i for i in range(1, amount) if holding[i] < largest] or [i for i in range(1, amount) if holding[i] < reach]
        pool, remaining = sum([portions[i] for i in free]), rest
        for i in free:
            addition = min(reach - holding[i], max(1, remaining * portions[i] // pool), rest)
            holding[i] = holding[i] + addition
            rest = rest - addition
    return np.array(holding)


def noise(stream_key, extent, scale, limit, cuts=(), dtype=jnp.bfloat16):
    loudness = block_levels(stream_key, extent, cuts, -0.22, 0.18) if cuts else 1.0
    values = jax.random.normal(stream_key, extent, jnp.float32) * scale * loudness
    return jnp.minimum(jnp.maximum(values, -limit), limit).astype(dtype)


def setup_inputs(seed: int = 0) -> dict:
    splits = jax.random.split(jax.random.key(seed), 12)
    adj_final = noise(splits[0], (2, FIELDS, NR, NT, PH), 1.0, 6.0, ((0, 2), (2, 2), (3, 8)), jnp.float32)
    cond = jnp.clip(jnp.exp(math.log(1.5) - 1.0986123 * jax.random.uniform(splits[1], (2, NR, NT, PH), jnp.float32) ** block_levels(splits[1], (2, NR, NT, PH), ((0, 2), (1, 2), (2, 8)), -0.2, 0.2)), 0.5, 1.5)
    diffus = jnp.clip(jnp.exp(jax.random.uniform(splits[2], (FIELDS,), jnp.float32, math.log(0.02), math.log(0.1))), 0.02, 0.1)
    couple = jnp.clip(jax.random.uniform(splits[3], (FIELDS, FIELDS), jnp.float32, -0.1, 0.1), -0.1, 0.1)
    ghost_row = touch_ends(jax.random.randint(splits[4], (2, 4, NT), 0, NT), jax.random.fold_in(splits[4], 1), 0, NT - 1).astype(jnp.int32)
    ghost_col = touch_ends(jax.random.randint(splits[5], (2, 4, NT), 0, PH), jax.random.fold_in(splits[5], 1), 0, PH - 1).astype(jnp.int32)
    ghost_wt = jnp.clip(jax.random.uniform(splits[6], (2, 4, NT), jnp.float32, 0.5, 1.5), 0.5, 1.5)
    obs_dest_keys = jax.random.split(jax.random.fold_in(splits[7], 1), 2 * RGROUPS * NOBS // OBS_DEV)
    obs_dest_turns = jax.random.permutation(jax.random.fold_in(splits[7], 3), 2 * RGROUPS * NOBS // OBS_DEV)
    obs_dest = jax.vmap(lambda own, number: routed_block(jax.random.fold_in(splits[7], 2), own, number, OBS_DEV, TILES, 1, CAP, 2))(obs_dest_keys, obs_dest_turns).reshape((2, RGROUPS, NOBS, 1))
    obs_cell = touch_ends(jax.random.randint(splits[8], (2, RGROUPS, 4, NOBS), 0, TH_DEV * PH), jax.random.fold_in(splits[8], 1), 0, (TH_DEV * PH) - 1).astype(jnp.int32)
    obs_wt = jnp.clip(0.2 + 0.8 * jax.random.uniform(splits[9], (2, RGROUPS, 4, NOBS), jnp.float32) ** block_levels(splits[9], (2, RGROUPS, 4, NOBS), ((0, 2), (1, 2), (3, 8)), -0.2, 0.2), 0.2, 1.0)
    misfit = noise(splits[10], (2, RGROUPS, 2, NOBS), 1.0, 6.0, ((0, 2), (1, 2), (3, 8)), jnp.float32)
    return dict(adj_final=adj_final, cond=cond, diffus=diffus, couple=couple, ghost_row=ghost_row, ghost_col=ghost_col, ghost_wt=ghost_wt, obs_dest=obs_dest, obs_cell=obs_cell, obs_wt=obs_wt, misfit=misfit)


def laplace(scaled):
    padded = jnp.pad(scaled, ((0, 0), (0, 0), (1, 1), (1, 1), (1, 1)))
    total = padded[:, :, 2:, 1:-1, 1:-1] + padded[:, :, :-2, 1:-1, 1:-1]
    total = total + padded[:, :, 1:-1, 2:, 1:-1] + padded[:, :, 1:-1, :-2, 1:-1]
    total = total + padded[:, :, 1:-1, 1:-1, 2:] + padded[:, :, 1:-1, 1:-1, :-2]
    return total - 6.0 * scaled


def ghost_panel(other, ghost_row, ghost_col, ghost_wt):
    fields, layers, rows, columns = other.shape
    edges = jnp.stack([other[..., 0], other[..., -1]], axis=2)
    values = edges[:, :, :, None, :] * ghost_wt[None, None]
    flat_index = (ghost_row * columns + ghost_col).reshape(-1)
    target = jnp.zeros((fields, layers, rows * columns), jnp.float32)
    target = target.at[:, :, flat_index].add(values.reshape(fields, layers, -1))
    return target.reshape(fields, layers, rows, columns)


def surface_forcing(obs_dest, obs_cell, obs_wt, misfit):
    panels = []
    for panel_index in range(2):
        owners = obs_dest[panel_index, :, :, 0]
        cells = obs_cell[panel_index]
        row_index = owners[:, None, :] * TH_DEV + cells // PH
        flat_index = row_index * PH + cells % PH
        values = misfit[panel_index][:, :, None, :] * obs_wt[panel_index][:, None, :, :]
        values = jnp.transpose(values, (1, 0, 2, 3)).reshape(2, -1)
        target = jnp.zeros((2, NT * PH), jnp.float32)
        target = target.at[:, flat_index.reshape(-1)].add(values)
        panels.append(target)
    return jnp.stack(panels)


def adjoint_step(adjoint, coeff, couple, ghost_row, ghost_col, ghost_wt, source):
    scaled = coeff * adjoint
    lap = laplace(scaled)
    ghost = jnp.stack([ghost_panel(scaled[1], ghost_row, ghost_col, ghost_wt),
                       ghost_panel(scaled[0], ghost_row, ghost_col, ghost_wt)])
    coupled = jnp.einsum("ec,pelrk->pclrk", couple, adjoint, precision=lax.Precision.HIGHEST)
    updated = adjoint + lap + ghost + coupled
    return updated.at[:, 3, NR - 1].add(source)


def reference(adj_final, cond, diffus, couple, ghost_row, ghost_col, ghost_wt, obs_dest, obs_cell, obs_wt, misfit):
    forcing = surface_forcing(obs_dest, obs_cell, obs_wt, misfit)
    coeff = diffus[None, :, None, None, None] * cond[:, None]
    first = adjoint_step(adj_final, coeff, couple, ghost_row, ghost_col, ghost_wt,
                         forcing[:, 1].reshape(2, NT, PH))
    return adjoint_step(first, coeff, couple, ghost_row, ghost_col, ghost_wt,
                        forcing[:, 0].reshape(2, NT, PH))
```

```python
import functools

import jax
import jax.numpy as jnp
from jax import lax
from jax.experimental import pallas as pl
from jax.experimental.pallas import tpu as pltpu
from jax.sharding import PartitionSpec as P

LANES = 128
SUBL = 8
POINTS = 4
TIMES = 2
LOW = 256
F32 = jnp.float32
BF16 = jnp.bfloat16
NT_DIMS = (((1,), (1,)), ((), ()))


def parts_of(x, count):
    parts = []
    for _ in range(count):
        part = x.astype(BF16)
        parts.append(part)
        x = x - part.astype(F32)
    return parts


def split_dot(x, onehot, count, dims):
    total = None
    for part in parts_of(x, count):
        term = lax.dot_general(part, onehot, dims, preferred_element_type=F32)
        total = term if total is None else total + term
    return total


def iota(shape, dim):
    return lax.broadcasted_iota(jnp.int32, shape, dim)


class Sizes:
    def __init__(self, adj, obs_cell, ghost_row):
        self.fields, self.rows, self.cols = adj.shape[1], adj.shape[3], adj.shape[4]
        self.panels = lax.axis_size("panel")
        self.rads = lax.axis_size("rad")
        self.tiles = lax.axis_size("ang")
        self.devices = self.panels * self.rads * self.tiles
        self.total_rows = self.tiles * self.rows
        self.edge = 2 * self.total_rows
        self.count = obs_cell.shape[-1]
        self.slots = 2 * self.count // self.tiles
        self.spr = min(POINTS, LANES // self.slots)
        self.npr = POINTS // self.spr
        self.feat_rows = 2 * self.npr + 1
        self.edge_rows = self.edge // LANES
        self.strip = self.feat_rows + self.edge_rows
        self.block = -(-(self.strip + 2) // SUBL) * SUBL
        self.stencil = ghost_row.shape[1]
        self.hi = self.rows * self.cols // LOW
        self.pair = self.rads == 2


def rolled(x, shift, axis):
    size = x.shape[axis]
    shift = shift % size
    return x if shift == 0 else pltpu.roll(x, shift, axis)


def pack_kernel(z, adj, cond, diffus, dest, cell, wt, misfit, pay, up, down):
    for f in range(z.fields):
        s = adj[0, f, 0] * (cond[0, 0] * diffus[f])
        up[f : f + 1, :] = s[z.rows - 1 :, :]
        down[f : f + 1, :] = s[:1, :]
    up[z.fields :, :] = jnp.zeros((SUBL - z.fields, z.cols), F32)
    down[z.fields :, :] = jnp.zeros((SUBL - z.fields, z.cols), F32)

    owner = dest[...]
    height = max(16, z.tiles)
    mine = (iota((height, z.count), 0) == owner).astype(F32)
    earlier = (iota((z.count, z.count), 0) < iota((z.count, z.count), 1)).astype(F32)
    ranks = jnp.dot(mine.astype(BF16), earlier.astype(BF16), preferred_element_type=F32)
    rank = jnp.sum(ranks * mine, axis=0, keepdims=True)
    place = owner * LANES + rank.astype(jnp.int32)
    spread = (iota((z.tiles * LANES, z.count), 0) == place).astype(F32).astype(BF16)

    where = cell[0, 0]
    row = ((where.astype(F32) + 0.5) * (1.0 / z.cols)).astype(jnp.int32)
    col = where - row * z.cols
    code = ((col // LOW) * z.rows + row) * LOW + col % LOW
    code = code.astype(F32)
    weight = wt[0, 0]
    mis = misfit[0, 0]
    feats = []
    for g in range(z.spr):
        picked = [weight[h * z.spr + g : h * z.spr + g + 1] for h in range(z.npr)]
        picked += [code[h * z.spr + g : h * z.spr + g + 1] for h in range(z.npr)]
        picked.append(mis[g : g + 1] if g < TIMES else jnp.zeros((1, z.count), F32))
        feats += picked
    used = len(feats)
    padded = -(-used // 16) * 16
    if padded > used:
        feats.append(jnp.zeros((padded - used, z.count), F32))
    boxed = split_dot(jnp.concatenate(feats, axis=0), spread, 3, NT_DIMS)
    slots = boxed[: z.feat_rows]
    for g in range(1, z.spr):
        slots = slots + rolled(boxed[g * z.feat_rows : (g + 1) * z.feat_rows], g * z.slots, 1)

    full_row = owner * z.rows + row
    edge_at = jnp.where(col == 0, full_row, jnp.where(col == z.cols - 1, z.total_rows + full_row, -1))
    total = None
    for s in range(POINTS):
        value = mis[1:2] * weight[s : s + 1]
        value = jnp.concatenate([value, jnp.zeros((15, z.count), F32)], axis=0)
        hits = (iota((z.edge, z.count), 0) == edge_at[s : s + 1]).astype(F32).astype(BF16)
        term = split_dot(value, hits, 3, NT_DIMS)
        total = term if total is None else total + term
    edge_force = total[:1]

    lane = iota((z.rows, LANES), 1)
    sub = iota((z.rows, LANES), 0)
    strips = []
    for side in range(2):
        acc = jnp.zeros((z.rows, LANES), F32)
        for f in range(z.fields + 1):
            for inner in range(2):
                at = inner if side == 0 else z.cols - 1 - inner
                line = adj[0, f, 0, :, at : at + 1] if f < z.fields else cond[0, 0, :, at : at + 1]
                acc = jnp.where(lane == (f * 2 + inner) * z.rows + sub, line, acc)
        strips.append(jnp.sum(acc, axis=0, keepdims=True))

    common = [edge_force[:, k * LANES : (k + 1) * LANES] for k in range(z.edge_rows)] + strips
    spare = z.block - z.strip - 2
    if spare:
        common.append(jnp.zeros((spare, LANES), F32))
    common = jnp.concatenate(common, axis=0)
    for t in range(z.tiles):
        part = jnp.concatenate([slots[:, t * LANES : (t + 1) * LANES], common], axis=0)
        for group in range(z.panels * z.rads):
            pay[group * z.tiles + t] = part


def by_field(z, scalar, width):
    sub = iota((SUBL, width), 0)
    out = jnp.zeros((SUBL, width), F32)
    for f in range(z.fields):
        out = jnp.where(sub == f, scalar(f), out)
    return out


def unpack_strips(z, recv, sets):
    height = 2 * z.tiles
    stacked = []
    for panel, rad in sets:
        base = (panel * z.rads + rad) * z.tiles * z.block + z.strip
        for side in range(2):
            stacked.append(recv[pl.ds(base + side, z.tiles, stride=z.block), :])
    stacked = jnp.concatenate(stacked, axis=0)
    width = 2 * SUBL * z.edge
    lane = iota((LANES, width), 1)
    slot = lane // z.edge
    inner, plane = slot // SUBL, slot % SUBL
    picks = (iota((LANES, width), 0) == (plane * 2 + inner) * z.rows + lane % z.rows).astype(F32)
    moved = split_dot(stacked, picks.astype(BF16), 3, (((1,), (0,)), ((), ())))
    lane = iota((height, z.edge), 1)
    keep = lane // z.rows == iota((height, z.edge), 0)
    out = []
    for number in range(len(sets)):
        both = []
        for inner in range(2):
            rows = []
            for f in range(z.fields + 1):
                at = (inner * SUBL + f) * z.edge
                tile = moved[number * height : (number + 1) * height, at : at + z.edge]
                rows.append(jnp.sum(jnp.where(keep, tile, 0.0), axis=0, keepdims=True))
            both.append(jnp.concatenate(rows, axis=0))
        out.append(both)
    return out


def edge_scaled(z, values, dif):
    return values * values[z.fields : z.fields + 1] * dif


def coupled(z, couple, state, c):
    total = None
    for e in range(z.fields):
        term = state(e) * couple[e, c]
        total = term if total is None else total + term
    return total


def line_of(ref, s, q):
    return jnp.concatenate([ref[side, q : q + 1, :] for side in range(2)], axis=1) if s is None else ref[s, q : q + 1, :]


def deposit(z, recv, panel, spread_a, spread_b):
    sources = z.rads * z.tiles
    base = panel * sources * z.block
    feat = [recv[pl.ds(base + k, sources, stride=z.block), :] for k in range(z.feat_rows)]
    lane = iota((sources, LANES), 1)
    scaled = []
    for t in range(TIMES):
        mis = jnp.where(lane // z.slots == t, feat[2 * z.npr], 0.0)
        full = None
        for g in range(z.spr):
            term = rolled(mis, (g - t) * z.slots, 1)
            full = term if full is None else full + term
        scaled.append(full)
    sub_hi = iota((z.hi, LANES), 0)
    sub_lo = iota((LOW, LANES), 0)
    for h in range(z.npr):
        code = feat[z.npr + h].astype(jnp.int32)
        high, low = code // LOW, code % LOW
        parts = []
        for t in range(TIMES):
            parts += [p.astype(F32) for p in parts_of(scaled[t] * feat[h], 2)]
        for n in range(sources):
            at = (n * z.npr + h) * LANES
            hit = sub_hi == high[n : n + 1]
            for k, part in enumerate(parts):
                spread_a[k * z.hi : (k + 1) * z.hi, at : at + LANES] = jnp.where(hit, part[n : n + 1], 0.0).astype(BF16)
            spread_b[:, at : at + LANES] = (sub_lo == low[n : n + 1]).astype(F32).astype(BF16)
    grid = lax.dot_general(spread_a[...], spread_b[...], NT_DIMS, preferred_element_type=F32)
    out = []
    for t in range(TIMES):
        both = grid[2 * t * z.hi : (2 * t + 1) * z.hi] + grid[(2 * t + 1) * z.hi : (2 * t + 2) * z.hi]
        out.append(jnp.concatenate([both[k * z.rows : (k + 1) * z.rows] for k in range(z.cols // LOW)], axis=1))
    return out


def sideways(s):
    cols = s.shape[1]
    lane = iota(s.shape, 1)
    west = jnp.where(lane == 0, 0.0, pltpu.roll(s, 1, 1))
    east = jnp.where(lane == cols - 1, 0.0, pltpu.roll(s, cols - 1, 1))
    return west + east


def upright(s, above, below):
    rows = s.shape[0]
    sub = iota(s.shape, 0)
    north = jnp.where(sub == 0, above, pltpu.roll(s, 1, 0))
    south = jnp.where(sub == rows - 1, below, pltpu.roll(s, rows - 1, 0))
    return north + south


def first_kernel(z, adj, cond, *refs):
    if z.pair:
        adj2, cond2, *refs = refs
    else:
        beside, *refs = refs
    above, below, recv, diffus, couple, grow, gcol, gwt, *refs = refs
    first, base, up, down, spread_a, spread_b = refs
    panel, rad, tile = lax.axis_index("panel"), lax.axis_index("rad"), lax.axis_index("ang")
    other = 1 - panel
    outer = jnp.where(rad == z.rads - 1, 1.0, 0.0)

    sets = [(other, rad), (panel, rad)]
    if z.pair:
        sets.append((other, 1 - rad))
        near = [1.0]
    else:
        sets += [(other, jnp.maximum(rad - 1, 0)), (other, jnp.minimum(rad + 1, z.rads - 1))]
        near = [jnp.where(rad > 0, 1.0, 0.0), jnp.where(rad < z.rads - 1, 1.0, 0.0)]
    strips = unpack_strips(z, recv, sets)
    dif = by_field(z, lambda f: diffus[f], z.edge)
    rim, inside = strips[0]
    rim_s = edge_scaled(z, rim, dif)
    home_s = edge_scaled(z, strips[1][0], dif)
    layers_s = [edge_scaled(z, strips[2 + k][0], dif) for k in range(len(near))]
    lap = edge_scaled(z, inside, dif) - 6.0 * rim_s
    for k, one in enumerate(near):
        lap = lap + layers_s[k] * one
    spot = iota((SUBL, z.edge), 1) % z.total_rows
    lap = lap + jnp.where(spot == 0, 0.0, pltpu.roll(rim_s, 1, 1))
    lap = lap + jnp.where(spot == z.total_rows - 1, 0.0, pltpu.roll(rim_s, z.edge - 1, 1))
    rows = [coupled(z, couple, lambda e: rim[e : e + 1], c) for c in range(z.fields)]
    mixed = jnp.concatenate(rows + [jnp.zeros((SUBL - z.fields, z.edge), F32)], axis=0)

    g_row = [line_of(grow, None, q) for q in range(z.stencil)]
    g_col = [line_of(gcol, None, q) for q in range(z.stencil)]
    g_wt = [line_of(gwt, None, q) for q in range(z.stencil)]
    rim_ghost = None
    for q in range(z.stencil):
        target = jnp.where(
            g_col[q] == 0, g_row[q], jnp.where(g_col[q] == z.cols - 1, z.total_rows + g_row[q], -1)
        )
        hits = (iota((z.edge, z.edge), 0) == target).astype(F32).astype(BF16)
        values = jnp.concatenate([home_s * g_wt[q], jnp.zeros((SUBL, z.edge), F32)], axis=0)
        term = split_dot(values, hits, 3, NT_DIMS)
        rim_ghost = term if rim_ghost is None else rim_ghost + term
    sources = z.rads * z.tiles
    force = []
    for k in range(z.edge_rows):
        at = other * sources * z.block + z.feat_rows + k
        force.append(jnp.sum(recv[pl.ds(at, sources, stride=z.block), :], axis=0, keepdims=True))
    force = jnp.concatenate(force, axis=1) * outer
    rim_first = rim + lap + mixed + rim_ghost[:SUBL]
    rim_first = rim_first + jnp.where(iota((SUBL, z.edge), 0) == 3, force, 0.0)
    rim_second = rim_first * rim[z.fields : z.fields + 1] * dif

    row0 = tile * z.rows
    aimed = [jnp.where(iota((z.rows, z.edge), 0) == g_row[q] - row0, g_wt[q], 0.0) for q in range(z.stencil)]
    loads = [rim_s, rim_second] + ([layers_s[0]] if z.pair else [])
    stacked = []
    for load in loads:
        for f in range(z.fields):
            stacked.append(jnp.concatenate([load[f : f + 1] * aimed[q] for q in range(z.stencil)], axis=1))
    height = len(stacked) * z.rows
    if height % 16:
        stacked.append(jnp.zeros((16 - height % 16, z.stencil * z.edge), F32))
    stacked = jnp.concatenate(stacked, axis=0)
    spots = jnp.concatenate(g_col, axis=1)
    columns = (iota((z.cols, z.stencil * z.edge), 0) == spots).astype(F32).astype(BF16)
    ghost = split_dot(stacked, columns, 2, NT_DIMS)

    def ghost_of(step, f):
        at = (step * z.fields + f) * z.rows
        return ghost[at : at + z.rows]

    force0, force1 = deposit(z, recv, panel, spread_a, spread_b)

    own_c = cond[0, 0]
    far_c = cond2[0, 0] if z.pair else None
    for f in range(z.fields):
        s = adj[0, f, 0] * (own_c * diffus[f])
        new = adj[0, f, 0] - 6.0 * s + sideways(s) + upright(s, above[f : f + 1], below[f : f + 1])
        new = new + coupled(z, couple, lambda e: adj[0, e, 0], f) + ghost_of(0, f)
        second = ghost_of(1, f)
        if z.pair:
            far = adj2[0, f, 0] * (far_c * diffus[f])
            new = new + far
            part = adj2[0, f, 0] - 6.0 * far + sideways(far) + upright(far, 0.0, 0.0) + s
            part = part + coupled(z, couple, lambda e: adj2[0, e, 0], f) + ghost_of(2, f)
            if f == 3:
                part = part + force1 * (1.0 - outer)
            second = second + part * (far_c * diffus[f])
            up[SUBL + f : SUBL + f + 1, :] = far[z.rows - 1 :]
            down[SUBL + f : SUBL + f + 1, :] = far[:1]
        else:
            new = new + beside[f]
        if f == 3:
            new = new + force1 * outer
            second = second + force0 * outer
        first[f] = new
        base[f] = second
        s = new * (own_c * diffus[f])
        up[f : f + 1, :] = s[z.rows - 1 :]
        down[f : f + 1, :] = s[:1]
    for half in range(2 if z.pair else 1):
        for ref in (up, down):
            ref[half * SUBL + z.fields : (half + 1) * SUBL, :] = jnp.zeros((SUBL - z.fields, z.cols), F32)


def second_kernel(z, first, base, cond, *refs):
    if z.pair:
        cond2, *refs = refs
    else:
        beside, *refs = refs
    above, below, diffus, couple, out = refs
    own_c = cond[0, 0]
    for f in range(z.fields):
        s = first[f] * (own_c * diffus[f])
        new = first[f] - 6.0 * s + sideways(s) + base[f]
        high, low = above[f : f + 1], below[f : f + 1]
        if z.pair:
            far_c = cond2[0, 0]
            high = high + above[SUBL + f : SUBL + f + 1] * (far_c[:1] * diffus[f])
            low = low + below[SUBL + f : SUBL + f + 1] * (far_c[z.rows - 1 :] * diffus[f])
        else:
            new = new + beside[f]
        new = new + upright(s, high, low)
        out[0, f, 0] = new + coupled(z, couple, lambda e: first[e], f)


def shifted(x, axis, step):
    count = lax.axis_size(axis)
    pairs = [(i, i + step) for i in range(count) if 0 <= i + step < count]
    return lax.ppermute(x, axis, pairs)


def both_sides(x, axis):
    return shifted(x, axis, 1) + shifted(x, axis, -1)


def call(kernel, shapes, scratch, args, scalars):
    specs = [
        pl.BlockSpec(memory_space=pltpu.SMEM if n in scalars else pltpu.VMEM) for n in range(len(args))
    ]
    return pl.pallas_call(
        kernel,
        out_shape=[jax.ShapeDtypeStruct(shape, F32) for shape in shapes],
        in_specs=specs,
        out_specs=[pl.BlockSpec(memory_space=pltpu.VMEM)] * len(shapes),
        scratch_shapes=scratch,
        compiler_params=pltpu.CompilerParams(vmem_limit_bytes=48 << 20),
    )(*args)


def body(adj, cond, diffus, couple, ghost_row, ghost_col, ghost_wt, obs_dest, obs_cell, obs_wt, misfit):
    z = Sizes(adj, obs_cell, ghost_row)
    state = (z.fields, z.rows, z.cols)
    if z.pair:
        swap = [(0, 1), (1, 0)]
        adj2 = lax.ppermute(adj, "rad", swap)
        cond2 = lax.ppermute(cond, "rad", swap)
    else:
        scaled = diffus[:, None, None] * cond[0, 0][None] * adj[0, :, 0]
        beside = both_sides(scaled, "rad")
    pay, up, down = call(
        functools.partial(pack_kernel, z),
        [(z.devices, z.block, LANES), (SUBL, z.cols), (SUBL, z.cols)],
        [],
        [adj, cond, diffus, obs_dest.reshape(1, z.count), obs_cell, obs_wt, misfit],
        (2,),
    )
    recv = lax.all_to_all(pay, ("panel", "rad", "ang"), split_axis=0, concat_axis=0, tiled=True)
    above, below = shifted(up, "ang", 1), shifted(down, "ang", -1)
    points = z.rads * z.tiles * z.npr * LANES
    lines = (SUBL * (2 if z.pair else 1), z.cols)
    args = [adj, cond] + ([adj2, cond2] if z.pair else [beside])
    args += [above, below, recv.reshape(z.devices * z.block, LANES), diffus, couple]
    scalars = (len(args) - 2, len(args) - 1)
    first, base, up, down = call(
        functools.partial(first_kernel, z),
        [state, state, lines, lines],
        [pltpu.VMEM((2 * TIMES * z.hi, points), BF16), pltpu.VMEM((LOW, points), BF16)],
        args + [ghost_row, ghost_col, ghost_wt],
        scalars,
    )
    above, below = shifted(up, "ang", 1), shifted(down, "ang", -1)
    if z.pair:
        args = [first, base, cond, cond2]
    else:
        scaled = diffus[:, None, None] * cond[0, 0][None] * first
        args = [first, base, cond, both_sides(scaled, "rad")]
    args += [above, below, diffus, couple]
    (out,) = call(functools.partial(second_kernel, z), [adj.shape], [], args, (6, 7))
    return out


def solution(mesh):
    placed = (
        P("panel", None, "rad", "ang", None),
        P("panel", "rad", "ang", None),
        P(),
        P(),
        P(),
        P(),
        P(),
        P("panel", "rad", "ang", None),
        P("panel", "rad", None, "ang"),
        P("panel", "rad", None, "ang"),
        P("panel", "rad", None, "ang"),
    )
    return jax.shard_map(
        body,
        mesh=mesh,
        in_specs=placed,
        out_specs=P("panel", None, "rad", "ang", None),
        check_vma=False,
    )
```

```python
import functools

import jax
import jax.numpy as jnp
from jax import lax
from jax.experimental import pallas as pl
from jax.experimental.pallas import tpu as pltpu
from jax.sharding import PartitionSpec as P

LANES = 128
SUBL = 8
POINTS = 4
TIMES = 2
LOW = 256
F32 = jnp.float32
BF16 = jnp.bfloat16
NT_DIMS = (((1,), (1,)), ((), ()))


def parts_of(x, count):
    parts = []
    for _ in range(count):
        part = x.astype(BF16)
        parts.append(part)
        x = x - part.astype(F32)
    return parts


def split_dot(x, onehot, count, dims):
    total = None
    for part in parts_of(x, count):
        term = lax.dot_general(part, onehot, dims, preferred_element_type=F32)
        total = term if total is None else total + term
    return total


def iota(shape, dim):
    return lax.broadcasted_iota(jnp.int32, shape, dim)


class Sizes:
    def __init__(self, adj, obs_cell, ghost_row):
        self.fields, self.rows, self.cols = adj.shape[1], adj.shape[3], adj.shape[4]
        self.panels = lax.axis_size("panel")
        self.rads = lax.axis_size("rad")
        self.tiles = lax.axis_size("ang")
        self.devices = self.panels * self.rads * self.tiles
        self.total_rows = self.tiles * self.rows
        self.edge = 2 * self.total_rows
        self.count = obs_cell.shape[-1]
        self.slots = 2 * self.count // self.tiles
        self.spr = min(POINTS, LANES // self.slots)
        self.npr = POINTS // self.spr
        self.feat_rows = 2 * self.npr + 1
        self.edge_rows = self.edge // LANES
        self.strip = self.feat_rows + self.edge_rows
        self.block = -(-(self.strip + 2) // SUBL) * SUBL
        self.stencil = ghost_row.shape[1]
        self.hi = self.rows * self.cols // LOW
        self.pair = self.rads == 2


def rolled(x, shift, axis):
    size = x.shape[axis]
    shift = shift % size
    return x if shift == 0 else pltpu.roll(x, shift, axis)


def pack_kernel(z, *refs):
    count = 7
    given, (pay, mate, next_), held, sems = refs[:count], refs[count : count + 3], refs[count + 3 : -1], refs[-1]
    order = (3, 4, 5, 6, 2, 1, 0)
    copies = [pltpu.make_async_copy(given[n], held[n], sems.at[n]) for n in range(count)]
    for n in order:
        copies[n].start()
    adj, cond, diffus, dest, cell, wt, misfit = held
    for n in order[:4]:
        copies[n].wait()

    owner = dest[...]
    height = max(16, z.tiles)
    mine = (iota((height, z.count), 0) == owner).astype(F32)
    earlier = (iota((z.count, z.count), 0) < iota((z.count, z.count), 1)).astype(F32)
    ranks = jnp.dot(mine.astype(BF16), earlier.astype(BF16), preferred_element_type=F32)
    rank = jnp.sum(ranks * mine, axis=0, keepdims=True)
    place = owner * LANES + rank.astype(jnp.int32)
    spread = (iota((z.tiles * LANES, z.count), 0) == place).astype(F32).astype(BF16)

    where = cell[0, 0]
    row = ((where.astype(F32) + 0.5) * (1.0 / z.cols)).astype(jnp.int32)
    col = where - row * z.cols
    code = ((col // LOW) * z.rows + row) * LOW + col % LOW
    code = code.astype(F32)
    weight = wt[0, 0]
    mis = misfit[0, 0]
    feats = []
    for g in range(z.spr):
        picked = [weight[h * z.spr + g : h * z.spr + g + 1] for h in range(z.npr)]
        picked += [code[h * z.spr + g : h * z.spr + g + 1] for h in range(z.npr)]
        picked.append(mis[g : g + 1] if g < TIMES else jnp.zeros((1, z.count), F32))
        feats += picked
    used = len(feats)
    padded = -(-used // 16) * 16
    if padded > used:
        feats.append(jnp.zeros((padded - used, z.count), F32))
    boxed = split_dot(jnp.concatenate(feats, axis=0), spread, 3, NT_DIMS)
    slots = boxed[: z.feat_rows]
    for g in range(1, z.spr):
        slots = slots + rolled(boxed[g * z.feat_rows : (g + 1) * z.feat_rows], g * z.slots, 1)

    full_row = owner * z.rows + row
    edge_at = jnp.where(col == 0, full_row, jnp.where(col == z.cols - 1, z.total_rows + full_row, -1))
    total = None
    for s in range(POINTS):
        value = mis[1:2] * weight[s : s + 1]
        value = jnp.concatenate([value, jnp.zeros((15, z.count), F32)], axis=0)
        hits = (iota((z.edge, z.count), 0) == edge_at[s : s + 1]).astype(F32).astype(BF16)
        term = split_dot(value, hits, 3, NT_DIMS)
        total = term if total is None else total + term
    edge_force = total[:1]

    for n in order[4:]:
        copies[n].wait()

    lane = iota((z.rows, LANES), 1)
    sub = iota((z.rows, LANES), 0)
    strips = []
    for side in range(2):
        acc = jnp.zeros((z.rows, LANES), F32)
        for f in range(z.fields + 1):
            for inner in range(2):
                at = inner if side == 0 else z.cols - 1 - inner
                line = adj[0, f, 0, :, at : at + 1] if f < z.fields else cond[0, 0, :, at : at + 1]
                acc = jnp.where(lane == (f * 2 + inner) * z.rows + sub, line, acc)
        strips.append(jnp.sum(acc, axis=0, keepdims=True))

    common = [edge_force[:, k * LANES : (k + 1) * LANES] for k in range(z.edge_rows)] + strips
    spare = z.block - z.strip - 2
    if spare:
        common.append(jnp.zeros((spare, LANES), F32))
    common = jnp.concatenate(common, axis=0)
    for t in range(z.tiles):
        part = jnp.concatenate([slots[:, t * LANES : (t + 1) * LANES], common], axis=0)
        for group in range(z.panels * z.rads):
            pay[group * z.tiles + t] = part

    for f in range(z.fields):
        s = adj[0, f, 0] * (cond[0, 0] * diffus[f])
        mate[f : f + 1, :], next_[f : f + 1, :] = facing(s)
    for ref in (mate, next_):
        ref[z.fields :, :] = jnp.zeros((SUBL - z.fields, z.cols), F32)


def even_tile():
    return lax.axis_index("ang") % 2 == 0


def facing(s):
    top, bottom = s[:1], s[s.shape[0] - 1 :]
    even = even_tile()
    return jnp.where(even, bottom, top), jnp.where(even, top, bottom)


def around(z, mate, next_):
    even = even_tile()
    tile = lax.axis_index("ang")
    next_ = jnp.where((tile == 0) | (tile == z.tiles - 1), 0.0, next_)
    return jnp.where(even, next_, mate), jnp.where(even, mate, next_)


def by_field(z, scalar, width):
    sub = iota((SUBL, width), 0)
    out = jnp.zeros((SUBL, width), F32)
    for f in range(z.fields):
        out = jnp.where(sub == f, scalar(f), out)
    return out


def unpack_strips(z, recv, sets):
    height = 2 * z.tiles
    stacked = []
    for panel, rad in sets:
        base = (panel * z.rads + rad) * z.tiles * z.block + z.strip
        for side in range(2):
            stacked.append(recv[pl.ds(base + side, z.tiles, stride=z.block), :])
    stacked = jnp.concatenate(stacked, axis=0)
    width = 2 * SUBL * z.edge
    lane = iota((LANES, width), 1)
    slot = lane // z.edge
    inner, plane = slot // SUBL, slot % SUBL
    picks = (iota((LANES, width), 0) == (plane * 2 + inner) * z.rows + lane % z.rows).astype(F32)
    moved = split_dot(stacked, picks.astype(BF16), 3, (((1,), (0,)), ((), ())))
    lane = iota((height, z.edge), 1)
    keep = lane // z.rows == iota((height, z.edge), 0)
    out = []
    for number in range(len(sets)):
        both = []
        for inner in range(2):
            rows = []
            for f in range(z.fields + 1):
                at = (inner * SUBL + f) * z.edge
                tile = moved[number * height : (number + 1) * height, at : at + z.edge]
                rows.append(jnp.sum(jnp.where(keep, tile, 0.0), axis=0, keepdims=True))
            both.append(jnp.concatenate(rows, axis=0))
        out.append(both)
    return out


def edge_scaled(z, values, dif):
    return values * values[z.fields : z.fields + 1] * dif


def coupled(z, couple, state, c):
    total = None
    for e in range(z.fields):
        term = state(e) * couple[e, c]
        total = term if total is None else total + term
    return total


def line_of(ref, s, q):
    return jnp.concatenate([ref[side, q : q + 1, :] for side in range(2)], axis=1) if s is None else ref[s, q : q + 1, :]


def deposit(z, recv, panel, spread_a, spread_b):
    sources = z.rads * z.tiles
    base = panel * sources * z.block
    feat = [recv[pl.ds(base + k, sources, stride=z.block), :] for k in range(z.feat_rows)]
    lane = iota((sources, LANES), 1)
    scaled = []
    for t in range(TIMES):
        mis = jnp.where(lane // z.slots == t, feat[2 * z.npr], 0.0)
        full = None
        for g in range(z.spr):
            term = rolled(mis, (g - t) * z.slots, 1)
            full = term if full is None else full + term
        scaled.append(full)
    sub_hi = iota((z.hi, LANES), 0)
    sub_lo = iota((LOW, LANES), 0)
    for h in range(z.npr):
        code = feat[z.npr + h].astype(jnp.int32)
        high, low = code // LOW, code % LOW
        parts = []
        for t in range(TIMES):
            parts += [p.astype(F32) for p in parts_of(scaled[t] * feat[h], 2)]
        for n in range(sources):
            at = (n * z.npr + h) * LANES
            hit = sub_hi == high[n : n + 1]
            for k, part in enumerate(parts):
                spread_a[k * z.hi : (k + 1) * z.hi, at : at + LANES] = jnp.where(hit, part[n : n + 1], 0.0).astype(BF16)
            spread_b[:, at : at + LANES] = (sub_lo == low[n : n + 1]).astype(F32).astype(BF16)
    grid = lax.dot_general(spread_a[...], spread_b[...], NT_DIMS, preferred_element_type=F32)
    out = []
    for t in range(TIMES):
        both = grid[2 * t * z.hi : (2 * t + 1) * z.hi] + grid[(2 * t + 1) * z.hi : (2 * t + 2) * z.hi]
        out.append(jnp.concatenate([both[k * z.rows : (k + 1) * z.rows] for k in range(z.cols // LOW)], axis=1))
    return out


def sideways(s):
    cols = s.shape[1]
    lane = iota(s.shape, 1)
    west = jnp.where(lane == 0, 0.0, pltpu.roll(s, 1, 1))
    east = jnp.where(lane == cols - 1, 0.0, pltpu.roll(s, cols - 1, 1))
    return west + east


def upright(s, above, below):
    rows = s.shape[0]
    sub = iota(s.shape, 0)
    north = jnp.where(sub == 0, above, pltpu.roll(s, 1, 0))
    south = jnp.where(sub == rows - 1, below, pltpu.roll(s, rows - 1, 0))
    return north + south


def first_kernel(z, adj, cond, *refs):
    if z.pair:
        adj2, cond2, *refs = refs
    else:
        beside, *refs = refs
    mate_in, next_in, recv, diffus, couple, grow, gcol, gwt, *refs = refs
    first, base, mate, next_, spread_a, spread_b = refs
    above, below = around(z, mate_in[...], next_in[...])
    panel, rad, tile = lax.axis_index("panel"), lax.axis_index("rad"), lax.axis_index("ang")
    other = 1 - panel
    outer = jnp.where(rad == z.rads - 1, 1.0, 0.0)

    sets = [(other, rad), (panel, rad)]
    if z.pair:
        sets.append((other, 1 - rad))
        near = [1.0]
    else:
        sets += [(other, jnp.maximum(rad - 1, 0)), (other, jnp.minimum(rad + 1, z.rads - 1))]
        near = [jnp.where(rad > 0, 1.0, 0.0), jnp.where(rad < z.rads - 1, 1.0, 0.0)]
    strips = unpack_strips(z, recv, sets)
    dif = by_field(z, lambda f: diffus[f], z.edge)
    rim, inside = strips[0]
    rim_s = edge_scaled(z, rim, dif)
    home_s = edge_scaled(z, strips[1][0], dif)
    layers_s = [edge_scaled(z, strips[2 + k][0], dif) for k in range(len(near))]
    lap = edge_scaled(z, inside, dif) - 6.0 * rim_s
    for k, one in enumerate(near):
        lap = lap + layers_s[k] * one
    spot = iota((SUBL, z.edge), 1) % z.total_rows
    lap = lap + jnp.where(spot == 0, 0.0, pltpu.roll(rim_s, 1, 1))
    lap = lap + jnp.where(spot == z.total_rows - 1, 0.0, pltpu.roll(rim_s, z.edge - 1, 1))
    rows = [coupled(z, couple, lambda e: rim[e : e + 1], c) for c in range(z.fields)]
    mixed = jnp.concatenate(rows + [jnp.zeros((SUBL - z.fields, z.edge), F32)], axis=0)

    g_row = [line_of(grow, None, q) for q in range(z.stencil)]
    g_col = [line_of(gcol, None, q) for q in range(z.stencil)]
    g_wt = [line_of(gwt, None, q) for q in range(z.stencil)]
    rim_ghost = None
    for q in range(z.stencil):
        target = jnp.where(
            g_col[q] == 0, g_row[q], jnp.where(g_col[q] == z.cols - 1, z.total_rows + g_row[q], -1)
        )
        hits = (iota((z.edge, z.edge), 0) == target).astype(F32).astype(BF16)
        values = jnp.concatenate([home_s * g_wt[q], jnp.zeros((SUBL, z.edge), F32)], axis=0)
        term = split_dot(values, hits, 3, NT_DIMS)
        rim_ghost = term if rim_ghost is None else rim_ghost + term
    sources = z.rads * z.tiles
    force = []
    for k in range(z.edge_rows):
        at = other * sources * z.block + z.feat_rows + k
        force.append(jnp.sum(recv[pl.ds(at, sources, stride=z.block), :], axis=0, keepdims=True))
    force = jnp.concatenate(force, axis=1) * outer
    rim_first = rim + lap + mixed + rim_ghost[:SUBL]
    rim_first = rim_first + jnp.where(iota((SUBL, z.edge), 0) == 3, force, 0.0)
    rim_second = rim_first * rim[z.fields : z.fields + 1] * dif

    row0 = tile * z.rows
    aimed = [jnp.where(iota((z.rows, z.edge), 0) == g_row[q] - row0, g_wt[q], 0.0) for q in range(z.stencil)]
    loads = [rim_s, rim_second] + ([layers_s[0]] if z.pair else [])
    stacked = []
    for load in loads:
        for f in range(z.fields):
            stacked.append(jnp.concatenate([load[f : f + 1] * aimed[q] for q in range(z.stencil)], axis=1))
    height = len(stacked) * z.rows
    if height % 16:
        stacked.append(jnp.zeros((16 - height % 16, z.stencil * z.edge), F32))
    stacked = jnp.concatenate(stacked, axis=0)
    spots = jnp.concatenate(g_col, axis=1)
    columns = (iota((z.cols, z.stencil * z.edge), 0) == spots).astype(F32).astype(BF16)
    ghost = split_dot(stacked, columns, 2, NT_DIMS)

    def ghost_of(step, f):
        at = (step * z.fields + f) * z.rows
        return ghost[at : at + z.rows]

    force0, force1 = deposit(z, recv, panel, spread_a, spread_b)

    own_c = cond[0, 0]
    far_c = cond2[0, 0] if z.pair else None
    for f in range(z.fields):
        s = adj[0, f, 0] * (own_c * diffus[f])
        new = adj[0, f, 0] - 6.0 * s + sideways(s) + upright(s, above[f : f + 1], below[f : f + 1])
        new = new + coupled(z, couple, lambda e: adj[0, e, 0], f) + ghost_of(0, f)
        second = ghost_of(1, f)
        if z.pair:
            far = adj2[0, f, 0] * (far_c * diffus[f])
            new = new + far
            part = adj2[0, f, 0] - 6.0 * far + sideways(far) + upright(far, 0.0, 0.0) + s
            part = part + coupled(z, couple, lambda e: adj2[0, e, 0], f) + ghost_of(2, f)
            if f == 3:
                part = part + force1 * (1.0 - outer)
            second = second + part * (far_c * diffus[f])
            at = SUBL + f
            mate[at : at + 1, :], next_[at : at + 1, :] = facing(far)
        else:
            new = new + beside[f]
        if f == 3:
            new = new + force1 * outer
            second = second + force0 * outer
        first[f] = new
        base[f] = second
        s = new * (own_c * diffus[f])
        mate[f : f + 1, :], next_[f : f + 1, :] = facing(s)
    for half in range(2 if z.pair else 1):
        for ref in (mate, next_):
            ref[half * SUBL + z.fields : (half + 1) * SUBL, :] = jnp.zeros((SUBL - z.fields, z.cols), F32)


def second_kernel(z, first, base, cond, *refs):
    if z.pair:
        cond2, *refs = refs
    else:
        beside, *refs = refs
    mate_in, next_in, diffus, couple, out = refs
    above, below = around(z, mate_in[...], next_in[...])
    own_c = cond[0, 0]
    for f in range(z.fields):
        s = first[f] * (own_c * diffus[f])
        new = first[f] - 6.0 * s + sideways(s) + base[f]
        high, low = above[f : f + 1], below[f : f + 1]
        if z.pair:
            far_c = cond2[0, 0]
            high = high + above[SUBL + f : SUBL + f + 1] * (far_c[:1] * diffus[f])
            low = low + below[SUBL + f : SUBL + f + 1] * (far_c[z.rows - 1 :] * diffus[f])
        else:
            new = new + beside[f]
        new = new + upright(s, high, low)
        out[0, f, 0] = new + coupled(z, couple, lambda e: first[e], f)


def shifted(x, axis, step):
    count = lax.axis_size(axis)
    pairs = [(i, i + step) for i in range(count) if 0 <= i + step < count]
    return lax.ppermute(x, axis, pairs)


def both_sides(x, axis):
    return shifted(x, axis, 1) + shifted(x, axis, -1)


def beside_rows(z, mate, next_):
    pairs, links = [], []
    for rad in range(z.rads):
        at = rad * z.tiles
        other = (rad ^ 1) * z.tiles
        for i in range(z.tiles):
            pairs.append((at + i, at + (i ^ 1)))
            if 0 < i < z.tiles - 1:
                links.append((at + i, at + (i + 1 if i % 2 else i - 1)))
            else:
                links.append((at + i, other + i))
    axes = ("rad", "ang")
    return lax.ppermute(mate, axes, pairs), lax.ppermute(next_, axes, links)


def call(kernel, shapes, scratch, args, scalars=(), spaces=None, room=48):
    specs = [
        pl.BlockSpec(memory_space=spaces or (pltpu.SMEM if n in scalars else pltpu.VMEM))
        for n in range(len(args))
    ]
    return pl.pallas_call(
        kernel,
        out_shape=[jax.ShapeDtypeStruct(shape, F32) for shape in shapes],
        in_specs=specs,
        out_specs=[pl.BlockSpec(memory_space=pltpu.VMEM)] * len(shapes),
        scratch_shapes=scratch,
        compiler_params=pltpu.CompilerParams(vmem_limit_bytes=room << 20),
    )(*args)


def body(adj, cond, diffus, couple, ghost_row, ghost_col, ghost_wt, obs_dest, obs_cell, obs_wt, misfit):
    z = Sizes(adj, obs_cell, ghost_row)
    state = (z.fields, z.rows, z.cols)
    if z.pair:
        swap = [(0, 1), (1, 0)]
        adj2 = lax.ppermute(adj, "rad", swap)
        cond2 = lax.ppermute(cond, "rad", swap)
    else:
        scaled = diffus[:, None, None] * cond[0, 0][None] * adj[0, :, 0]
        beside = both_sides(scaled, "rad")
    given = [adj, cond, diffus, obs_dest.reshape(1, z.count), obs_cell, obs_wt, misfit]
    held = [pltpu.SMEM(x.shape, x.dtype) if x is diffus else pltpu.VMEM(x.shape, x.dtype) for x in given]
    pay, mate, next_ = call(
        functools.partial(pack_kernel, z),
        [(z.devices, z.block, LANES), (SUBL, z.cols), (SUBL, z.cols)],
        held + [pltpu.SemaphoreType.DMA((len(given),))],
        given,
        spaces=pltpu.HBM,
        room=64,
    )
    recv = lax.all_to_all(pay, ("panel", "rad", "ang"), split_axis=0, concat_axis=0, tiled=True)
    mate, next_ = beside_rows(z, mate, next_)
    points = z.rads * z.tiles * z.npr * LANES
    lines = (SUBL * (2 if z.pair else 1), z.cols)
    args = [adj, cond] + ([adj2, cond2] if z.pair else [beside])
    args += [mate, next_, recv.reshape(z.devices * z.block, LANES), diffus, couple]
    scalars = (len(args) - 2, len(args) - 1)
    first, base, mate, next_ = call(
        functools.partial(first_kernel, z),
        [state, state, lines, lines],
        [pltpu.VMEM((2 * TIMES * z.hi, points), BF16), pltpu.VMEM((LOW, points), BF16)],
        args + [ghost_row, ghost_col, ghost_wt],
        scalars,
    )
    mate, next_ = beside_rows(z, mate, next_)
    if z.pair:
        args = [first, base, cond, cond2]
    else:
        scaled = diffus[:, None, None] * cond[0, 0][None] * first
        args = [first, base, cond, both_sides(scaled, "rad")]
    args += [mate, next_, diffus, couple]
    (out,) = call(functools.partial(second_kernel, z), [adj.shape], [], args, (6, 7))
    return out


def solution(mesh):
    placed = (
        P("panel", None, "rad", "ang", None),
        P("panel", "rad", "ang", None),
        P(),
        P(),
        P(),
        P(),
        P(),
        P("panel", "rad", "ang", None),
        P("panel", "rad", None, "ang"),
        P("panel", "rad", None, "ang"),
        P("panel", "rad", None, "ang"),
    )
    return jax.shard_map(
        body,
        mesh=mesh,
        in_specs=placed,
        out_specs=P("panel", None, "rad", "ang", None),
        check_vma=False,
    )
```

```python
import functools

import jax
import jax.numpy as jnp
from jax import lax
from jax.experimental import pallas as pl
from jax.experimental.pallas import tpu as pltpu
from jax.sharding import PartitionSpec as P

LANES = 128
SUBL = 8
POINTS = 4
TIMES = 2
LOW = 256
F32 = jnp.float32
BF16 = jnp.bfloat16
NT_DIMS = (((1,), (1,)), ((), ()))


def parts_of(x, count):
    parts = []
    for _ in range(count):
        part = x.astype(BF16)
        parts.append(part)
        x = x - part.astype(F32)
    return parts


def split_dot(x, onehot, count, dims):
    total = None
    for part in parts_of(x, count):
        term = lax.dot_general(part, onehot, dims, preferred_element_type=F32)
        total = term if total is None else total + term
    return total


def joint_dot(x, onehot, count, dims):
    rows = x.shape[0]
    parts = [part.astype(F32) for part in parts_of(x, count)]
    spare = -(rows * count) % 16
    if spare:
        parts.append(jnp.zeros((spare, x.shape[1]), F32))
    joined = jnp.concatenate(parts, axis=0).astype(BF16)
    out = lax.dot_general(joined, onehot, dims, preferred_element_type=F32)
    return sum(out[k * rows : (k + 1) * rows] for k in range(1, count)) + out[:rows]


def iota(shape, dim):
    return lax.broadcasted_iota(jnp.int32, shape, dim)


class Sizes:
    def __init__(self, adj, obs_cell, ghost_row):
        self.fields, self.rows, self.cols = adj.shape[1], adj.shape[3], adj.shape[4]
        self.panels = lax.axis_size("panel")
        self.rads = lax.axis_size("rad")
        self.tiles = lax.axis_size("ang")
        self.devices = self.panels * self.rads * self.tiles
        self.total_rows = self.tiles * self.rows
        self.edge = 2 * self.total_rows
        self.count = obs_cell.shape[-1]
        self.slots = 2 * self.count // self.tiles
        self.spr = min(POINTS, LANES // self.slots)
        self.npr = POINTS // self.spr
        self.feat_rows = 2 * self.npr + 1
        self.edge_rows = self.edge // LANES
        self.strip = self.feat_rows + self.edge_rows
        self.block = -(-(self.strip + 2) // SUBL) * SUBL
        self.stencil = ghost_row.shape[1]
        self.hi = self.rows * self.cols // LOW
        self.pair = self.rads == 2


def rolled(x, shift, axis):
    size = x.shape[axis]
    shift = shift % size
    return x if shift == 0 else pltpu.roll(x, shift, axis)


def pack_kernel(z, *refs):
    count = 7
    given, (pay, mate, next_), held, sems = refs[:count], refs[count : count + 3], refs[count + 3 : -1], refs[-1]
    order = (3, 4, 5, 6, 2, 1, 0)
    copies = [pltpu.make_async_copy(given[n], held[n], sems.at[n]) for n in range(count)]
    for n in order:
        copies[n].start()
    adj, cond, diffus, dest, cell, wt, misfit = held
    for n in order[:4]:
        copies[n].wait()

    owner = dest[...]
    height = max(16, z.tiles)
    mine = (iota((height, z.count), 0) == owner).astype(F32)
    earlier = (iota((z.count, z.count), 0) < iota((z.count, z.count), 1)).astype(F32)
    ranks = jnp.dot(mine.astype(BF16), earlier.astype(BF16), preferred_element_type=F32)

    where = cell[0, 0]
    weight = wt[0, 0]
    mis = misfit[0, 0]
    row = ((where.astype(F32) + 0.5) * (1.0 / z.cols)).astype(jnp.int32)
    col = where - row * z.cols
    full_row = owner * z.rows + row
    edge_at = jnp.where(col == 0, full_row, jnp.where(col == z.cols - 1, z.total_rows + full_row, -1))
    hits = jnp.concatenate(
        [(iota((z.edge, z.count), 0) == edge_at[s : s + 1]).astype(F32) for s in range(POINTS)], axis=1
    )
    value = jnp.concatenate([mis[1:2] * weight[s : s + 1] for s in range(POINTS)], axis=1)
    edge_force = joint_dot(value, hits.astype(BF16), 3, NT_DIMS)

    rank = jnp.sum(ranks * mine, axis=0, keepdims=True)
    place = owner * LANES + rank.astype(jnp.int32)
    spread = (iota((z.tiles * LANES, z.count), 0) == place).astype(F32).astype(BF16)
    code = ((col // LOW) * z.rows + row) * LOW + col % LOW
    code = code.astype(F32)
    feats = []
    for g in range(z.spr):
        picked = [weight[h * z.spr + g : h * z.spr + g + 1] for h in range(z.npr)]
        picked += [code[h * z.spr + g : h * z.spr + g + 1] for h in range(z.npr)]
        picked.append(mis[g : g + 1] if g < TIMES else jnp.zeros((1, z.count), F32))
        feats += picked
    boxed = joint_dot(jnp.concatenate(feats, axis=0), spread, 3, NT_DIMS)
    slots = boxed[: z.feat_rows]
    for g in range(1, z.spr):
        slots = slots + rolled(boxed[g * z.feat_rows : (g + 1) * z.feat_rows], g * z.slots, 1)

    for n in order[4:]:
        copies[n].wait()

    lane = iota((z.rows, LANES), 1)
    sub = iota((z.rows, LANES), 0)
    strips = []
    for side in range(2):
        acc = jnp.zeros((z.rows, LANES), F32)
        for f in range(z.fields + 1):
            for inner in range(2):
                at = inner if side == 0 else z.cols - 1 - inner
                line = adj[0, f, 0, :, at : at + 1] if f < z.fields else cond[0, 0, :, at : at + 1]
                acc = jnp.where(lane == (f * 2 + inner) * z.rows + sub, line, acc)
        strips.append(jnp.sum(acc, axis=0, keepdims=True))

    common = [edge_force[:, k * LANES : (k + 1) * LANES] for k in range(z.edge_rows)] + strips
    spare = z.block - z.strip - 2
    if spare:
        common.append(jnp.zeros((spare, LANES), F32))
    common = jnp.concatenate(common, axis=0)
    for t in range(z.tiles):
        part = jnp.concatenate([slots[:, t * LANES : (t + 1) * LANES], common], axis=0)
        for group in range(z.panels * z.rads):
            pay[group * z.tiles + t] = part

    for f in range(z.fields):
        mate[f : f + 1, :], next_[f : f + 1, :] = facing(adj[0, f, 0] * (cond[0, 0] * diffus[f]))
    mate[z.fields :, :], next_[z.fields :, :] = facing(cond[0, 0])


def even_tile():
    return lax.axis_index("ang") % 2 == 0


def facing(s):
    top, bottom = s[:1], s[s.shape[0] - 1 :]
    even = even_tile()
    return jnp.where(even, bottom, top), jnp.where(even, top, bottom)


def around(z, mate, next_):
    even = even_tile()
    tile = lax.axis_index("ang")
    next_ = jnp.where((tile == 0) | (tile == z.tiles - 1), 0.0, next_)
    return jnp.where(even, next_, mate), jnp.where(even, mate, next_)


def by_field(z, scalar, width):
    sub = iota((SUBL, width), 0)
    out = jnp.zeros((SUBL, width), F32)
    for f in range(z.fields):
        out = jnp.where(sub == f, scalar(f), out)
    return out


def unpack_strips(z, recv, sets):
    height = 2 * z.tiles
    stacked = []
    for panel, rad in sets:
        base = (panel * z.rads + rad) * z.tiles * z.block + z.strip
        for side in range(2):
            stacked.append(recv[pl.ds(base + side, z.tiles, stride=z.block), :])
    stacked = jnp.concatenate(stacked, axis=0)
    width = 2 * SUBL * z.edge
    lane = iota((LANES, width), 1)
    slot = lane // z.edge
    inner, plane = slot // SUBL, slot % SUBL
    picks = (iota((LANES, width), 0) == (plane * 2 + inner) * z.rows + lane % z.rows).astype(F32)
    moved = split_dot(stacked, picks.astype(BF16), 3, (((1,), (0,)), ((), ())))
    lane = iota((height, z.edge), 1)
    keep = lane // z.rows == iota((height, z.edge), 0)
    out = []
    for number in range(len(sets)):
        both = []
        for inner in range(2):
            rows = []
            for f in range(z.fields + 1):
                at = (inner * SUBL + f) * z.edge
                tile = moved[number * height : (number + 1) * height, at : at + z.edge]
                rows.append(jnp.sum(jnp.where(keep, tile, 0.0), axis=0, keepdims=True))
            both.append(jnp.concatenate(rows, axis=0))
        out.append(both)
    return out


def edge_scaled(z, values, dif):
    return values * values[z.fields : z.fields + 1] * dif


def coupled(z, couple, state, c):
    total = None
    for e in range(z.fields):
        term = state(e) * couple[e, c]
        total = term if total is None else total + term
    return total


def line_of(ref, q):
    return jnp.concatenate([ref[side, q : q + 1, :] for side in range(2)], axis=1)


def observed(z, recv, panel):
    sources = z.rads * z.tiles
    base = panel * sources * z.block
    feat = [recv[pl.ds(base + k, sources, stride=z.block), :] for k in range(z.feat_rows)]
    lane = iota((sources, LANES), 1)
    misfits = []
    for t in range(TIMES):
        mis = jnp.where(lane // z.slots == t, feat[2 * z.npr], 0.0)
        full = None
        for g in range(z.spr):
            term = rolled(mis, (g - t) * z.slots, 1)
            full = term if full is None else full + term
        misfits.append(full)
    return feat[: z.npr], [code.astype(jnp.int32) for code in feat[z.npr : 2 * z.npr]], misfits


def dealt(z, values, highs, lows, height, spread_a, spread_b):
    width = spread_b.shape[0]
    sources = highs[0].shape[0]
    sub_high = iota((height, LANES), 0)
    sub_low = iota((width, LANES), 0)
    for h in range(z.npr):
        parts = []
        for value in values[h]:
            parts += [part.astype(F32) for part in parts_of(value, 2)]
        for n in range(sources):
            at = (n * z.npr + h) * LANES
            hit = sub_high == highs[h][n : n + 1]
            for k, part in enumerate(parts):
                spread_a[k * height : (k + 1) * height, at : at + LANES] = jnp.where(hit, part[n : n + 1], 0.0).astype(BF16)
            spread_b[:, at : at + LANES] = (sub_low == lows[h][n : n + 1]).astype(F32).astype(BF16)
    grid = lax.dot_general(spread_a[...], spread_b[...], NT_DIMS, preferred_element_type=F32)
    return [
        grid[2 * k * height : (2 * k + 1) * height] + grid[(2 * k + 1) * height : (2 * k + 2) * height]
        for k in range(len(values[0]))
    ]


def deposit(z, recv, panel, spread_a, spread_b):
    weights, codes, misfits = observed(z, recv, panel)
    values = [[mis * weight for mis in misfits] for weight in weights]
    highs = [code // LOW for code in codes]
    lows = [code % LOW for code in codes]
    out = []
    for both in dealt(z, values, highs, lows, z.hi, spread_a, spread_b):
        out.append(jnp.concatenate([both[k * z.rows : (k + 1) * z.rows] for k in range(z.cols // LOW)], axis=1))
    return out


def deposit_ends(z, recv, panel, spread_a, spread_b):
    weights, codes, misfits = observed(z, recv, panel)
    values = [[misfits[1] * weight] for weight in weights]
    chunks = z.cols // LANES
    highs, lows = [], []
    for code in codes:
        row = (code // LOW) % z.rows
        chunk = (code // LOW) // z.rows * (LOW // LANES) + (code % LOW) // LANES
        end = jnp.where(row == z.rows - 1, chunk + chunks, -1)
        highs.append(jnp.where(row == 0, chunk, end))
        lows.append(code % LANES)
    (both,) = dealt(z, values, highs, lows, 2 * chunks, spread_a, spread_b)
    ends = [[both[e * chunks + k : e * chunks + k + 1] for k in range(chunks)] for e in range(2)]
    return [jnp.concatenate(end, axis=1) for end in ends]


def sideways(s):
    cols = s.shape[1]
    lane = iota(s.shape, 1)
    west = jnp.where(lane == 0, 0.0, pltpu.roll(s, 1, 1))
    east = jnp.where(lane == cols - 1, 0.0, pltpu.roll(s, cols - 1, 1))
    return west + east


def upright(s, above, below):
    rows = s.shape[0]
    sub = iota(s.shape, 0)
    north = jnp.where(sub == 0, above, pltpu.roll(s, 1, 0))
    south = jnp.where(sub == rows - 1, below, pltpu.roll(s, rows - 1, 0))
    return north + south


def early_kernel(z, adj, cond, *refs):
    if z.pair:
        adj2, cond2, diffus, couple, out, mate, next_, own, far = refs
    else:
        beside, diffus, couple, out, mate, next_, own = refs
    own_c = cond[0, 0]
    far_c = cond2[0, 0] if z.pair else None
    for f in range(z.fields):
        s = adj[0, f, 0] * (own_c * diffus[f])
        new = adj[0, f, 0] - 6.0 * s + sideways(s) + upright(s, 0.0, 0.0)
        new = new + coupled(z, couple, lambda e: adj[0, e, 0], f)
        if z.pair:
            other = adj2[0, f, 0] * (far_c * diffus[f])
            new = new + other
            part = adj2[0, f, 0] - 6.0 * other + sideways(other) + upright(other, 0.0, 0.0) + s
            far[f] = part + coupled(z, couple, lambda e: adj2[0, e, 0], f)
            at = SUBL + f
            mate[at : at + 1, :], next_[at : at + 1, :] = facing(other)
        else:
            new = new + beside[f]
        own[f] = new
        mate[f : f + 1, :], next_[f : f + 1, :] = facing(new * (own_c * diffus[f]))
    for half in range(2 if z.pair else 1):
        for ref in (mate, next_):
            ref[half * SUBL + z.fields : (half + 1) * SUBL, :] = jnp.zeros((SUBL - z.fields, z.cols), F32)
    for f in range(z.fields):
        s = own[f] * (own_c * diffus[f])
        new = own[f] - 6.0 * s + sideways(s) + upright(s, 0.0, 0.0)
        new = new + coupled(z, couple, lambda e: own[e], f)
        if z.pair:
            new = new + far[f] * (far_c * diffus[f])
        out[f] = new


def ends_kernel(z, recv, cond, diffus, mate_row, next_row, mate_in, next_in, mate, next_, spread_a, spread_b):
    panel, rad, tile = lax.axis_index("panel"), lax.axis_index("rad"), lax.axis_index("ang")
    outer = jnp.where(rad == z.rads - 1, 1.0, 0.0)
    inner = jnp.where((tile == 0) | (tile == z.tiles - 1), 0.0, 1.0)
    top, bottom = deposit_ends(z, recv, panel, spread_a, spread_b)
    even = even_tile()
    to_mate = jnp.where(even, bottom, top) * outer
    to_next = jnp.where(even, top, bottom) * outer
    cond_mate, cond_next = facing(cond[0, 0])
    for f in range(z.fields):
        from_mate, from_next = mate_row[f : f + 1, :], next_row[f : f + 1, :] * inner
        if f == 3:
            from_mate, from_next = from_mate + to_mate, from_next + to_next
        mate[f : f + 1, :] = mate_in[f : f + 1, :] + from_mate * (cond_mate * diffus[f])
        next_[f : f + 1, :] = next_in[f : f + 1, :] + from_next * (cond_next * diffus[f])


def ghost_kernel(z, early, recv, cond, *refs):
    if z.pair:
        cond2, mate_in, next_in, diffus, couple, grow, gcol, gwt, out, added, spread_a, spread_b = refs
    else:
        mate_in, next_in, diffus, couple, grow, gcol, gwt, out, added, spread_a, spread_b = refs
    panel, rad, tile = lax.axis_index("panel"), lax.axis_index("rad"), lax.axis_index("ang")
    other = 1 - panel
    outer = jnp.where(rad == z.rads - 1, 1.0, 0.0)
    above, below = around(z, mate_in[...], next_in[...])

    sets = [(other, rad), (panel, rad)]
    if z.pair:
        sets.append((other, 1 - rad))
        near = [1.0]
    else:
        sets += [(other, jnp.maximum(rad - 1, 0)), (other, jnp.minimum(rad + 1, z.rads - 1))]
        near = [jnp.where(rad > 0, 1.0, 0.0), jnp.where(rad < z.rads - 1, 1.0, 0.0)]
    strips = unpack_strips(z, recv, sets)
    dif = by_field(z, lambda f: diffus[f], z.edge)
    rim, inside = strips[0]
    rim_s = edge_scaled(z, rim, dif)
    home_s = edge_scaled(z, strips[1][0], dif)
    layers_s = [edge_scaled(z, strips[2 + k][0], dif) for k in range(len(near))]
    lap = edge_scaled(z, inside, dif) - 6.0 * rim_s
    for k, one in enumerate(near):
        lap = lap + layers_s[k] * one
    spot = iota((SUBL, z.edge), 1) % z.total_rows
    lap = lap + jnp.where(spot == 0, 0.0, pltpu.roll(rim_s, 1, 1))
    lap = lap + jnp.where(spot == z.total_rows - 1, 0.0, pltpu.roll(rim_s, z.edge - 1, 1))
    rows = [coupled(z, couple, lambda e: rim[e : e + 1], c) for c in range(z.fields)]
    mixed = jnp.concatenate(rows + [jnp.zeros((SUBL - z.fields, z.edge), F32)], axis=0)

    g_row = [line_of(grow, q) for q in range(z.stencil)]
    g_col = [line_of(gcol, q) for q in range(z.stencil)]
    g_wt = [line_of(gwt, q) for q in range(z.stencil)]
    rim_ghost = None
    for q in range(z.stencil):
        target = jnp.where(
            g_col[q] == 0, g_row[q], jnp.where(g_col[q] == z.cols - 1, z.total_rows + g_row[q], -1)
        )
        hits = (iota((z.edge, z.edge), 0) == target).astype(F32).astype(BF16)
        values = jnp.concatenate([home_s * g_wt[q], jnp.zeros((SUBL, z.edge), F32)], axis=0)
        term = split_dot(values, hits, 3, NT_DIMS)
        rim_ghost = term if rim_ghost is None else rim_ghost + term
    sources = z.rads * z.tiles
    pulse = []
    for k in range(z.edge_rows):
        at = other * sources * z.block + z.feat_rows + k
        pulse.append(jnp.sum(recv[pl.ds(at, sources, stride=z.block), :], axis=0, keepdims=True))
    pulse = jnp.concatenate(pulse, axis=1) * outer
    rim_first = rim + lap + mixed + rim_ghost[:SUBL]
    rim_first = rim_first + jnp.where(iota((SUBL, z.edge), 0) == 3, pulse, 0.0)
    rim_second = rim_first * rim[z.fields : z.fields + 1] * dif

    row0 = tile * z.rows
    aimed = [jnp.where(iota((z.rows, z.edge), 0) == g_row[q] - row0, g_wt[q], 0.0) for q in range(z.stencil)]
    loads = [rim_s, rim_second] + ([layers_s[0]] if z.pair else [])
    stacked = []
    for load in loads:
        for f in range(z.fields):
            stacked.append(jnp.concatenate([load[f : f + 1] * aimed[q] for q in range(z.stencil)], axis=1))
    for row in (row0 - 1, row0 + z.rows):
        stacked.append(
            jnp.concatenate([rim_s * jnp.where(g_row[q] == row, g_wt[q], 0.0) for q in range(z.stencil)], axis=1)
        )
    height = len(loads) * z.fields * z.rows + 2 * SUBL
    if height % 16:
        stacked.append(jnp.zeros((16 - height % 16, z.stencil * z.edge), F32))
    stacked = jnp.concatenate(stacked, axis=0)
    spots = jnp.concatenate(g_col, axis=1)
    columns = (iota((z.cols, z.stencil * z.edge), 0) == spots).astype(F32).astype(BF16)
    ghost = split_dot(stacked, columns, 2, NT_DIMS)

    def ghost_of(step, f):
        at = (step * z.fields + f) * z.rows
        return ghost[at : at + z.rows]

    force = deposit(z, recv, panel, spread_a, spread_b)
    at = len(loads) * z.fields * z.rows
    ghost_above, ghost_below = ghost[at : at + SUBL], ghost[at + SUBL : at + 2 * SUBL]
    own_c = cond[0, 0]
    for f in range(z.fields):
        new = ghost_of(0, f) + brim(above[f : f + 1], below[f : f + 1], z.rows)
        added[f] = new + force[1] * outer if f == 3 else new
    for f in range(z.fields):
        s = added[f] * (own_c * diffus[f])
        high = ghost_above[f : f + 1] * (above[z.fields :] * diffus[f])
        low = ghost_below[f : f + 1] * (below[z.fields :] * diffus[f])
        new = early[f] + added[f] - 6.0 * s + sideways(s) + upright(s, high, low)
        new = new + coupled(z, couple, lambda e: added[e], f) + ghost_of(1, f)
        if z.pair:
            part = ghost_of(2, f)
            if f == 3:
                part = part + force[1] * (1.0 - outer)
            new = new + part * (cond2[0, 0] * diffus[f])
        if f == 3:
            new = new + force[0] * outer
        out[f] = new


def brim(high, low, rows):
    sub = iota((rows, high.shape[1]), 0)
    return jnp.where(sub == 0, high, 0.0) + jnp.where(sub == rows - 1, low, 0.0)


def last_kernel(z, late, *refs):
    if z.pair:
        cond2, mate_in, next_in, diffus, out = refs
    else:
        beside, mate_in, next_in, diffus, out = refs
    above, below = around(z, mate_in[...], next_in[...])
    for f in range(z.fields):
        high, low = above[f : f + 1], below[f : f + 1]
        if z.pair:
            far_c = cond2[0, 0]
            high = high + above[SUBL + f : SUBL + f + 1] * (far_c[:1] * diffus[f])
            low = low + below[SUBL + f : SUBL + f + 1] * (far_c[z.rows - 1 :] * diffus[f])
        new = late[f] + brim(high, low, z.rows)
        out[0, f, 0] = new if z.pair else new + beside[f]


def shifted(x, axis, step):
    count = lax.axis_size(axis)
    pairs = [(i, i + step) for i in range(count) if 0 <= i + step < count]
    return lax.ppermute(x, axis, pairs)


def both_sides(x, axis):
    return shifted(x, axis, 1) + shifted(x, axis, -1)


def beside_rows(z, mate, next_):
    pairs, links = [], []
    for rad in range(z.rads):
        at = rad * z.tiles
        other = (rad ^ 1) * z.tiles
        for i in range(z.tiles):
            pairs.append((at + i, at + (i ^ 1)))
            if 0 < i < z.tiles - 1:
                links.append((at + i, at + (i + 1 if i % 2 else i - 1)))
            else:
                links.append((at + i, other + i))
    axes = ("rad", "ang")
    return lax.ppermute(mate, axes, pairs), lax.ppermute(next_, axes, links)


def call(kernel, shapes, scratch, args, scalars=(), spaces=None, room=48, aliases=None):
    specs = [
        pl.BlockSpec(memory_space=spaces or (pltpu.SMEM if n in scalars else pltpu.VMEM))
        for n in range(len(args))
    ]
    return pl.pallas_call(
        kernel,
        out_shape=[x if isinstance(x, jax.ShapeDtypeStruct) else jax.ShapeDtypeStruct(x, F32) for x in shapes],
        in_specs=specs,
        out_specs=[pl.BlockSpec(memory_space=pltpu.VMEM)] * len(shapes),
        scratch_shapes=scratch,
        input_output_aliases=aliases or {},
        compiler_params=pltpu.CompilerParams(vmem_limit_bytes=room << 20),
    )(*args)


def body(adj, cond, diffus, couple, ghost_row, ghost_col, ghost_wt, obs_dest, obs_cell, obs_wt, misfit):
    z = Sizes(adj, obs_cell, ghost_row)
    state = (z.fields, z.rows, z.cols)
    line, lines = (SUBL, z.cols), (SUBL * (2 if z.pair else 1), z.cols)
    if z.pair:
        swap = [(0, 1), (1, 0)]
        beside = [lax.ppermute(adj, "rad", swap), lax.ppermute(cond, "rad", swap)]
    else:
        coeff = diffus[:, None, None] * cond[0, 0][None]
        beside = [both_sides(coeff * adj[0, :, 0], "rad")]
    far = beside[1:]

    given = [adj, cond, diffus, obs_dest.reshape(1, z.count), obs_cell, obs_wt, misfit]
    held = [pltpu.SMEM(x.shape, x.dtype) if x is diffus else pltpu.VMEM(x.shape, x.dtype) for x in given]
    pay, *rows = call(
        functools.partial(pack_kernel, z),
        [(z.devices, z.block, LANES), line, line],
        held + [pltpu.SemaphoreType.DMA((len(given),))],
        given,
        spaces=pltpu.HBM,
        room=64,
    )
    recv = lax.all_to_all(pay, ("panel", "rad", "ang"), split_axis=0, concat_axis=0, tiled=True)
    recv = recv.reshape(z.devices * z.block, LANES)
    rows = list(beside_rows(z, *rows))

    args = [adj, cond] + beside + [diffus, couple]
    early, mate, next_, *first = call(
        functools.partial(early_kernel, z),
        [state, lines, lines] + ([] if z.pair else [state]),
        [pltpu.VMEM(state, F32)] * (2 if z.pair else 0),
        args,
        (len(args) - 2, len(args) - 1),
    )
    points = z.rads * z.tiles * z.npr * LANES
    ends = 2 * z.cols // LANES
    mate, next_ = call(
        functools.partial(ends_kernel, z),
        [lines, lines],
        [pltpu.VMEM((2 * ends, points), BF16), pltpu.VMEM((LANES, points), BF16)],
        [recv, cond, diffus] + rows + [mate, next_],
        (2,),
        aliases={5: 0, 6: 1},
    )
    mate, next_ = beside_rows(z, mate, next_)
    args = [early, recv, cond] + far + rows + [diffus, couple]
    late, *added = call(
        functools.partial(ghost_kernel, z),
        [state] if z.pair else [state, state],
        ([pltpu.VMEM(state, F32)] if z.pair else [])
        + [pltpu.VMEM((2 * TIMES * z.hi, points), BF16), pltpu.VMEM((LOW, points), BF16)],
        args + [ghost_row, ghost_col, ghost_wt],
        (len(args) - 2, len(args) - 1),
    )
    if not z.pair:
        far = [both_sides(coeff * (first[0] + added[0]), "rad")]
    args = [late] + far + [mate, next_, diffus]
    (out,) = call(functools.partial(last_kernel, z), [adj.shape], [], args, (len(args) - 1,))
    return out


def solution(mesh):
    placed = (
        P("panel", None, "rad", "ang", None),
        P("panel", "rad", "ang", None),
        P(),
        P(),
        P(),
        P(),
        P(),
        P("panel", "rad", "ang", None),
        P("panel", "rad", None, "ang"),
        P("panel", "rad", None, "ang"),
        P("panel", "rad", None, "ang"),
    )
    return jax.shard_map(
        body,
        mesh=mesh,
        in_specs=placed,
        out_specs=P("panel", None, "rad", "ang", None),
        check_vma=False,
    )
```

```python
import functools

import jax
import jax.numpy as jnp
from jax import lax
from jax.experimental import pallas as pl
from jax.experimental.pallas import tpu as pltpu
from jax.sharding import PartitionSpec as P

LANES = 128
SUBL = 8
POINTS = 4
TIMES = 2
LOW = 256
F32 = jnp.float32
BF16 = jnp.bfloat16
NT_DIMS = (((1,), (1,)), ((), ()))


def parts_of(x, count):
    parts = []
    for _ in range(count):
        part = x.astype(BF16)
        parts.append(part)
        x = x - part.astype(F32)
    return parts


def joint_dot(x, onehot, count, dims):
    rows = x.shape[0]
    parts = [part.astype(F32) for part in parts_of(x, count)]
    spare = -(rows * count) % 16
    if spare:
        parts.append(jnp.zeros((spare, x.shape[1]), F32))
    joined = jnp.concatenate(parts, axis=0).astype(BF16)
    out = lax.dot_general(joined, onehot, dims, preferred_element_type=F32)
    return sum(out[k * rows : (k + 1) * rows] for k in range(1, count)) + out[:rows]


def iota(shape, dim):
    return lax.broadcasted_iota(jnp.int32, shape, dim)


class Sizes:
    def __init__(self, adj, obs_cell, ghost_row):
        self.fields, self.rows, self.cols = adj.shape[1], adj.shape[3], adj.shape[4]
        self.panels = lax.axis_size("panel")
        self.rads = lax.axis_size("rad")
        self.tiles = lax.axis_size("ang")
        self.devices = self.panels * self.rads * self.tiles
        self.total_rows = self.tiles * self.rows
        self.edge = 2 * self.total_rows
        self.count = obs_cell.shape[-1]
        self.slots = 2 * self.count // self.tiles
        self.spr = min(POINTS, LANES // self.slots)
        self.npr = POINTS // self.spr
        self.feat_rows = 2 * self.npr + 1
        self.edge_rows = self.edge // LANES
        self.strip = self.feat_rows + self.edge_rows
        self.block = -(-(self.strip + 2) // SUBL) * SUBL
        self.stencil = ghost_row.shape[1]
        self.hi = self.rows * self.cols // LOW
        self.pair = self.rads == 2


def rolled(x, shift, axis):
    size = x.shape[axis]
    shift = shift % size
    return x if shift == 0 else pltpu.roll(x, shift, axis)


def pack_kernel(z, *refs):
    count = 7
    given, (pay, mate, next_), held, sems = refs[:count], refs[count : count + 3], refs[count + 3 : -1], refs[-1]
    order = (3, 4, 5, 6, 2, 1, 0)
    copies = [pltpu.make_async_copy(given[n], held[n], sems.at[n]) for n in range(count)]
    for n in order:
        copies[n].start()
    adj, cond, diffus, dest, cell, wt, misfit = held
    for n in order[:4]:
        copies[n].wait()

    owner = dest[...]
    height = max(16, z.tiles)
    mine = (iota((height, z.count), 0) == owner).astype(F32)
    earlier = (iota((z.count, z.count), 0) < iota((z.count, z.count), 1)).astype(F32)
    ranks = jnp.dot(mine.astype(BF16), earlier.astype(BF16), preferred_element_type=F32)

    where = cell[0, 0]
    weight = wt[0, 0]
    mis = misfit[0, 0]
    row = ((where.astype(F32) + 0.5) * (1.0 / z.cols)).astype(jnp.int32)
    col = where - row * z.cols
    full_row = owner * z.rows + row
    edge_at = jnp.where(col == 0, full_row, jnp.where(col == z.cols - 1, z.total_rows + full_row, -1))
    hits = jnp.concatenate(
        [(iota((z.edge, z.count), 0) == edge_at[s : s + 1]).astype(F32) for s in range(POINTS)], axis=1
    )
    value = jnp.concatenate([mis[1:2] * weight[s : s + 1] for s in range(POINTS)], axis=1)
    edge_force = joint_dot(value, hits.astype(BF16), 3, NT_DIMS)

    rank = jnp.sum(ranks * mine, axis=0, keepdims=True)
    place = owner * LANES + rank.astype(jnp.int32)
    spread = (iota((z.tiles * LANES, z.count), 0) == place).astype(F32).astype(BF16)
    code = ((col // LOW) * z.rows + row) * LOW + col % LOW
    code = code.astype(F32)
    feats = []
    for g in range(z.spr):
        picked = [weight[h * z.spr + g : h * z.spr + g + 1] for h in range(z.npr)]
        picked += [code[h * z.spr + g : h * z.spr + g + 1] for h in range(z.npr)]
        picked.append(mis[g : g + 1] if g < TIMES else jnp.zeros((1, z.count), F32))
        feats += picked
    boxed = joint_dot(jnp.concatenate(feats, axis=0), spread, 3, NT_DIMS)
    slots = boxed[: z.feat_rows]
    for g in range(1, z.spr):
        slots = slots + rolled(boxed[g * z.feat_rows : (g + 1) * z.feat_rows], g * z.slots, 1)

    for n in order[4:]:
        copies[n].wait()

    lane = iota((z.rows, LANES), 1)
    sub = iota((z.rows, LANES), 0)
    strips = []
    for side in range(2):
        acc = jnp.zeros((z.rows, LANES), F32)
        for f in range(z.fields + 1):
            for inner in range(2):
                at = inner if side == 0 else z.cols - 1 - inner
                line = adj[0, f, 0, :, at : at + 1] if f < z.fields else cond[0, 0, :, at : at + 1]
                acc = jnp.where(lane == (f * 2 + inner) * z.rows + sub, line, acc)
        strips.append(jnp.sum(acc, axis=0, keepdims=True))

    common = [edge_force[:, k * LANES : (k + 1) * LANES] for k in range(z.edge_rows)] + strips
    spare = z.block - z.strip - 2
    if spare:
        common.append(jnp.zeros((spare, LANES), F32))
    common = jnp.concatenate(common, axis=0)
    for t in range(z.tiles):
        part = jnp.concatenate([slots[:, t * LANES : (t + 1) * LANES], common], axis=0)
        for group in range(z.panels * z.rads):
            pay[group * z.tiles + t] = part

    for f in range(z.fields):
        mate[f : f + 1, :], next_[f : f + 1, :] = facing(adj[0, f, 0] * (cond[0, 0] * diffus[f]))
    mate[z.fields :, :], next_[z.fields :, :] = facing(cond[0, 0])


def even_tile():
    return lax.axis_index("ang") % 2 == 0


def facing(s):
    top, bottom = s[:1], s[s.shape[0] - 1 :]
    even = even_tile()
    return jnp.where(even, bottom, top), jnp.where(even, top, bottom)


def around(z, mate, next_):
    even = even_tile()
    tile = lax.axis_index("ang")
    next_ = jnp.where((tile == 0) | (tile == z.tiles - 1), 0.0, next_)
    return jnp.where(even, next_, mate), jnp.where(even, mate, next_)


def wide(value, rows, cols):
    return jnp.concatenate([jnp.broadcast_to(value, (rows, LANES))] * (cols // LANES), axis=1)


def weights_of(z, steps, couple, rows, cols):
    dif = [wide(steps[:, f : f + 1], rows, cols) for f in range(z.fields)]
    mix = [[wide(couple[e : e + 1, c : c + 1], rows, cols) for c in range(z.fields)] for e in range(z.fields)]
    return dif, mix


def unpack_strips(z, recv, sets):
    height = 2 * z.tiles
    stacked = []
    for panel, rad in sets:
        base = (panel * z.rads + rad) * z.tiles * z.block + z.strip
        for side in range(2):
            stacked.append(recv[pl.ds(base + side, z.tiles, stride=z.block), :])
    stacked = jnp.concatenate(stacked, axis=0)
    width = 2 * SUBL * z.edge
    lane = iota((LANES, width), 1)
    slot = lane // z.edge
    inner, plane = slot // SUBL, slot % SUBL
    picks = (iota((LANES, width), 0) == (plane * 2 + inner) * z.rows + lane % z.rows).astype(F32)
    moved = joint_dot(stacked, picks.astype(BF16), 3, (((1,), (0,)), ((), ())))
    lane = iota((height, z.edge), 1)
    keep = lane // z.rows == iota((height, z.edge), 0)
    out = []
    for number in range(len(sets)):
        both = []
        for inner in range(2):
            rows = []
            for f in range(z.fields + 1):
                at = (inner * SUBL + f) * z.edge
                tile = moved[number * height : (number + 1) * height, at : at + z.edge]
                rows.append(jnp.sum(jnp.where(keep, tile, 0.0), axis=0, keepdims=True))
            both.append(jnp.concatenate(rows, axis=0))
        out.append(both)
    return out


def edge_scaled(z, values, dif):
    return values * values[z.fields : z.fields + 1] * dif


def coupled(z, mix, state, c):
    total = None
    for e in range(z.fields):
        term = state(e) * mix[e][c]
        total = term if total is None else total + term
    return total


def line_of(ref, q):
    return jnp.concatenate([ref[side, q : q + 1, :] for side in range(2)], axis=1)


def observed(z, recv, panel):
    sources = z.rads * z.tiles
    base = panel * sources * z.block
    feat = [recv[pl.ds(base + k, sources, stride=z.block), :] for k in range(z.feat_rows)]
    lane = iota((sources, LANES), 1)
    misfits = []
    for t in range(TIMES):
        mis = jnp.where(lane // z.slots == t, feat[2 * z.npr], 0.0)
        full = None
        for g in range(z.spr):
            term = rolled(mis, (g - t) * z.slots, 1)
            full = term if full is None else full + term
        misfits.append(full)
    return feat[: z.npr], [code.astype(jnp.int32) for code in feat[z.npr : 2 * z.npr]], misfits


def dealt(z, values, highs, lows, height, spread_a, spread_b):
    width = spread_b.shape[0]
    sources = highs[0].shape[0]
    sub_high = iota((height, LANES), 0)
    sub_low = iota((width, LANES), 0)
    for h in range(z.npr):
        parts = []
        for value in values[h]:
            parts += [part.astype(F32) for part in parts_of(value, 2)]
        for n in range(sources):
            at = (n * z.npr + h) * LANES
            hit = sub_high == highs[h][n : n + 1]
            for k, part in enumerate(parts):
                spread_a[k * height : (k + 1) * height, at : at + LANES] = jnp.where(hit, part[n : n + 1], 0.0).astype(BF16)
            spread_b[:, at : at + LANES] = (sub_low == lows[h][n : n + 1]).astype(F32).astype(BF16)
    grid = lax.dot_general(spread_a[...], spread_b[...], NT_DIMS, preferred_element_type=F32)
    return [
        grid[2 * k * height : (2 * k + 1) * height] + grid[(2 * k + 1) * height : (2 * k + 2) * height]
        for k in range(len(values[0]))
    ]


def deposit(z, recv, panel, spread_a, spread_b):
    weights, codes, misfits = observed(z, recv, panel)
    values = [[mis * weight for mis in misfits] for weight in weights]
    highs = [code // LOW for code in codes]
    lows = [code % LOW for code in codes]
    out = []
    for both in dealt(z, values, highs, lows, z.hi, spread_a, spread_b):
        out.append(jnp.concatenate([both[k * z.rows : (k + 1) * z.rows] for k in range(z.cols // LOW)], axis=1))
    return out


def deposit_ends(z, recv, panel, spread_a, spread_b):
    weights, codes, misfits = observed(z, recv, panel)
    values = [[misfits[1] * weight] for weight in weights]
    chunks = z.cols // LANES
    highs, lows = [], []
    for code in codes:
        row = (code // LOW) % z.rows
        chunk = (code // LOW) // z.rows * (LOW // LANES) + (code % LOW) // LANES
        end = jnp.where(row == z.rows - 1, chunk + chunks, -1)
        highs.append(jnp.where(row == 0, chunk, end))
        lows.append(code % LANES)
    (both,) = dealt(z, values, highs, lows, 2 * chunks, spread_a, spread_b)
    ends = [[both[e * chunks + k : e * chunks + k + 1] for k in range(chunks)] for e in range(2)]
    return [jnp.concatenate(end, axis=1) for end in ends]


def sideways(s):
    cols = s.shape[1]
    lane = iota(s.shape, 1)
    west = jnp.where(lane == 0, 0.0, pltpu.roll(s, 1, 1))
    east = jnp.where(lane == cols - 1, 0.0, pltpu.roll(s, cols - 1, 1))
    return west + east


def upright(s, above, below):
    rows = s.shape[0]
    sub = iota(s.shape, 0)
    north = jnp.where(sub == 0, above, pltpu.roll(s, 1, 0))
    south = jnp.where(sub == rows - 1, below, pltpu.roll(s, rows - 1, 0))
    return north + south


def own_kernel(z, adj, cond, steps, couple, out, scaled):
    dif, mix = weights_of(z, steps, couple, z.rows, z.cols)
    for f in range(z.fields):
        s = adj[0, f, 0] * (cond[0, 0] * dif[f])
        scaled[f] = s
        new = adj[0, f, 0] - 6.0 * s + sideways(s) + upright(s, 0.0, 0.0)
        out[f] = new + coupled(z, mix, lambda e: adj[0, e, 0], f)


def far_kernel(z, adj2, steps, couple, state, out):
    dif, mix = weights_of(z, steps, couple, z.rows, z.cols)
    for f in range(z.fields):
        state[f] = adj2[0, f, 0] * dif[f]
        out[f] = adj2[0, f, 0] + coupled(z, mix, lambda e: adj2[0, e, 0], f)


def early_kernel(z, cond, first, scaled, *refs):
    if z.pair:
        weighed, mixed, cond2, steps, couple, out, mate, next_, own, far = refs
    else:
        beside, steps, couple, out, mate, next_, own = refs
    dif, mix = weights_of(z, steps, couple, z.rows, z.cols)
    own_c = cond[0, 0]
    far_c = cond2[0, 0] if z.pair else None
    for f in range(z.fields):
        if z.pair:
            other = weighed[f] * far_c
            new = first[f] + other
            far[f] = mixed[f] - 6.0 * other + sideways(other) + upright(other, 0.0, 0.0) + scaled[f]
            at = SUBL + f
            mate[at : at + 1, :], next_[at : at + 1, :] = facing(other)
        else:
            new = first[f] + beside[f]
        own[f] = new
        mate[f : f + 1, :], next_[f : f + 1, :] = facing(new * (own_c * dif[f]))
    for half in range(2 if z.pair else 1):
        for ref in (mate, next_):
            ref[half * SUBL + z.fields : (half + 1) * SUBL, :] = jnp.zeros((SUBL - z.fields, z.cols), F32)
    for f in range(z.fields):
        s = own[f] * (own_c * dif[f])
        new = own[f] - 6.0 * s + sideways(s) + upright(s, 0.0, 0.0)
        new = new + coupled(z, mix, lambda e: own[e], f)
        if z.pair:
            new = new + far[f] * (far_c * dif[f])
        out[f] = new


def link_kernel(z, cond, steps, mate_row, next_row, mate_in, next_in, mate, next_):
    tile = lax.axis_index("ang")
    inner = jnp.where((tile == 0) | (tile == z.tiles - 1), 0.0, 1.0)
    cond_mate, cond_next = facing(cond[0, 0])
    for f in range(z.fields):
        dif = wide(steps[:, f : f + 1], 1, z.cols)
        mate[f : f + 1, :] = mate_in[f : f + 1, :] + mate_row[f : f + 1, :] * (cond_mate * dif)
        next_[f : f + 1, :] = next_in[f : f + 1, :] + next_row[f : f + 1, :] * (cond_next * dif * inner)


def ends_kernel(z, recv, cond, steps, mate, next_, spread_a, spread_b):
    panel, rad = lax.axis_index("panel"), lax.axis_index("rad")
    mate[...] = jnp.zeros_like(mate)
    next_[...] = jnp.zeros_like(next_)

    @pl.when(rad == z.rads - 1)
    def _():
        top, bottom = deposit_ends(z, recv, panel, spread_a, spread_b)
        weight = cond[0, 0] * wide(steps[:, 3:4], z.rows, z.cols)
        top = top * weight[:1]
        bottom = bottom * weight[z.rows - 1 :]
        even = even_tile()
        mate[...] = jnp.where(even, bottom, top)
        next_[...] = jnp.where(even, top, bottom)


def ghost_kernel(z, early, recv, cond, *refs):
    if z.pair:
        cond2, mate_in, next_in, steps, couple, grow, gcol, gwt, out, added, spread_a, spread_b = refs
    else:
        mate_in, next_in, steps, couple, grow, gcol, gwt, out, added, spread_a, spread_b = refs
    panel, rad, tile = lax.axis_index("panel"), lax.axis_index("rad"), lax.axis_index("ang")
    other = 1 - panel
    outer = jnp.where(rad == z.rads - 1, 1.0, 0.0)
    above, below = around(z, mate_in[...], next_in[...])

    sets = [(other, rad), (panel, rad)]
    if z.pair:
        sets.append((other, 1 - rad))
        near = [1.0]
    else:
        sets += [(other, jnp.maximum(rad - 1, 0)), (other, jnp.minimum(rad + 1, z.rads - 1))]
        near = [jnp.where(rad > 0, 1.0, 0.0), jnp.where(rad < z.rads - 1, 1.0, 0.0)]
    strips = unpack_strips(z, recv, sets)
    dif, mix = weights_of(z, steps, couple, z.rows, z.cols)
    plane = iota((SUBL, z.edge), 0)
    by_plane = jnp.zeros((SUBL, z.edge), F32)
    for f in range(z.fields):
        by_plane = jnp.where(plane == f, wide(steps[:, f : f + 1], SUBL, z.edge), by_plane)
    rim, inside = strips[0]
    rim_s = edge_scaled(z, rim, by_plane)
    home_s = edge_scaled(z, strips[1][0], by_plane)
    layers_s = [edge_scaled(z, strips[2 + k][0], by_plane) for k in range(len(near))]
    lap = edge_scaled(z, inside, by_plane) - 6.0 * rim_s
    for k, one in enumerate(near):
        lap = lap + layers_s[k] * one
    spot = iota((SUBL, z.edge), 1) % z.total_rows
    lap = lap + jnp.where(spot == 0, 0.0, pltpu.roll(rim_s, 1, 1))
    lap = lap + jnp.where(spot == z.total_rows - 1, 0.0, pltpu.roll(rim_s, z.edge - 1, 1))
    thin = [[mix[e][f][:1, : z.edge] for f in range(z.fields)] for e in range(z.fields)]
    rows = [coupled(z, thin, lambda e: rim[e : e + 1], c) for c in range(z.fields)]
    mixed = jnp.concatenate(rows + [jnp.zeros((SUBL - z.fields, z.edge), F32)], axis=0)

    g_row = [line_of(grow, q) for q in range(z.stencil)]
    g_col = [line_of(gcol, q) for q in range(z.stencil)]
    g_wt = [line_of(gwt, q) for q in range(z.stencil)]
    targets = []
    for q in range(z.stencil):
        last_one = jnp.where(g_col[q] == z.cols - 1, z.total_rows + g_row[q], -1)
        targets.append(jnp.where(g_col[q] == 0, g_row[q], last_one))
    hits = (iota((z.edge, z.stencil * z.edge), 0) == jnp.concatenate(targets, axis=1)).astype(F32)
    values = jnp.concatenate([home_s * g_wt[q] for q in range(z.stencil)], axis=1)
    rim_ghost = joint_dot(values, hits.astype(BF16), 3, NT_DIMS)
    sources = z.rads * z.tiles
    pulse = []
    for k in range(z.edge_rows):
        at = other * sources * z.block + z.feat_rows + k
        pulse.append(jnp.sum(recv[pl.ds(at, sources, stride=z.block), :], axis=0, keepdims=True))
    pulse = jnp.concatenate(pulse, axis=1) * outer
    rim_first = rim + lap + mixed + rim_ghost
    rim_first = rim_first + jnp.where(iota((SUBL, z.edge), 0) == 3, pulse, 0.0)
    rim_second = rim_first * rim[z.fields : z.fields + 1] * by_plane

    row0 = tile * z.rows
    aimed = [jnp.where(iota((z.rows, z.edge), 0) == g_row[q] - row0, g_wt[q], 0.0) for q in range(z.stencil)]
    loads = [rim_s, rim_second] + ([layers_s[0]] if z.pair else [])
    stacked = []
    for load in loads:
        for f in range(z.fields):
            stacked.append(jnp.concatenate([load[f : f + 1] * aimed[q] for q in range(z.stencil)], axis=1))
    for row in (row0 - 1, row0 + z.rows):
        stacked.append(
            jnp.concatenate([rim_s * jnp.where(g_row[q] == row, g_wt[q], 0.0) for q in range(z.stencil)], axis=1)
        )
    stacked = jnp.concatenate(stacked, axis=0)
    spots = jnp.concatenate(g_col, axis=1)
    columns = (iota((z.cols, z.stencil * z.edge), 0) == spots).astype(F32).astype(BF16)
    ghost = joint_dot(stacked, columns, 2, NT_DIMS)

    def ghost_of(step, f):
        at = (step * z.fields + f) * z.rows
        return ghost[at : at + z.rows]

    force = deposit(z, recv, panel, spread_a, spread_b)
    at = len(loads) * z.fields * z.rows
    ghost_above, ghost_below = ghost[at : at + SUBL], ghost[at + SUBL : at + 2 * SUBL]
    own_c = cond[0, 0]
    for f in range(z.fields):
        new = ghost_of(0, f) + brim(above[f : f + 1], below[f : f + 1], z.rows)
        added[f] = new + force[1] * outer if f == 3 else new
    for f in range(z.fields):
        s = added[f] * (own_c * dif[f])
        high = ghost_above[f : f + 1] * (above[z.fields :] * dif[f][:1])
        low = ghost_below[f : f + 1] * (below[z.fields :] * dif[f][:1])
        new = early[f] + added[f] - 6.0 * s + sideways(s) + upright(s, high, low)
        new = new + coupled(z, mix, lambda e: added[e], f) + ghost_of(1, f)
        if z.pair:
            part = ghost_of(2, f)
            if f == 3:
                part = part + force[1] * (1.0 - outer)
            new = new + part * (cond2[0, 0] * dif[f])
        if f == 3:
            new = new + force[0] * outer
        out[f] = new


def brim(high, low, rows):
    sub = iota((rows, high.shape[1]), 0)
    return jnp.where(sub == 0, high, 0.0) + jnp.where(sub == rows - 1, low, 0.0)


def last_kernel(z, late, *refs):
    if z.pair:
        cond2, mate_in, next_in, mate_end, next_end, steps, out = refs
    else:
        beside, mate_in, next_in, mate_end, next_end, steps, out = refs
    above, below = around(z, mate_in[...], next_in[...])
    above_end, below_end = around(z, mate_end[...], next_end[...])
    for f in range(z.fields):
        high, low = above[f : f + 1], below[f : f + 1]
        if f == 3:
            high, low = high + above_end, low + below_end
        if z.pair:
            far_c = cond2[0, 0] * wide(steps[:, f : f + 1], z.rows, z.cols)
            high = high + above[SUBL + f : SUBL + f + 1] * far_c[:1]
            low = low + below[SUBL + f : SUBL + f + 1] * far_c[z.rows - 1 :]
        new = late[f] + brim(high, low, z.rows)
        out[0, f, 0] = new if z.pair else new + beside[f]


def shifted(x, axis, step):
    count = lax.axis_size(axis)
    pairs = [(i, i + step) for i in range(count) if 0 <= i + step < count]
    return lax.ppermute(x, axis, pairs)


def both_sides(x, axis):
    return shifted(x, axis, 1) + shifted(x, axis, -1)


def beside_rows(z, mate, next_):
    pairs, links = [], []
    for rad in range(z.rads):
        at = rad * z.tiles
        other = (rad ^ 1) * z.tiles
        for i in range(z.tiles):
            pairs.append((at + i, at + (i ^ 1)))
            if 0 < i < z.tiles - 1:
                links.append((at + i, at + (i + 1 if i % 2 else i - 1)))
            else:
                links.append((at + i, other + i))
    axes = ("rad", "ang")
    return lax.ppermute(mate, axes, pairs), lax.ppermute(next_, axes, links)


def outer_rows(z, mate, next_):
    pairs, links = [], []
    for panel in range(z.panels):
        for rad in range(z.rads):
            at = (panel * z.rads + rad) * z.tiles
            for i in range(z.tiles):
                pairs.append((at + i, at + (i ^ 1)))
                if rad < z.rads - 1:
                    links.append((at + i, at + (i ^ 1)))
                elif 0 < i < z.tiles - 1:
                    links.append((at + i, at + (i + 1 if i % 2 else i - 1)))
                else:
                    links.append((at + i, ((panel ^ 1) * z.rads + rad) * z.tiles + i))
    axes = ("panel", "rad", "ang")
    return lax.ppermute(mate, axes, pairs), lax.ppermute(next_, axes, links)


def call(kernel, shapes, scratch, args, spaces=pltpu.VMEM, room=48, aliases=None):
    return pl.pallas_call(
        kernel,
        out_shape=[jax.ShapeDtypeStruct(shape, F32) for shape in shapes],
        in_specs=[pl.BlockSpec(memory_space=spaces)] * len(args),
        out_specs=[pl.BlockSpec(memory_space=pltpu.VMEM)] * len(shapes),
        scratch_shapes=scratch,
        input_output_aliases=aliases or {},
        compiler_params=pltpu.CompilerParams(vmem_limit_bytes=room << 20),
    )(*args)


def body(adj, cond, diffus, couple, ghost_row, ghost_col, ghost_wt, obs_dest, obs_cell, obs_wt, misfit):
    z = Sizes(adj, obs_cell, ghost_row)
    state = (z.fields, z.rows, z.cols)
    line, lines = (SUBL, z.cols), (SUBL * (2 if z.pair else 1), z.cols)
    if z.pair:
        swap = [(0, 1), (1, 0)]
        beside = [lax.ppermute(adj, "rad", swap), lax.ppermute(cond, "rad", swap)]
    else:
        coeff = diffus[:, None, None] * cond[0, 0][None]
        beside = [both_sides(coeff * adj[0, :, 0], "rad")]
    far = beside[1:]

    given = [adj, cond, diffus, obs_dest.reshape(1, z.count), obs_cell, obs_wt, misfit]
    held = [pltpu.SMEM(x.shape, x.dtype) if x is diffus else pltpu.VMEM(x.shape, x.dtype) for x in given]
    pay, *rows = call(
        functools.partial(pack_kernel, z),
        [(z.devices, z.block, LANES), line, line],
        held + [pltpu.SemaphoreType.DMA((len(given),))],
        given,
        spaces=pltpu.HBM,
        room=64,
    )
    recv = lax.all_to_all(pay, ("panel", "rad", "ang"), split_axis=0, concat_axis=0, tiled=True)
    recv = recv.reshape(z.devices * z.block, LANES)
    rows = list(beside_rows(z, *rows))

    steps = diffus.reshape(1, z.fields)
    own = call(functools.partial(own_kernel, z), [state, state], [], [adj, cond, steps, couple])
    if z.pair:
        beside[:1] = call(functools.partial(far_kernel, z), [state, state], [], [beside[0], steps, couple])
    args = [cond] + list(own) + beside + [steps, couple]
    early, mate, next_, *first = call(
        functools.partial(early_kernel, z),
        [state, lines, lines] + ([] if z.pair else [state]),
        [pltpu.VMEM(state, F32)] * (2 if z.pair else 0),
        args,
    )
    links = call(
        functools.partial(link_kernel, z),
        [lines, lines],
        [],
        [cond, steps] + rows + [mate, next_],
        aliases={4: 0, 5: 1},
    )
    beyond = list(beside_rows(z, *links))
    points = z.rads * z.tiles * z.npr * LANES
    ends = 2 * z.cols // LANES
    ends = call(
        functools.partial(ends_kernel, z),
        [(1, z.cols), (1, z.cols)],
        [pltpu.VMEM((2 * ends, points), BF16), pltpu.VMEM((LANES, points), BF16)],
        [recv, cond, steps],
    )
    beyond += outer_rows(z, *ends)
    args = [early, recv, cond] + far + rows + [steps, couple]
    late, *added = call(
        functools.partial(ghost_kernel, z),
        [state] if z.pair else [state, state],
        ([pltpu.VMEM(state, F32)] if z.pair else [])
        + [pltpu.VMEM((2 * TIMES * z.hi, points), BF16), pltpu.VMEM((LOW, points), BF16)],
        args + [ghost_row, ghost_col, ghost_wt],
    )
    if not z.pair:
        far = [both_sides(coeff * (first[0] + added[0]), "rad")]
    args = [late] + far + beyond + [steps]
    (out,) = call(functools.partial(last_kernel, z), [adj.shape], [], args)
    return out


def solution(mesh):
    placed = (
        P("panel", None, "rad", "ang", None),
        P("panel", "rad", "ang", None),
        P(),
        P(),
        P(),
        P(),
        P(),
        P("panel", "rad", "ang", None),
        P("panel", "rad", None, "ang"),
        P("panel", "rad", None, "ang"),
        P("panel", "rad", None, "ang"),
    )
    return jax.shard_map(
        body,
        mesh=mesh,
        in_specs=placed,
        out_specs=P("panel", None, "rad", "ang", None),
        check_vma=False,
    )
```

```python
import functools

import jax
import jax.numpy as jnp
from jax import lax
from jax.experimental import pallas as pl
from jax.experimental.pallas import tpu as pltpu
from jax.sharding import PartitionSpec as P

LANES = 128
SUBL = 8
POINTS = 4
TIMES = 2
LOW = 256
F32 = jnp.float32
BF16 = jnp.bfloat16
NT_DIMS = (((1,), (1,)), ((), ()))


def parts_of(x, count):
    parts = []
    for _ in range(count):
        part = x.astype(BF16)
        parts.append(part)
        x = x - part.astype(F32)
    return parts


def joint_dot(x, onehot, count, dims):
    rows = x.shape[0]
    parts = [part.astype(F32) for part in parts_of(x, count)]
    spare = -(rows * count) % 16
    if spare:
        parts.append(jnp.zeros((spare, x.shape[1]), F32))
    joined = jnp.concatenate(parts, axis=0).astype(BF16)
    out = lax.dot_general(joined, onehot, dims, preferred_element_type=F32)
    return sum(out[k * rows : (k + 1) * rows] for k in range(1, count)) + out[:rows]


def iota(shape, dim):
    return lax.broadcasted_iota(jnp.int32, shape, dim)


class Sizes:
    def __init__(self, adj, obs_cell, ghost_row):
        self.fields, self.rows, self.cols = adj.shape[1], adj.shape[3], adj.shape[4]
        self.panels = lax.axis_size("panel")
        self.rads = lax.axis_size("rad")
        self.tiles = lax.axis_size("ang")
        self.devices = self.panels * self.rads * self.tiles
        self.total_rows = self.tiles * self.rows
        self.edge = 2 * self.total_rows
        self.count = obs_cell.shape[-1]
        self.slots = 2 * self.count // self.tiles
        self.spr = min(POINTS, LANES // self.slots)
        self.npr = POINTS // self.spr
        self.feat_rows = 2 * self.npr + 1
        self.edge_rows = self.edge // LANES
        self.strip = self.feat_rows + self.edge_rows
        self.block = -(-(self.strip + 2) // SUBL) * SUBL
        self.stencil = ghost_row.shape[1]
        self.hi = self.rows * self.cols // LOW
        self.pair = self.rads == 2


def rolled(x, shift, axis):
    size = x.shape[axis]
    shift = shift % size
    return x if shift == 0 else pltpu.roll(x, shift, axis)


def pack_kernel(z, *refs):
    count = 7
    given, (pay, mate, next_), held, sems = refs[:count], refs[count : count + 3], refs[count + 3 : -1], refs[-1]
    order = (3, 4, 5, 6, 2, 1, 0)
    copies = [pltpu.make_async_copy(given[n], held[n], sems.at[n]) for n in range(count)]
    for n in order:
        copies[n].start()
    adj, cond, diffus, dest, cell, wt, misfit = held
    for n in order[:4]:
        copies[n].wait()

    owner = dest[...]
    height = max(16, z.tiles)
    mine = (iota((height, z.count), 0) == owner).astype(F32)
    earlier = (iota((z.count, z.count), 0) < iota((z.count, z.count), 1)).astype(F32)
    ranks = jnp.dot(mine.astype(BF16), earlier.astype(BF16), preferred_element_type=F32)

    where = cell[0, 0]
    weight = wt[0, 0]
    mis = misfit[0, 0]
    row = ((where.astype(F32) + 0.5) * (1.0 / z.cols)).astype(jnp.int32)
    col = where - row * z.cols
    full_row = owner * z.rows + row
    edge_at = jnp.where(col == 0, full_row, jnp.where(col == z.cols - 1, z.total_rows + full_row, -1))
    hits = jnp.concatenate(
        [(iota((z.edge, z.count), 0) == edge_at[s : s + 1]).astype(F32) for s in range(POINTS)], axis=1
    )
    value = jnp.concatenate([mis[1:2] * weight[s : s + 1] for s in range(POINTS)], axis=1)
    edge_force = joint_dot(value, hits.astype(BF16), 3, NT_DIMS)

    rank = jnp.sum(ranks * mine, axis=0, keepdims=True)
    place = owner * LANES + rank.astype(jnp.int32)
    spread = (iota((z.tiles * LANES, z.count), 0) == place).astype(F32).astype(BF16)
    code = ((col // LOW) * z.rows + row) * LOW + col % LOW
    code = code.astype(F32)
    feats = []
    for g in range(z.spr):
        picked = [weight[h * z.spr + g : h * z.spr + g + 1] for h in range(z.npr)]
        picked += [code[h * z.spr + g : h * z.spr + g + 1] for h in range(z.npr)]
        picked.append(mis[g : g + 1] if g < TIMES else jnp.zeros((1, z.count), F32))
        feats += picked
    boxed = joint_dot(jnp.concatenate(feats, axis=0), spread, 3, NT_DIMS)
    slots = boxed[: z.feat_rows]
    for g in range(1, z.spr):
        slots = slots + rolled(boxed[g * z.feat_rows : (g + 1) * z.feat_rows], g * z.slots, 1)

    for n in order[4:]:
        copies[n].wait()

    lane = iota((z.rows, LANES), 1)
    sub = iota((z.rows, LANES), 0)
    strips = []
    for side in range(2):
        acc = jnp.zeros((z.rows, LANES), F32)
        for f in range(z.fields + 1):
            for inner in range(2):
                at = inner if side == 0 else z.cols - 1 - inner
                line = adj[0, f, 0, :, at : at + 1] if f < z.fields else cond[0, 0, :, at : at + 1]
                acc = jnp.where(lane == (f * 2 + inner) * z.rows + sub, line, acc)
        strips.append(jnp.sum(acc, axis=0, keepdims=True))

    common = [edge_force[:, k * LANES : (k + 1) * LANES] for k in range(z.edge_rows)] + strips
    spare = z.block - z.strip - 2
    if spare:
        common.append(jnp.zeros((spare, LANES), F32))
    common = jnp.concatenate(common, axis=0)
    for t in range(z.tiles):
        part = jnp.concatenate([slots[:, t * LANES : (t + 1) * LANES], common], axis=0)
        for group in range(z.panels * z.rads):
            pay[group * z.tiles + t] = part

    for f in range(z.fields):
        mate[f : f + 1, :], next_[f : f + 1, :] = facing(adj[0, f, 0] * (cond[0, 0] * diffus[f]))
    mate[z.fields :, :], next_[z.fields :, :] = facing(cond[0, 0])


def even_tile():
    return lax.axis_index("ang") % 2 == 0


def facing(s):
    top, bottom = s[:1], s[s.shape[0] - 1 :]
    even = even_tile()
    return jnp.where(even, bottom, top), jnp.where(even, top, bottom)


def around(z, mate, next_):
    even = even_tile()
    tile = lax.axis_index("ang")
    next_ = jnp.where((tile == 0) | (tile == z.tiles - 1), 0.0, next_)
    return jnp.where(even, next_, mate), jnp.where(even, mate, next_)


def wide(value, rows, cols):
    return jnp.concatenate([jnp.broadcast_to(value, (rows, LANES))] * (cols // LANES), axis=1)


def weights_of(z, steps, couple, rows, cols):
    dif = [wide(steps[:, f : f + 1], rows, cols) for f in range(z.fields)]
    mix = [[wide(couple[e : e + 1, c : c + 1], rows, cols) for c in range(z.fields)] for e in range(z.fields)]
    return dif, mix


def unpack_strips(z, recv, sets):
    height = 2 * z.tiles
    stacked = []
    for panel, rad in sets:
        base = (panel * z.rads + rad) * z.tiles * z.block + z.strip
        for side in range(2):
            stacked.append(recv[pl.ds(base + side, z.tiles, stride=z.block), :])
    stacked = jnp.concatenate(stacked, axis=0)
    width = 2 * SUBL * z.edge
    lane = iota((LANES, width), 1)
    slot = lane // z.edge
    inner, plane = slot // SUBL, slot % SUBL
    picks = (iota((LANES, width), 0) == (plane * 2 + inner) * z.rows + lane % z.rows).astype(F32)
    moved = joint_dot(stacked, picks.astype(BF16), 3, (((1,), (0,)), ((), ())))
    lane = iota((height, z.edge), 1)
    keep = lane // z.rows == iota((height, z.edge), 0)
    out = []
    for number in range(len(sets)):
        both = []
        for inner in range(2):
            rows = []
            for f in range(z.fields + 1):
                at = (inner * SUBL + f) * z.edge
                tile = moved[number * height : (number + 1) * height, at : at + z.edge]
                rows.append(jnp.sum(jnp.where(keep, tile, 0.0), axis=0, keepdims=True))
            both.append(jnp.concatenate(rows, axis=0))
        out.append(both)
    return out


def edge_scaled(z, values, dif):
    return values * values[z.fields : z.fields + 1] * dif


def coupled(z, mix, state, c):
    total = None
    for e in range(z.fields):
        term = state(e) * mix[e][c]
        total = term if total is None else total + term
    return total


def line_of(ref, q):
    return jnp.concatenate([ref[side, q : q + 1, :] for side in range(2)], axis=1)


def observed(z, recv, panel):
    sources = z.rads * z.tiles
    base = panel * sources * z.block
    feat = [recv[pl.ds(base + k, sources, stride=z.block), :] for k in range(z.feat_rows)]
    lane = iota((sources, LANES), 1)
    misfits = []
    for t in range(TIMES):
        mis = jnp.where(lane // z.slots == t, feat[2 * z.npr], 0.0)
        full = None
        for g in range(z.spr):
            term = rolled(mis, (g - t) * z.slots, 1)
            full = term if full is None else full + term
        misfits.append(full)
    return feat[: z.npr], [code.astype(jnp.int32) for code in feat[z.npr : 2 * z.npr]], misfits


def dealt(z, values, highs, lows, height, spread_a, spread_b):
    width = spread_b.shape[0]
    sources = highs[0].shape[0]
    used = 2 * len(values[0]) * height
    sub_high = iota((height, LANES), 0)
    sub_low = iota((width, LANES), 0)
    for h in range(z.npr):
        parts = []
        for value in values[h]:
            parts += [part.astype(F32) for part in parts_of(value, 2)]
        for n in range(sources):
            at = (n * z.npr + h) * LANES
            hit = sub_high == highs[h][n : n + 1]
            for k, part in enumerate(parts):
                spread_a[k * height : (k + 1) * height, at : at + LANES] = jnp.where(hit, part[n : n + 1], 0.0).astype(BF16)
            spread_b[:, at : at + LANES] = (sub_low == lows[h][n : n + 1]).astype(F32).astype(BF16)
    grid = lax.dot_general(spread_a[:used, :], spread_b[...], NT_DIMS, preferred_element_type=F32)
    return [
        grid[2 * k * height : (2 * k + 1) * height] + grid[(2 * k + 1) * height : (2 * k + 2) * height]
        for k in range(len(values[0]))
    ]


def deposit(z, recv, panel, times, spread_a, spread_b):
    weights, codes, misfits = observed(z, recv, panel)
    values = [[misfits[t] * weight for t in times] for weight in weights]
    highs = [code // LOW for code in codes]
    lows = [code % LOW for code in codes]
    out = []
    for both in dealt(z, values, highs, lows, z.hi, spread_a, spread_b):
        out.append(jnp.concatenate([both[k * z.rows : (k + 1) * z.rows] for k in range(z.cols // LOW)], axis=1))
    return out


def deposit_ends(z, recv, panel, spread_a, spread_b):
    weights, codes, misfits = observed(z, recv, panel)
    values = [[misfits[1] * weight] for weight in weights]
    chunks = z.cols // LANES
    highs, lows = [], []
    for code in codes:
        row = (code // LOW) % z.rows
        chunk = (code // LOW) // z.rows * (LOW // LANES) + (code % LOW) // LANES
        end = jnp.where(row == z.rows - 1, chunk + chunks, -1)
        highs.append(jnp.where(row == 0, chunk, end))
        lows.append(code % LANES)
    (both,) = dealt(z, values, highs, lows, 2 * chunks, spread_a, spread_b)
    ends = [[both[e * chunks + k : e * chunks + k + 1] for k in range(chunks)] for e in range(2)]
    return [jnp.concatenate(end, axis=1) for end in ends]


def sideways(s):
    cols = s.shape[1]
    lane = iota(s.shape, 1)
    west = jnp.where(lane == 0, 0.0, pltpu.roll(s, 1, 1))
    east = jnp.where(lane == cols - 1, 0.0, pltpu.roll(s, cols - 1, 1))
    return west + east


def upright(s, above, below):
    rows = s.shape[0]
    sub = iota(s.shape, 0)
    north = jnp.where(sub == 0, above, pltpu.roll(s, 1, 0))
    south = jnp.where(sub == rows - 1, below, pltpu.roll(s, rows - 1, 0))
    return north + south


def far_kernel(z, adj2, out):
    out[...] = adj2[0, :, 0]


def early_kernel(z, adj, cond, *refs):
    if z.pair:
        adj2, cond2, steps, couple, out, mate, next_, own, far = refs
    else:
        beside, steps, couple, out, mate, next_, own = refs
    dif, mix = weights_of(z, steps, couple, z.rows, z.cols)
    own_c = cond[0, 0]
    far_c = cond2[0, 0] if z.pair else None
    for f in range(z.fields):
        s = adj[0, f, 0] * (own_c * dif[f])
        new = adj[0, f, 0] - 6.0 * s + sideways(s) + upright(s, 0.0, 0.0)
        new = new + coupled(z, mix, lambda e: adj[0, e, 0], f)
        if z.pair:
            other = adj2[f] * (far_c * dif[f])
            new = new + other
            part = adj2[f] - 6.0 * other + sideways(other) + upright(other, 0.0, 0.0) + s
            far[f] = part + coupled(z, mix, lambda e: adj2[e], f)
            at = SUBL + f
            mate[at : at + 1, :], next_[at : at + 1, :] = facing(other)
        else:
            new = new + beside[f]
        own[f] = new
        mate[f : f + 1, :], next_[f : f + 1, :] = facing(new * (own_c * dif[f]))
    for half in range(2 if z.pair else 1):
        for ref in (mate, next_):
            ref[half * SUBL + z.fields : (half + 1) * SUBL, :] = jnp.zeros((SUBL - z.fields, z.cols), F32)
    for f in range(z.fields):
        s = own[f] * (own_c * dif[f])
        new = own[f] - 6.0 * s + sideways(s) + upright(s, 0.0, 0.0)
        new = new + coupled(z, mix, lambda e: own[e], f)
        if z.pair:
            new = new + far[f] * (far_c * dif[f])
        out[f] = new


def link_kernel(z, cond, steps, mate_row, next_row, mate_in, next_in, mate, next_):
    tile = lax.axis_index("ang")
    inner = jnp.where((tile == 0) | (tile == z.tiles - 1), 0.0, 1.0)
    cond_mate, cond_next = facing(cond[0, 0])
    for f in range(z.fields):
        dif = wide(steps[:, f : f + 1], 1, z.cols)
        mate[f : f + 1, :] = mate_in[f : f + 1, :] + mate_row[f : f + 1, :] * (cond_mate * dif)
        next_[f : f + 1, :] = next_in[f : f + 1, :] + next_row[f : f + 1, :] * (cond_next * dif * inner)


def is_outer(z):
    return lax.axis_index("rad") == z.rads - 1


def ends_kernel(z, recv, cond, steps, mate_in, next_in, mate, next_, spread_a, spread_b):
    panel = lax.axis_index("panel")
    next_[mate.shape[0] :, :] = jnp.zeros((next_.shape[0] - mate.shape[0], z.cols), F32)
    for f in range(mate.shape[0]):
        at = f % z.fields + f // z.fields * SUBL
        mate[f : f + 1, :] = mate_in[at : at + 1, :]
        next_[f : f + 1, :] = next_in[at : at + 1, :]

    @pl.when(is_outer(z))
    def _():
        top, bottom = deposit_ends(z, recv, panel, spread_a, spread_b)
        weight = cond[0, 0] * wide(steps[:, 3:4], z.rows, z.cols)
        top = top * weight[:1]
        bottom = bottom * weight[z.rows - 1 :]
        even = even_tile()
        mate[3:4, :] = mate_in[3:4, :] + jnp.where(even, bottom, top)
        next_[3:4, :] = next_in[3:4, :] + jnp.where(even, top, bottom)


def ghost_kernel(z, early, recv, cond, *refs):
    if z.pair:
        cond2, mate_in, next_in, steps, couple, grow, gcol, gwt, out, added, spread_a, spread_b = refs
    else:
        mate_in, next_in, steps, couple, grow, gcol, gwt, out, added, spread_a, spread_b = refs
    panel, rad, tile = lax.axis_index("panel"), lax.axis_index("rad"), lax.axis_index("ang")
    other = 1 - panel
    outer = jnp.where(rad == z.rads - 1, 1.0, 0.0)
    above, below = around(z, mate_in[...], next_in[...])

    sets = [(other, rad), (panel, rad)]
    if z.pair:
        sets.append((other, 1 - rad))
        near = [1.0]
    else:
        sets += [(other, jnp.maximum(rad - 1, 0)), (other, jnp.minimum(rad + 1, z.rads - 1))]
        near = [jnp.where(rad > 0, 1.0, 0.0), jnp.where(rad < z.rads - 1, 1.0, 0.0)]
    strips = unpack_strips(z, recv, sets)
    dif, mix = weights_of(z, steps, couple, z.rows, z.cols)
    plane = iota((SUBL, z.edge), 0)
    by_plane = jnp.zeros((SUBL, z.edge), F32)
    for f in range(z.fields):
        by_plane = jnp.where(plane == f, wide(steps[:, f : f + 1], SUBL, z.edge), by_plane)
    rim, inside = strips[0]
    rim_s = edge_scaled(z, rim, by_plane)
    home_s = edge_scaled(z, strips[1][0], by_plane)
    layers_s = [edge_scaled(z, strips[2 + k][0], by_plane) for k in range(len(near))]
    lap = edge_scaled(z, inside, by_plane) - 6.0 * rim_s
    for k, one in enumerate(near):
        lap = lap + layers_s[k] * one
    spot = iota((SUBL, z.edge), 1) % z.total_rows
    lap = lap + jnp.where(spot == 0, 0.0, pltpu.roll(rim_s, 1, 1))
    lap = lap + jnp.where(spot == z.total_rows - 1, 0.0, pltpu.roll(rim_s, z.edge - 1, 1))
    thin = [[mix[e][f][:1, : z.edge] for f in range(z.fields)] for e in range(z.fields)]
    rows = [coupled(z, thin, lambda e: rim[e : e + 1], c) for c in range(z.fields)]
    mixed = jnp.concatenate(rows + [jnp.zeros((SUBL - z.fields, z.edge), F32)], axis=0)

    g_row = [line_of(grow, q) for q in range(z.stencil)]
    g_col = [line_of(gcol, q) for q in range(z.stencil)]
    g_wt = [line_of(gwt, q) for q in range(z.stencil)]
    targets = []
    for q in range(z.stencil):
        last_one = jnp.where(g_col[q] == z.cols - 1, z.total_rows + g_row[q], -1)
        targets.append(jnp.where(g_col[q] == 0, g_row[q], last_one))
    hits = (iota((z.edge, z.stencil * z.edge), 0) == jnp.concatenate(targets, axis=1)).astype(F32)
    values = jnp.concatenate([home_s * g_wt[q] for q in range(z.stencil)], axis=1)
    rim_ghost = joint_dot(values, hits.astype(BF16), 3, NT_DIMS)
    sources = z.rads * z.tiles
    pulse = []
    for k in range(z.edge_rows):
        at = other * sources * z.block + z.feat_rows + k
        pulse.append(jnp.sum(recv[pl.ds(at, sources, stride=z.block), :], axis=0, keepdims=True))
    pulse = jnp.concatenate(pulse, axis=1) * outer
    rim_first = rim + lap + mixed + rim_ghost
    rim_first = rim_first + jnp.where(iota((SUBL, z.edge), 0) == 3, pulse, 0.0)
    rim_second = rim_first * rim[z.fields : z.fields + 1] * by_plane

    row0 = tile * z.rows
    aimed = [jnp.where(iota((z.rows, z.edge), 0) == g_row[q] - row0, g_wt[q], 0.0) for q in range(z.stencil)]
    loads = [rim_s, rim_second] + ([layers_s[0]] if z.pair else [])
    stacked = []
    for load in loads:
        for f in range(z.fields):
            stacked.append(jnp.concatenate([load[f : f + 1] * aimed[q] for q in range(z.stencil)], axis=1))
    for row in (row0 - 1, row0 + z.rows):
        stacked.append(
            jnp.concatenate([rim_s * jnp.where(g_row[q] == row, g_wt[q], 0.0) for q in range(z.stencil)], axis=1)
        )
    stacked = jnp.concatenate(stacked, axis=0)
    spots = jnp.concatenate(g_col, axis=1)
    columns = (iota((z.cols, z.stencil * z.edge), 0) == spots).astype(F32).astype(BF16)
    ghost = joint_dot(stacked, columns, 2, NT_DIMS)

    def ghost_of(step, f):
        at = (step * z.fields + f) * z.rows
        return ghost[at : at + z.rows]

    force = deposit(z, recv, panel, (0, 1), spread_a, spread_b)
    at = len(loads) * z.fields * z.rows
    ghost_above, ghost_below = ghost[at : at + SUBL], ghost[at + SUBL : at + 2 * SUBL]
    own_c = cond[0, 0]
    for f in range(z.fields):
        new = ghost_of(0, f) + brim(above[f : f + 1], below[f : f + 1], z.rows)
        added[f] = new + force[1] * outer if f == 3 else new
    for f in range(z.fields):
        s = added[f] * (own_c * dif[f])
        high = ghost_above[f : f + 1] * (above[z.fields :] * dif[f][:1])
        low = ghost_below[f : f + 1] * (below[z.fields :] * dif[f][:1])
        new = early[f] + added[f] - 6.0 * s + sideways(s) + upright(s, high, low)
        new = new + coupled(z, mix, lambda e: added[e], f) + ghost_of(1, f)
        if z.pair:
            part = ghost_of(2, f)
            if f == 3:
                part = part + force[1] * (1.0 - outer)
            new = new + part * (cond2[0, 0] * dif[f])
        if f == 3:
            new = new + force[0] * outer
        out[f] = new


def brim(high, low, rows):
    sub = iota((rows, high.shape[1]), 0)
    return jnp.where(sub == 0, high, 0.0) + jnp.where(sub == rows - 1, low, 0.0)


def last_kernel(z, late, *refs):
    if z.pair:
        cond2, mate_inner, next_inner, mate_outer, next_outer, steps, out = refs
    else:
        beside, mate_inner, next_inner, mate_outer, next_outer, steps, out = refs
    outer = is_outer(z)

    def beyond(half, f):
        inner_at, outer_at = half * SUBL + f, half * z.fields + f
        mate_in = jnp.where(outer, mate_outer[outer_at : outer_at + 1, :], mate_inner[inner_at : inner_at + 1, :])
        next_in = jnp.where(outer, next_outer[outer_at : outer_at + 1, :], next_inner[inner_at : inner_at + 1, :])
        return around(z, mate_in, next_in)

    for f in range(z.fields):
        high, low = beyond(0, f)
        if z.pair:
            far_high, far_low = beyond(1, f)
            far_c = cond2[0, 0] * wide(steps[:, f : f + 1], z.rows, z.cols)
            high = high + far_high * far_c[:1]
            low = low + far_low * far_c[z.rows - 1 :]
        new = late[f] + brim(high, low, z.rows)
        out[0, f, 0] = new if z.pair else new + beside[f]


def shifted(x, axis, step):
    count = lax.axis_size(axis)
    pairs = [(i, i + step) for i in range(count) if 0 <= i + step < count]
    return lax.ppermute(x, axis, pairs)


def both_sides(x, axis):
    return shifted(x, axis, 1) + shifted(x, axis, -1)


def beside_rows(z, mate, next_):
    pairs, links = [], []
    for rad in range(z.rads):
        at = rad * z.tiles
        other = (rad ^ 1) * z.tiles
        for i in range(z.tiles):
            pairs.append((at + i, at + (i ^ 1)))
            if 0 < i < z.tiles - 1:
                links.append((at + i, at + (i + 1 if i % 2 else i - 1)))
            else:
                links.append((at + i, other + i))
    axes = ("rad", "ang")
    return lax.ppermute(mate, axes, pairs), lax.ppermute(next_, axes, links)


def some_rows(z, mate, next_, outer):
    pairs, links = [], []
    for panel in range(z.panels):
        for rad in range(z.rads):
            at = (panel * z.rads + rad) * z.tiles
            for i in range(z.tiles):
                pairs.append((at + i, at + (i ^ 1)))
                if (rad == z.rads - 1) != outer:
                    links.append((at + i, at + (i ^ 1)))
                elif 0 < i < z.tiles - 1:
                    links.append((at + i, at + (i + 1 if i % 2 else i - 1)))
                else:
                    links.append((at + i, ((panel ^ 1) * z.rads + rad) * z.tiles + i))
    axes = ("panel", "rad", "ang")
    return lax.ppermute(mate, axes, pairs), lax.ppermute(next_, axes, links)


def call(kernel, shapes, scratch, args, spaces=pltpu.VMEM, room=48, aliases=None, cost=0):
    return pl.pallas_call(
        kernel,
        out_shape=[jax.ShapeDtypeStruct(shape, F32) for shape in shapes],
        in_specs=[pl.BlockSpec(memory_space=spaces)] * len(args),
        out_specs=[pl.BlockSpec(memory_space=pltpu.VMEM)] * len(shapes),
        scratch_shapes=scratch,
        input_output_aliases=aliases or {},
        cost_estimate=pl.CostEstimate(flops=0, bytes_accessed=cost, transcendentals=0) if cost else None,
        compiler_params=pltpu.CompilerParams(vmem_limit_bytes=room << 20),
    )(*args)


def body(adj, cond, diffus, couple, ghost_row, ghost_col, ghost_wt, obs_dest, obs_cell, obs_wt, misfit):
    z = Sizes(adj, obs_cell, ghost_row)
    state = (z.fields, z.rows, z.cols)
    line, lines = (SUBL, z.cols), (SUBL * (2 if z.pair else 1), z.cols)
    if z.pair:
        swap = [(0, 1), (1, 0)]
        beside = [lax.ppermute(adj, "rad", swap), lax.ppermute(cond, "rad", swap)]
    else:
        coeff = diffus[:, None, None] * cond[0, 0][None]
        beside = [both_sides(coeff * adj[0, :, 0], "rad")]
    far = beside[1:]

    given = [adj, cond, diffus, obs_dest.reshape(1, z.count), obs_cell, obs_wt, misfit]
    held = [pltpu.SMEM(x.shape, x.dtype) if x is diffus else pltpu.VMEM(x.shape, x.dtype) for x in given]
    pay, *rows = call(
        functools.partial(pack_kernel, z),
        [(z.devices, z.block, LANES), line, line],
        held + [pltpu.SemaphoreType.DMA((len(given),))],
        given,
        spaces=pltpu.HBM,
        room=64,
    )
    recv = lax.all_to_all(pay, ("panel", "rad", "ang"), split_axis=0, concat_axis=0, tiled=True)
    recv = recv.reshape(z.devices * z.block, LANES)
    rows = list(beside_rows(z, *rows))

    steps = diffus.reshape(1, z.fields)
    if z.pair:
        beside[:1] = call(functools.partial(far_kernel, z), [state], [], [beside[0]], cost=16 << 20)
    args = [adj, cond] + beside + [steps, couple]
    early, mate, next_, *first = call(
        functools.partial(early_kernel, z),
        [state, lines, lines] + ([] if z.pair else [state]),
        [pltpu.VMEM(state, F32)] * (2 if z.pair else 0),
        args,
    )
    links = call(
        functools.partial(link_kernel, z),
        [lines, lines],
        [],
        [cond, steps] + rows + [mate, next_],
        aliases={4: 0, 5: 1},
    )
    beyond = list(some_rows(z, *links, outer=False))
    points = z.rads * z.tiles * z.npr * LANES
    ends = 2 * z.cols // LANES
    ends = call(
        functools.partial(ends_kernel, z),
        [(z.fields * (2 if z.pair else 1) + spare, z.cols) for spare in range(2)],
        [pltpu.VMEM((2 * ends, points), BF16), pltpu.VMEM((LANES, points), BF16)],
        [recv, cond, steps, *links],
    )
    beyond += some_rows(z, *ends, outer=True)
    args = [early, recv, cond] + far + rows + [steps, couple]
    late, *added = call(
        functools.partial(ghost_kernel, z),
        [state] if z.pair else [state, state],
        ([pltpu.VMEM(state, F32)] if z.pair else [])
        + [pltpu.VMEM((2 * TIMES * z.hi, points), BF16), pltpu.VMEM((LOW, points), BF16)],
        args + [ghost_row, ghost_col, ghost_wt],
    )
    if not z.pair:
        far = [both_sides(coeff * (first[0] + added[0]), "rad")]
    args = [late] + far + beyond + [steps]
    (out,) = call(functools.partial(last_kernel, z), [adj.shape], [], args)
    return out


def solution(mesh):
    placed = (
        P("panel", None, "rad", "ang", None),
        P("panel", "rad", "ang", None),
        P(),
        P(),
        P(),
        P(),
        P(),
        P("panel", "rad", "ang", None),
        P("panel", "rad", None, "ang"),
        P("panel", "rad", None, "ang"),
        P("panel", "rad", None, "ang"),
    )
    return jax.shard_map(
        body,
        mesh=mesh,
        in_specs=placed,
        out_specs=P("panel", None, "rad", "ang", None),
        check_vma=False,
    )
```

```python
import functools

import jax
import jax.numpy as jnp
from jax import lax
from jax.experimental import pallas as pl
from jax.experimental.pallas import tpu as pltpu
from jax.sharding import PartitionSpec as P

LANES = 128
SUBL = 8
POINTS = 4
TIMES = 2
LOW = 256
F32 = jnp.float32
BF16 = jnp.bfloat16
NT_DIMS = (((1,), (1,)), ((), ()))


def parts_of(x, count):
    parts = []
    for _ in range(count):
        part = x.astype(BF16)
        parts.append(part)
        x = x - part.astype(F32)
    return parts


def joint_dot(x, onehot, count, dims):
    rows = x.shape[0]
    parts = [part.astype(F32) for part in parts_of(x, count)]
    spare = -(rows * count) % 16
    if spare:
        parts.append(jnp.zeros((spare, x.shape[1]), F32))
    joined = jnp.concatenate(parts, axis=0).astype(BF16)
    out = lax.dot_general(joined, onehot, dims, preferred_element_type=F32)
    return sum(out[k * rows : (k + 1) * rows] for k in range(1, count)) + out[:rows]


def iota(shape, dim):
    return lax.broadcasted_iota(jnp.int32, shape, dim)


def tall(row, height):
    tile = jnp.broadcast_to(row, (16, row.shape[1])).astype(BF16)
    return jnp.concatenate([tile] * (height // 16), axis=0)


def matches(row, height):
    return iota((height, row.shape[1]), 0).astype(F32).astype(BF16) == tall(row.astype(F32), height)


def onehot(index, height):
    within = matches(jnp.maximum(index, 0) % LANES, LANES)
    nothing = jnp.zeros(within.shape, BF16)
    blocks = [jnp.where(within, tall((index // LANES == k).astype(F32), LANES), nothing) for k in range(height // LANES)]
    return jnp.concatenate(blocks, axis=0)


class Sizes:
    def __init__(self, adj, obs_cell, ghost_row):
        self.fields, self.rows, self.cols = adj.shape[1], adj.shape[3], adj.shape[4]
        self.panels = lax.axis_size("panel")
        self.rads = lax.axis_size("rad")
        self.tiles = lax.axis_size("ang")
        self.devices = self.panels * self.rads * self.tiles
        self.total_rows = self.tiles * self.rows
        self.edge = 2 * self.total_rows
        self.count = obs_cell.shape[-1]
        self.slots = 2 * self.count // self.tiles
        self.spr = min(POINTS, LANES // self.slots)
        self.npr = POINTS // self.spr
        self.feat_rows = 2 * self.npr + 1
        self.edge_rows = self.edge // LANES
        self.strip = self.feat_rows + self.edge_rows
        self.block = -(-(self.strip + 2) // SUBL) * SUBL
        self.stencil = ghost_row.shape[1]
        self.hi = self.rows * self.cols // LOW
        self.pair = self.rads == 2


def rolled(x, shift, axis):
    size = x.shape[axis]
    shift = shift % size
    return x if shift == 0 else pltpu.roll(x, shift, axis)


def pack_kernel(z, *refs):
    count = 7
    given, (pay, mate, next_), held, sems = refs[:count], refs[count : count + 3], refs[count + 3 : -1], refs[-1]
    order = (3, 4, 5, 6, 2, 1, 0)
    copies = [pltpu.make_async_copy(given[n], held[n], sems.at[n]) for n in range(count)]
    for n in order:
        copies[n].start()
    adj, cond, diffus, dest, cell, wt, misfit = held
    for n in order[:4]:
        copies[n].wait()

    owner = dest[...]
    height = max(16, z.tiles)
    mine = (iota((height, z.count), 0) == owner).astype(F32)
    earlier = (iota((z.count, z.count), 0) < iota((z.count, z.count), 1)).astype(F32)
    ranks = jnp.dot(mine.astype(BF16), earlier.astype(BF16), preferred_element_type=F32)

    where = cell[0, 0]
    weight = wt[0, 0]
    mis = misfit[0, 0]
    row = ((where.astype(F32) + 0.5) * (1.0 / z.cols)).astype(jnp.int32)
    col = where - row * z.cols
    full_row = owner * z.rows + row
    edge_at = jnp.where(col == 0, full_row, jnp.where(col == z.cols - 1, z.total_rows + full_row, -1))
    hits = onehot(jnp.concatenate([edge_at[s : s + 1] for s in range(POINTS)], axis=1), z.edge)
    value = jnp.concatenate([mis[1:2] * weight[s : s + 1] for s in range(POINTS)], axis=1)
    edge_force = joint_dot(value, hits, 3, NT_DIMS)

    rank = jnp.sum(ranks * mine, axis=0, keepdims=True)
    place = owner * LANES + rank.astype(jnp.int32)
    spread = onehot(place, z.tiles * LANES)
    code = ((col // LOW) * z.rows + row) * LOW + col % LOW
    code = code.astype(F32)
    feats = []
    for g in range(z.spr):
        picked = [weight[h * z.spr + g : h * z.spr + g + 1] for h in range(z.npr)]
        picked += [code[h * z.spr + g : h * z.spr + g + 1] for h in range(z.npr)]
        picked.append(mis[g : g + 1] if g < TIMES else jnp.zeros((1, z.count), F32))
        feats += picked
    boxed = joint_dot(jnp.concatenate(feats, axis=0), spread, 3, NT_DIMS)
    slots = boxed[: z.feat_rows]
    for g in range(1, z.spr):
        slots = slots + rolled(boxed[g * z.feat_rows : (g + 1) * z.feat_rows], g * z.slots, 1)

    for n in order[4:]:
        copies[n].wait()

    lane = iota((z.rows, LANES), 1)
    sub = iota((z.rows, LANES), 0)
    strips = []
    for side in range(2):
        acc = jnp.zeros((z.rows, LANES), F32)
        for f in range(z.fields + 1):
            for inner in range(2):
                at = inner if side == 0 else z.cols - 1 - inner
                line = adj[0, f, 0, :, at : at + 1] if f < z.fields else cond[0, 0, :, at : at + 1]
                acc = jnp.where(lane == (f * 2 + inner) * z.rows + sub, line, acc)
        strips.append(jnp.sum(acc, axis=0, keepdims=True))

    common = [edge_force[:, k * LANES : (k + 1) * LANES] for k in range(z.edge_rows)] + strips
    spare = z.block - z.strip - 2
    if spare:
        common.append(jnp.zeros((spare, LANES), F32))
    common = jnp.concatenate(common, axis=0)
    for t in range(z.tiles):
        part = jnp.concatenate([slots[:, t * LANES : (t + 1) * LANES], common], axis=0)
        for group in range(z.panels * z.rads):
            pay[group * z.tiles + t] = part

    for f in range(z.fields):
        mate[f : f + 1, :], next_[f : f + 1, :] = facing(adj[0, f, 0] * (cond[0, 0] * diffus[f]))
    mate[z.fields :, :], next_[z.fields :, :] = facing(cond[0, 0])


def even_tile():
    return lax.axis_index("ang") % 2 == 0


def facing(s):
    top, bottom = s[:1], s[s.shape[0] - 1 :]
    even = even_tile()
    return jnp.where(even, bottom, top), jnp.where(even, top, bottom)


def around(z, mate, next_):
    even = even_tile()
    tile = lax.axis_index("ang")
    next_ = jnp.where((tile == 0) | (tile == z.tiles - 1), 0.0, next_)
    return jnp.where(even, next_, mate), jnp.where(even, mate, next_)


def wide(value, rows, cols):
    return jnp.concatenate([jnp.broadcast_to(value, (rows, LANES))] * (cols // LANES), axis=1)


def weights_of(z, steps, couple, rows, cols):
    dif = [wide(steps[:, f : f + 1], rows, cols) for f in range(z.fields)]
    mix = [[wide(couple[e : e + 1, c : c + 1], rows, cols) for c in range(z.fields)] for e in range(z.fields)]
    return dif, mix


def unpack_strips(z, recv, sets):
    height = 2 * z.tiles
    stacked = []
    for panel, rad in sets:
        base = (panel * z.rads + rad) * z.tiles * z.block + z.strip
        for side in range(2):
            stacked.append(recv[pl.ds(base + side, z.tiles, stride=z.block), :])
    stacked = jnp.concatenate(stacked, axis=0)
    width = 2 * SUBL * z.edge
    lane = iota((LANES, width), 1)
    slot = lane // z.edge
    inner, plane = slot // SUBL, slot % SUBL
    picks = (iota((LANES, width), 0) == (plane * 2 + inner) * z.rows + lane % z.rows).astype(F32)
    moved = joint_dot(stacked, picks.astype(BF16), 3, (((1,), (0,)), ((), ())))
    lane = iota((height, z.edge), 1)
    keep = lane // z.rows == iota((height, z.edge), 0)
    out = []
    for number in range(len(sets)):
        both = []
        for inner in range(2):
            rows = []
            for f in range(z.fields + 1):
                at = (inner * SUBL + f) * z.edge
                tile = moved[number * height : (number + 1) * height, at : at + z.edge]
                rows.append(jnp.sum(jnp.where(keep, tile, 0.0), axis=0, keepdims=True))
            both.append(jnp.concatenate(rows, axis=0))
        out.append(both)
    return out


def edge_scaled(z, values, dif):
    return values * values[z.fields : z.fields + 1] * dif


def coupled(z, mix, state, c):
    total = None
    for e in range(z.fields):
        term = state(e) * mix[e][c]
        total = term if total is None else total + term
    return total


def line_of(ref, q):
    return jnp.concatenate([ref[side, q : q + 1, :] for side in range(2)], axis=1)


def observed(z, recv, panel):
    sources = z.rads * z.tiles
    base = panel * sources * z.block
    feat = [recv[pl.ds(base + k, sources, stride=z.block), :] for k in range(z.feat_rows)]
    lane = iota((sources, LANES), 1)
    misfits = []
    for t in range(TIMES):
        mis = jnp.where(lane // z.slots == t, feat[2 * z.npr], 0.0)
        full = None
        for g in range(z.spr):
            term = rolled(mis, (g - t) * z.slots, 1)
            full = term if full is None else full + term
        misfits.append(full)
    return feat[: z.npr], [code.astype(jnp.int32) for code in feat[z.npr : 2 * z.npr]], misfits


def dealt(z, values, highs, lows, height, spread_a, spread_b):
    width = spread_b.shape[0]
    sources = highs[0].shape[0]
    zero, one = jnp.zeros((height, LANES), BF16), jnp.ones((width, LANES), BF16)
    for h in range(z.npr):
        parts = []
        for value in values[h]:
            parts += [part.astype(F32) for part in parts_of(value, 2)]
        for n in range(sources):
            at = (n * z.npr + h) * LANES
            hit = matches(highs[h][n : n + 1], height)
            for k, part in enumerate(parts):
                spread_a[k * height : (k + 1) * height, at : at + LANES] = jnp.where(hit, tall(part[n : n + 1], height), zero)
            hit = matches(lows[h][n : n + 1], width)
            spread_b[:, at : at + LANES] = jnp.where(hit, one, jnp.zeros_like(one))
    grid = lax.dot_general(spread_a[...], spread_b[...], NT_DIMS, preferred_element_type=F32)
    return [
        grid[2 * k * height : (2 * k + 1) * height] + grid[(2 * k + 1) * height : (2 * k + 2) * height]
        for k in range(len(values[0]))
    ]


def deposit(z, recv, panel, times, spread_a, spread_b):
    weights, codes, misfits = observed(z, recv, panel)
    values = [[misfits[t] * weight for t in times] for weight in weights]
    highs = [code // LOW for code in codes]
    lows = [code % LOW for code in codes]
    out = []
    for both in dealt(z, values, highs, lows, z.hi, spread_a, spread_b):
        out.append(jnp.concatenate([both[k * z.rows : (k + 1) * z.rows] for k in range(z.cols // LOW)], axis=1))
    return out


def deposit_ends(z, recv, panel, spread_a, spread_b):
    weights, codes, misfits = observed(z, recv, panel)
    values = [[misfits[1] * weight] for weight in weights]
    chunks = -(-z.cols // LANES // 16) * 16
    highs, lows = [], []
    for code in codes:
        row = (code // LOW) % z.rows
        chunk = (code // LOW) // z.rows * (LOW // LANES) + (code % LOW) // LANES
        end = jnp.where(row == z.rows - 1, chunk + chunks, -1)
        highs.append(jnp.where(row == 0, chunk, end))
        lows.append(code % LANES)
    (both,) = dealt(z, values, highs, lows, 2 * chunks, spread_a, spread_b)
    ends = [[both[e * chunks + k : e * chunks + k + 1] for k in range(z.cols // LANES)] for e in range(2)]
    return [jnp.concatenate(end, axis=1) for end in ends]


def sideways(s):
    cols = s.shape[1]
    lane = iota(s.shape, 1)
    west = jnp.where(lane == 0, 0.0, pltpu.roll(s, 1, 1))
    east = jnp.where(lane == cols - 1, 0.0, pltpu.roll(s, cols - 1, 1))
    return west + east


def upright(s, above, below):
    rows = s.shape[0]
    sub = iota(s.shape, 0)
    north = jnp.where(sub == 0, above, pltpu.roll(s, 1, 0))
    south = jnp.where(sub == rows - 1, below, pltpu.roll(s, rows - 1, 0))
    return north + south


def far_kernel(z, adj2, out):
    out[...] = adj2[0, :, 0]


def early_kernel(z, adj, cond, *refs):
    if z.pair:
        adj2, cond2, steps, couple, out, mate, next_, own, far = refs
    else:
        beside, steps, couple, out, mate, next_, own = refs
    dif, mix = weights_of(z, steps, couple, z.rows, z.cols)
    own_c = cond[0, 0]
    far_c = cond2[0, 0] if z.pair else None
    for f in range(z.fields):
        s = adj[0, f, 0] * (own_c * dif[f])
        new = adj[0, f, 0] - 6.0 * s + sideways(s) + upright(s, 0.0, 0.0)
        new = new + coupled(z, mix, lambda e: adj[0, e, 0], f)
        if z.pair:
            other = adj2[f] * (far_c * dif[f])
            new = new + other
            part = adj2[f] - 6.0 * other + sideways(other) + upright(other, 0.0, 0.0) + s
            far[f] = part + coupled(z, mix, lambda e: adj2[e], f)
            at = SUBL + f
            mate[at : at + 1, :], next_[at : at + 1, :] = facing(other)
        else:
            new = new + beside[f]
        own[f] = new
        mate[f : f + 1, :], next_[f : f + 1, :] = facing(new * (own_c * dif[f]))
    for half in range(2 if z.pair else 1):
        for ref in (mate, next_):
            ref[half * SUBL + z.fields : (half + 1) * SUBL, :] = jnp.zeros((SUBL - z.fields, z.cols), F32)
    for f in range(z.fields):
        s = own[f] * (own_c * dif[f])
        new = own[f] - 6.0 * s + sideways(s) + upright(s, 0.0, 0.0)
        new = new + coupled(z, mix, lambda e: own[e], f)
        if z.pair:
            new = new + far[f] * (far_c * dif[f])
        out[f] = new


def link_kernel(z, cond, steps, mate_row, next_row, mate_in, next_in, mate, next_):
    tile = lax.axis_index("ang")
    inner = jnp.where((tile == 0) | (tile == z.tiles - 1), 0.0, 1.0)
    cond_mate, cond_next = facing(cond[0, 0])
    for f in range(z.fields):
        dif = wide(steps[:, f : f + 1], 1, z.cols)
        mate[f : f + 1, :] = mate_in[f : f + 1, :] + mate_row[f : f + 1, :] * (cond_mate * dif)
        next_[f : f + 1, :] = next_in[f : f + 1, :] + next_row[f : f + 1, :] * (cond_next * dif * inner)


def is_outer(z):
    return lax.axis_index("rad") == z.rads - 1


def ends_kernel(z, recv, cond, steps, mate_in, next_in, mate, next_, spread_a, spread_b):
    panel = lax.axis_index("panel")
    next_[mate.shape[0] :, :] = jnp.zeros((next_.shape[0] - mate.shape[0], z.cols), F32)
    for f in range(mate.shape[0]):
        at = f % z.fields + f // z.fields * SUBL
        mate[f : f + 1, :] = mate_in[at : at + 1, :]
        next_[f : f + 1, :] = next_in[at : at + 1, :]

    @pl.when(is_outer(z))
    def _():
        top, bottom = deposit_ends(z, recv, panel, spread_a, spread_b)
        weight = cond[0, 0] * wide(steps[:, 3:4], z.rows, z.cols)
        top = top * weight[:1]
        bottom = bottom * weight[z.rows - 1 :]
        even = even_tile()
        mate[3:4, :] = mate_in[3:4, :] + jnp.where(even, bottom, top)
        next_[3:4, :] = next_in[3:4, :] + jnp.where(even, top, bottom)


def ghost_kernel(z, early, recv, cond, *refs):
    if z.pair:
        cond2, mate_in, next_in, steps, couple, grow, gcol, gwt, out, added, spread_a, spread_b = refs
    else:
        mate_in, next_in, steps, couple, grow, gcol, gwt, out, added, spread_a, spread_b = refs
    panel, rad, tile = lax.axis_index("panel"), lax.axis_index("rad"), lax.axis_index("ang")
    other = 1 - panel
    outer = jnp.where(rad == z.rads - 1, 1.0, 0.0)
    above, below = around(z, mate_in[...], next_in[...])

    sets = [(other, rad), (panel, rad)]
    if z.pair:
        sets.append((other, 1 - rad))
        near = [1.0]
    else:
        sets += [(other, jnp.maximum(rad - 1, 0)), (other, jnp.minimum(rad + 1, z.rads - 1))]
        near = [jnp.where(rad > 0, 1.0, 0.0), jnp.where(rad < z.rads - 1, 1.0, 0.0)]
    strips = unpack_strips(z, recv, sets)
    dif, mix = weights_of(z, steps, couple, z.rows, z.cols)
    plane = iota((SUBL, z.edge), 0)
    by_plane = jnp.zeros((SUBL, z.edge), F32)
    for f in range(z.fields):
        by_plane = jnp.where(plane == f, wide(steps[:, f : f + 1], SUBL, z.edge), by_plane)
    rim, inside = strips[0]
    rim_s = edge_scaled(z, rim, by_plane)
    home_s = edge_scaled(z, strips[1][0], by_plane)
    layers_s = [edge_scaled(z, strips[2 + k][0], by_plane) for k in range(len(near))]
    lap = edge_scaled(z, inside, by_plane) - 6.0 * rim_s
    for k, one in enumerate(near):
        lap = lap + layers_s[k] * one
    spot = iota((SUBL, z.edge), 1) % z.total_rows
    lap = lap + jnp.where(spot == 0, 0.0, pltpu.roll(rim_s, 1, 1))
    lap = lap + jnp.where(spot == z.total_rows - 1, 0.0, pltpu.roll(rim_s, z.edge - 1, 1))
    thin = [[mix[e][f][:1, : z.edge] for f in range(z.fields)] for e in range(z.fields)]
    rows = [coupled(z, thin, lambda e: rim[e : e + 1], c) for c in range(z.fields)]
    mixed = jnp.concatenate(rows + [jnp.zeros((SUBL - z.fields, z.edge), F32)], axis=0)

    g_row = [line_of(grow, q) for q in range(z.stencil)]
    g_col = [line_of(gcol, q) for q in range(z.stencil)]
    g_wt = [line_of(gwt, q) for q in range(z.stencil)]
    targets = []
    for q in range(z.stencil):
        last_one = jnp.where(g_col[q] == z.cols - 1, z.total_rows + g_row[q], -1)
        targets.append(jnp.where(g_col[q] == 0, g_row[q], last_one))
    hits = onehot(jnp.concatenate(targets, axis=1), z.edge)
    values = jnp.concatenate([home_s * g_wt[q] for q in range(z.stencil)], axis=1)
    rim_ghost = joint_dot(values, hits, 3, NT_DIMS)
    sources = z.rads * z.tiles
    pulse = []
    for k in range(z.edge_rows):
        at = other * sources * z.block + z.feat_rows + k
        pulse.append(jnp.sum(recv[pl.ds(at, sources, stride=z.block), :], axis=0, keepdims=True))
    pulse = jnp.concatenate(pulse, axis=1) * outer
    rim_first = rim + lap + mixed + rim_ghost
    rim_first = rim_first + jnp.where(iota((SUBL, z.edge), 0) == 3, pulse, 0.0)
    rim_second = rim_first * rim[z.fields : z.fields + 1] * by_plane

    row0 = tile * z.rows
    aimed = [jnp.where(iota((z.rows, z.edge), 0) == g_row[q] - row0, g_wt[q], 0.0) for q in range(z.stencil)]
    loads = [rim_s, rim_second] + ([layers_s[0]] if z.pair else [])
    stacked = []
    for load in loads:
        for f in range(z.fields):
            stacked.append(jnp.concatenate([load[f : f + 1] * aimed[q] for q in range(z.stencil)], axis=1))
    for row in (row0 - 1, row0 + z.rows):
        stacked.append(
            jnp.concatenate([rim_s * jnp.where(g_row[q] == row, g_wt[q], 0.0) for q in range(z.stencil)], axis=1)
        )
    stacked = jnp.concatenate(stacked, axis=0)
    spots = jnp.concatenate(g_col, axis=1)
    columns = onehot(spots, z.cols)
    ghost = joint_dot(stacked, columns, 2, NT_DIMS)

    def ghost_of(step, f):
        at = (step * z.fields + f) * z.rows
        return ghost[at : at + z.rows]

    force = deposit(z, recv, panel, (0, 1), spread_a, spread_b)
    at = len(loads) * z.fields * z.rows
    ghost_above, ghost_below = ghost[at : at + SUBL], ghost[at + SUBL : at + 2 * SUBL]
    own_c = cond[0, 0]
    for f in range(z.fields):
        new = ghost_of(0, f) + brim(above[f : f + 1], below[f : f + 1], z.rows)
        added[f] = new + force[1] * outer if f == 3 else new
    for f in range(z.fields):
        s = added[f] * (own_c * dif[f])
        high = ghost_above[f : f + 1] * (above[z.fields :] * dif[f][:1])
        low = ghost_below[f : f + 1] * (below[z.fields :] * dif[f][:1])
        new = early[f] + added[f] - 6.0 * s + sideways(s) + upright(s, high, low)
        new = new + coupled(z, mix, lambda e: added[e], f) + ghost_of(1, f)
        if z.pair:
            part = ghost_of(2, f)
            if f == 3:
                part = part + force[1] * (1.0 - outer)
            new = new + part * (cond2[0, 0] * dif[f])
        if f == 3:
            new = new + force[0] * outer
        out[f] = new


def brim(high, low, rows):
    sub = iota((rows, high.shape[1]), 0)
    return jnp.where(sub == 0, high, 0.0) + jnp.where(sub == rows - 1, low, 0.0)


def last_kernel(z, late, *refs):
    if z.pair:
        cond2, mate_inner, next_inner, mate_outer, next_outer, steps, out = refs
    else:
        beside, mate_inner, next_inner, mate_outer, next_outer, steps, out = refs
    outer = is_outer(z)

    def beyond(half, f):
        inner_at, outer_at = half * SUBL + f, half * z.fields + f
        mate_in = jnp.where(outer, mate_outer[outer_at : outer_at + 1, :], mate_inner[inner_at : inner_at + 1, :])
        next_in = jnp.where(outer, next_outer[outer_at : outer_at + 1, :], next_inner[inner_at : inner_at + 1, :])
        return around(z, mate_in, next_in)

    for f in range(z.fields):
        high, low = beyond(0, f)
        if z.pair:
            far_high, far_low = beyond(1, f)
            far_c = cond2[0, 0] * wide(steps[:, f : f + 1], z.rows, z.cols)
            high = high + far_high * far_c[:1]
            low = low + far_low * far_c[z.rows - 1 :]
        new = late[f] + brim(high, low, z.rows)
        out[0, f, 0] = new if z.pair else new + beside[f]


def shifted(x, axis, step):
    count = lax.axis_size(axis)
    pairs = [(i, i + step) for i in range(count) if 0 <= i + step < count]
    return lax.ppermute(x, axis, pairs)


def both_sides(x, axis):
    return shifted(x, axis, 1) + shifted(x, axis, -1)


def beside_rows(z, mate, next_):
    pairs, links = [], []
    for rad in range(z.rads):
        at = rad * z.tiles
        other = (rad ^ 1) * z.tiles
        for i in range(z.tiles):
            pairs.append((at + i, at + (i ^ 1)))
            if 0 < i < z.tiles - 1:
                links.append((at + i, at + (i + 1 if i % 2 else i - 1)))
            else:
                links.append((at + i, other + i))
    axes = ("rad", "ang")
    return lax.ppermute(mate, axes, pairs), lax.ppermute(next_, axes, links)


def some_rows(z, mate, next_, outer):
    def at(panel, rad, tile):
        return (panel * z.rads + rad) * z.tiles + tile

    last, below = z.rads - 1, z.rads - 2
    pairs, links = [], {}
    for panel in range(z.panels):
        for rad in range(z.rads):
            for i in range(z.tiles):
                pairs.append((at(panel, rad, i), at(panel, rad, i ^ 1)))
                if (rad == last) != outer:
                    links[at(panel, rad, i)] = at(panel, rad, i ^ 1)
                elif 0 < i < z.tiles - 1:
                    links[at(panel, rad, i)] = at(panel, rad, i + 1 if i % 2 else i - 1)
                else:
                    links[at(panel, rad, i)] = at(panel ^ 1, rad, i)
    for end in (0, z.tiles - 1):
        for panel in range(0 if outer else z.panels):
            ring = [at(panel, below, end), at(panel, last, end ^ 1), at(panel, last, end)]
            for n, source in enumerate(ring):
                links[source] = ring[(n + 1) % len(ring)]
    axes = ("panel", "rad", "ang")
    return lax.ppermute(mate, axes, pairs), lax.ppermute(next_, axes, list(links.items()))


def call(kernel, shapes, scratch, args, spaces=pltpu.VMEM, room=48, aliases=None, cost=0):
    return pl.pallas_call(
        kernel,
        out_shape=[jax.ShapeDtypeStruct(shape, F32) for shape in shapes],
        in_specs=[pl.BlockSpec(memory_space=spaces)] * len(args),
        out_specs=[pl.BlockSpec(memory_space=pltpu.VMEM)] * len(shapes),
        scratch_shapes=scratch,
        input_output_aliases=aliases or {},
        cost_estimate=pl.CostEstimate(flops=0, bytes_accessed=cost, transcendentals=0) if cost else None,
        compiler_params=pltpu.CompilerParams(vmem_limit_bytes=room << 20),
    )(*args)


def body(adj, cond, diffus, couple, ghost_row, ghost_col, ghost_wt, obs_dest, obs_cell, obs_wt, misfit):
    z = Sizes(adj, obs_cell, ghost_row)
    state = (z.fields, z.rows, z.cols)
    line, lines = (SUBL, z.cols), (SUBL * (2 if z.pair else 1), z.cols)
    if z.pair:
        swap = [(0, 1), (1, 0)]
        beside = [lax.ppermute(adj, "rad", swap), lax.ppermute(cond, "rad", swap)]
    else:
        coeff = diffus[:, None, None] * cond[0, 0][None]
        beside = [both_sides(coeff * adj[0, :, 0], "rad")]
    far = beside[1:]

    given = [adj, cond, diffus, obs_dest.reshape(1, z.count), obs_cell, obs_wt, misfit]
    held = [pltpu.SMEM(x.shape, x.dtype) if x is diffus else pltpu.VMEM(x.shape, x.dtype) for x in given]
    pay, *rows = call(
        functools.partial(pack_kernel, z),
        [(z.devices, z.block, LANES), line, line],
        held + [pltpu.SemaphoreType.DMA((len(given),))],
        given,
        spaces=pltpu.HBM,
        room=64,
    )
    recv = lax.all_to_all(pay, ("panel", "rad", "ang"), split_axis=0, concat_axis=0, tiled=True)
    recv = recv.reshape(z.devices * z.block, LANES)
    rows = list(beside_rows(z, *rows))

    steps = diffus.reshape(1, z.fields)
    if z.pair:
        beside[:1] = call(functools.partial(far_kernel, z), [state], [], [beside[0]], cost=16 << 20)
    args = [adj, cond] + beside + [steps, couple]
    early, mate, next_, *first = call(
        functools.partial(early_kernel, z),
        [state, lines, lines] + ([] if z.pair else [state]),
        [pltpu.VMEM(state, F32)] * (2 if z.pair else 0),
        args,
    )
    links = call(
        functools.partial(link_kernel, z),
        [lines, lines],
        [],
        [cond, steps] + rows + [mate, next_],
        aliases={4: 0, 5: 1},
    )
    beyond = list(some_rows(z, *links, outer=False))
    points = z.rads * z.tiles * z.npr * LANES
    ends = 2 * (-(-z.cols // LANES // 16) * 16)
    ends = call(
        functools.partial(ends_kernel, z),
        [(z.fields * (2 if z.pair else 1) + spare, z.cols) for spare in range(2)],
        [pltpu.VMEM((2 * ends, points), BF16), pltpu.VMEM((LANES, points), BF16)],
        [recv, cond, steps, *links],
    )
    beyond += some_rows(z, *ends, outer=True)
    args = [early, recv, cond] + far + rows + [steps, couple]
    late, *added = call(
        functools.partial(ghost_kernel, z),
        [state] if z.pair else [state, state],
        ([pltpu.VMEM(state, F32)] if z.pair else [])
        + [pltpu.VMEM((2 * TIMES * z.hi, points), BF16), pltpu.VMEM((LOW, points), BF16)],
        args + [ghost_row, ghost_col, ghost_wt],
    )
    if not z.pair:
        far = [both_sides(coeff * (first[0] + added[0]), "rad")]
    args = [late] + far + beyond + [steps]
    (out,) = call(functools.partial(last_kernel, z), [adj.shape], [], args)
    return out


def solution(mesh):
    placed = (
        P("panel", None, "rad", "ang", None),
        P("panel", "rad", "ang", None),
        P(),
        P(),
        P(),
        P(),
        P(),
        P("panel", "rad", "ang", None),
        P("panel", "rad", None, "ang"),
        P("panel", "rad", None, "ang"),
        P("panel", "rad", None, "ang"),
    )
    return jax.shard_map(
        body,
        mesh=mesh,
        in_specs=placed,
        out_specs=P("panel", None, "rad", "ang", None),
        check_vma=False,
    )
```

```python
import functools

import jax
import jax.numpy as jnp
from jax import lax
from jax.experimental import pallas as pl
from jax.experimental.pallas import tpu as pltpu
from jax.sharding import PartitionSpec as P

LANES = 128
SUBL = 8
POINTS = 4
TIMES = 2
LOW = 256
F32 = jnp.float32
BF16 = jnp.bfloat16
NT_DIMS = (((1,), (1,)), ((), ()))


def parts_of(x, count):
    parts = []
    for _ in range(count):
        part = x.astype(BF16)
        parts.append(part)
        x = x - part.astype(F32)
    return parts


def joint_dot(x, onehot, count, dims):
    rows = x.shape[0]
    parts = [part.astype(F32) for part in parts_of(x, count)]
    spare = -(rows * count) % 16
    if spare:
        parts.append(jnp.zeros((spare, x.shape[1]), F32))
    joined = jnp.concatenate(parts, axis=0).astype(BF16)
    out = lax.dot_general(joined, onehot, dims, preferred_element_type=F32)
    return sum(out[k * rows : (k + 1) * rows] for k in range(1, count)) + out[:rows]


def iota(shape, dim):
    return lax.broadcasted_iota(jnp.int32, shape, dim)


def tall(row, height):
    tile = jnp.broadcast_to(row, (16, row.shape[1])).astype(BF16)
    return jnp.concatenate([tile] * (height // 16), axis=0)


def matches(row, height):
    return iota((height, row.shape[1]), 0).astype(F32).astype(BF16) == tall(row.astype(F32), height)


def onehot(index, height):
    within = matches(jnp.maximum(index, 0) % LANES, LANES)
    nothing = jnp.zeros(within.shape, BF16)
    blocks = [jnp.where(within, tall((index // LANES == k).astype(F32), LANES), nothing) for k in range(height // LANES)]
    return jnp.concatenate(blocks, axis=0)


class Sizes:
    def __init__(self, adj, obs_cell, ghost_row):
        self.fields, self.rows, self.cols = adj.shape[1], adj.shape[3], adj.shape[4]
        self.panels = lax.axis_size("panel")
        self.rads = lax.axis_size("rad")
        self.tiles = lax.axis_size("ang")
        self.devices = self.panels * self.rads * self.tiles
        self.total_rows = self.tiles * self.rows
        self.edge = 2 * self.total_rows
        self.count = obs_cell.shape[-1]
        self.slots = 2 * self.count // self.tiles
        self.spr = min(POINTS, LANES // self.slots)
        self.npr = POINTS // self.spr
        self.feat_rows = 2 * self.npr + 1
        self.edge_rows = self.edge // LANES
        self.strip = self.feat_rows + self.edge_rows
        self.block = -(-(self.strip + 2) // SUBL) * SUBL
        self.stencil = ghost_row.shape[1]
        self.hi = self.rows * self.cols // LOW
        self.pair = self.rads == 2


def rolled(x, shift, axis):
    size = x.shape[axis]
    shift = shift % size
    return x if shift == 0 else pltpu.roll(x, shift, axis)


def pack_kernel(z, *refs):
    count = 7
    given, (pay, mate, next_), held, sems = refs[:count], refs[count : count + 3], refs[count + 3 : -1], refs[-1]
    order = (3, 4, 5, 6, 2, 1, 0)
    copies = [pltpu.make_async_copy(given[n], held[n], sems.at[n]) for n in range(count)]
    for n in order:
        copies[n].start()
    adj, cond, diffus, dest, cell, wt, misfit = held
    for n in order[:4]:
        copies[n].wait()

    owner = dest[...]
    height = max(16, z.tiles)
    mine = (iota((height, z.count), 0) == owner).astype(F32)
    earlier = (iota((z.count, z.count), 0) < iota((z.count, z.count), 1)).astype(F32)
    ranks = jnp.dot(mine.astype(BF16), earlier.astype(BF16), preferred_element_type=F32)

    where = cell[0, 0]
    weight = wt[0, 0]
    mis = misfit[0, 0]
    row = ((where.astype(F32) + 0.5) * (1.0 / z.cols)).astype(jnp.int32)
    col = where - row * z.cols
    full_row = owner * z.rows + row
    edge_at = jnp.where(col == 0, full_row, jnp.where(col == z.cols - 1, z.total_rows + full_row, -1))
    hits = onehot(jnp.concatenate([edge_at[s : s + 1] for s in range(POINTS)], axis=1), z.edge)
    value = jnp.concatenate([mis[1:2] * weight[s : s + 1] for s in range(POINTS)], axis=1)
    edge_force = joint_dot(value, hits, 3, NT_DIMS)

    rank = jnp.sum(ranks * mine, axis=0, keepdims=True)
    place = owner * LANES + rank.astype(jnp.int32)
    spread = onehot(place, z.tiles * LANES)
    code = ((col // LOW) * z.rows + row) * LOW + col % LOW
    code = code.astype(F32)
    feats = []
    for g in range(z.spr):
        picked = [weight[h * z.spr + g : h * z.spr + g + 1] for h in range(z.npr)]
        picked += [code[h * z.spr + g : h * z.spr + g + 1] for h in range(z.npr)]
        picked.append(mis[g : g + 1] if g < TIMES else jnp.zeros((1, z.count), F32))
        feats += picked
    boxed = joint_dot(jnp.concatenate(feats, axis=0), spread, 3, NT_DIMS)
    slots = boxed[: z.feat_rows]
    for g in range(1, z.spr):
        slots = slots + rolled(boxed[g * z.feat_rows : (g + 1) * z.feat_rows], g * z.slots, 1)

    for n in order[4:]:
        copies[n].wait()

    lane = iota((z.rows, LANES), 1)
    sub = iota((z.rows, LANES), 0)
    strips = []
    for side in range(2):
        acc = jnp.zeros((z.rows, LANES), F32)
        for f in range(z.fields + 1):
            for inner in range(2):
                at = inner if side == 0 else z.cols - 1 - inner
                line = adj[0, f, 0, :, at : at + 1] if f < z.fields else cond[0, 0, :, at : at + 1]
                acc = jnp.where(lane == (f * 2 + inner) * z.rows + sub, line, acc)
        strips.append(jnp.sum(acc, axis=0, keepdims=True))

    common = [edge_force[:, k * LANES : (k + 1) * LANES] for k in range(z.edge_rows)] + strips
    spare = z.block - z.strip - 2
    if spare:
        common.append(jnp.zeros((spare, LANES), F32))
    common = jnp.concatenate(common, axis=0)
    for t in range(z.tiles):
        part = jnp.concatenate([slots[:, t * LANES : (t + 1) * LANES], common], axis=0)
        for group in range(z.panels * z.rads):
            pay[group * z.tiles + t] = part

    for f in range(z.fields):
        mate[f : f + 1, :], next_[f : f + 1, :] = facing(adj[0, f, 0] * (cond[0, 0] * diffus[f]))
    mate[z.fields :, :], next_[z.fields :, :] = facing(cond[0, 0])


def even_tile():
    return lax.axis_index("ang") % 2 == 0


def facing(s):
    top, bottom = s[:1], s[s.shape[0] - 1 :]
    even = even_tile()
    return jnp.where(even, bottom, top), jnp.where(even, top, bottom)


def around(z, mate, next_):
    even = even_tile()
    tile = lax.axis_index("ang")
    next_ = jnp.where((tile == 0) | (tile == z.tiles - 1), 0.0, next_)
    return jnp.where(even, next_, mate), jnp.where(even, mate, next_)


def wide(value, rows, cols):
    return jnp.concatenate([jnp.broadcast_to(value, (rows, LANES))] * (cols // LANES), axis=1)


def weights_of(z, steps, couple, rows, cols):
    dif = [wide(steps[:, f : f + 1], rows, cols) for f in range(z.fields)]
    mix = [[wide(couple[e : e + 1, c : c + 1], rows, cols) for c in range(z.fields)] for e in range(z.fields)]
    return dif, mix


def unpack_strips(z, recv, sets):
    height = 2 * z.tiles
    stacked = []
    for panel, rad in sets:
        base = (panel * z.rads + rad) * z.tiles * z.block + z.strip
        for side in range(2):
            stacked.append(recv[pl.ds(base + side, z.tiles, stride=z.block), :])
    stacked = jnp.concatenate(stacked, axis=0)
    width = 2 * SUBL * z.edge
    lane = iota((LANES, width), 1)
    slot = lane // z.edge
    inner, plane = slot // SUBL, slot % SUBL
    picks = (iota((LANES, width), 0) == (plane * 2 + inner) * z.rows + lane % z.rows).astype(F32)
    moved = joint_dot(stacked, picks.astype(BF16), 3, (((1,), (0,)), ((), ())))
    lane = iota((height, z.edge), 1)
    keep = lane // z.rows == iota((height, z.edge), 0)
    out = []
    for number in range(len(sets)):
        both = []
        for inner in range(2):
            rows = []
            for f in range(z.fields + 1):
                at = (inner * SUBL + f) * z.edge
                tile = moved[number * height : (number + 1) * height, at : at + z.edge]
                rows.append(jnp.sum(jnp.where(keep, tile, 0.0), axis=0, keepdims=True))
            both.append(jnp.concatenate(rows, axis=0))
        out.append(both)
    return out


def edge_scaled(z, values, dif):
    return values * values[z.fields : z.fields + 1] * dif


def coupled(z, mix, state, c):
    total = None
    for e in range(z.fields):
        term = state(e) * mix[e][c]
        total = term if total is None else total + term
    return total


def line_of(ref, q):
    return jnp.concatenate([ref[side, q : q + 1, :] for side in range(2)], axis=1)


def observed(z, recv, panel):
    sources = z.rads * z.tiles
    base = panel * sources * z.block
    feat = [recv[pl.ds(base + k, sources, stride=z.block), :] for k in range(z.feat_rows)]
    lane = iota((sources, LANES), 1)
    misfits = []
    for t in range(TIMES):
        mis = jnp.where(lane // z.slots == t, feat[2 * z.npr], 0.0)
        full = None
        for g in range(z.spr):
            term = rolled(mis, (g - t) * z.slots, 1)
            full = term if full is None else full + term
        misfits.append(full)
    return feat[: z.npr], [code.astype(jnp.int32) for code in feat[z.npr : 2 * z.npr]], misfits


def dealt(z, values, highs, lows, height, spread_a, spread_b):
    width = spread_b.shape[0]
    sources = highs[0].shape[0]
    zero, one = jnp.zeros((height, LANES), BF16), jnp.ones((width, LANES), BF16)
    for h in range(z.npr):
        parts = []
        for value in values[h]:
            parts += [part.astype(F32) for part in parts_of(value, 2)]
        for n in range(sources):
            at = (n * z.npr + h) * LANES
            hit = matches(highs[h][n : n + 1], height)
            for k, part in enumerate(parts):
                spread_a[k * height : (k + 1) * height, at : at + LANES] = jnp.where(hit, tall(part[n : n + 1], height), zero)
            hit = matches(lows[h][n : n + 1], width)
            spread_b[:, at : at + LANES] = jnp.where(hit, one, jnp.zeros_like(one))
    grid = lax.dot_general(spread_a[...], spread_b[...], NT_DIMS, preferred_element_type=F32)
    return [
        grid[2 * k * height : (2 * k + 1) * height] + grid[(2 * k + 1) * height : (2 * k + 2) * height]
        for k in range(len(values[0]))
    ]


def deposit(z, recv, panel, times, spread_a, spread_b):
    weights, codes, misfits = observed(z, recv, panel)
    values = [[misfits[t] * weight for t in times] for weight in weights]
    highs = [code // LOW for code in codes]
    lows = [code % LOW for code in codes]
    out = []
    for both in dealt(z, values, highs, lows, z.hi, spread_a, spread_b):
        out.append(jnp.concatenate([both[k * z.rows : (k + 1) * z.rows] for k in range(z.cols // LOW)], axis=1))
    return out


def deposit_ends(z, recv, panel, spread_a, spread_b):
    weights, codes, misfits = observed(z, recv, panel)
    values = [[misfits[1] * weight] for weight in weights]
    chunks = -(-z.cols // LANES // 16) * 16
    highs, lows = [], []
    for code in codes:
        row = (code // LOW) % z.rows
        chunk = (code // LOW) // z.rows * (LOW // LANES) + (code % LOW) // LANES
        end = jnp.where(row == z.rows - 1, chunk + chunks, -1)
        highs.append(jnp.where(row == 0, chunk, end))
        lows.append(code % LANES)
    (both,) = dealt(z, values, highs, lows, 2 * chunks, spread_a, spread_b)
    ends = [[both[e * chunks + k : e * chunks + k + 1] for k in range(z.cols // LANES)] for e in range(2)]
    return [jnp.concatenate(end, axis=1) for end in ends]


def sideways(s):
    cols = s.shape[1]
    lane = iota(s.shape, 1)
    west = jnp.where(lane == 0, 0.0, pltpu.roll(s, 1, 1))
    east = jnp.where(lane == cols - 1, 0.0, pltpu.roll(s, cols - 1, 1))
    return west + east


def upright(s, above, below):
    rows = s.shape[0]
    sub = iota(s.shape, 0)
    north = jnp.where(sub == 0, above, pltpu.roll(s, 1, 0))
    south = jnp.where(sub == rows - 1, below, pltpu.roll(s, rows - 1, 0))
    return north + south


def far_kernel(z, adj2, out):
    out[...] = adj2[0, :, 0]


def lone_kernel(z, adj, cond, *refs):
    if z.pair:
        adj2, steps, couple, first, mixed = refs
    else:
        steps, couple, first = refs
    dif, mix = weights_of(z, steps, couple, z.rows, z.cols)
    for f in range(z.fields):
        s = adj[0, f, 0] * (cond[0, 0] * dif[f])
        new = adj[0, f, 0] - 6.0 * s + sideways(s) + upright(s, 0.0, 0.0)
        first[f] = new + coupled(z, mix, lambda e: adj[0, e, 0], f)
        if z.pair:
            mixed[f] = adj2[f] + s + coupled(z, mix, lambda e: adj2[e], f)


def early_kernel(z, cond, first, *refs):
    if z.pair:
        mixed, adj2, cond2, steps, couple, out, mate, next_, own, far = refs
    else:
        beside, steps, couple, out, mate, next_, own = refs
    dif, mix = weights_of(z, steps, couple, z.rows, z.cols)
    own_c = cond[0, 0]
    far_c = cond2[0, 0] if z.pair else None
    for f in range(z.fields):
        if z.pair:
            other = adj2[f] * (far_c * dif[f])
            new = first[f] + other
            far[f] = mixed[f] - 6.0 * other + sideways(other) + upright(other, 0.0, 0.0)
            at = SUBL + f
            mate[at : at + 1, :], next_[at : at + 1, :] = facing(other)
        else:
            new = first[f] + beside[f]
        own[f] = new
        mate[f : f + 1, :], next_[f : f + 1, :] = facing(new * (own_c * dif[f]))
    for half in range(2 if z.pair else 1):
        for ref in (mate, next_):
            ref[half * SUBL + z.fields : (half + 1) * SUBL, :] = jnp.zeros((SUBL - z.fields, z.cols), F32)
    for f in range(z.fields):
        s = own[f] * (own_c * dif[f])
        new = own[f] - 6.0 * s + sideways(s) + upright(s, 0.0, 0.0)
        new = new + coupled(z, mix, lambda e: own[e], f)
        if z.pair:
            new = new + far[f] * (far_c * dif[f])
        out[f] = new


def link_kernel(z, cond, steps, mate_row, next_row, mate_in, next_in, mate, next_):
    tile = lax.axis_index("ang")
    inner = jnp.where((tile == 0) | (tile == z.tiles - 1), 0.0, 1.0)
    cond_mate, cond_next = facing(cond[0, 0])
    for f in range(z.fields):
        dif = wide(steps[:, f : f + 1], 1, z.cols)
        mate[f : f + 1, :] = mate_in[f : f + 1, :] + mate_row[f : f + 1, :] * (cond_mate * dif)
        next_[f : f + 1, :] = next_in[f : f + 1, :] + next_row[f : f + 1, :] * (cond_next * dif * inner)
        if z.pair:
            mate[z.fields + f : z.fields + f + 1, :] = mate_in[SUBL + f : SUBL + f + 1, :]
            next_[z.fields + f : z.fields + f + 1, :] = next_in[SUBL + f : SUBL + f + 1, :]
    spare = next_.shape[0] - 1
    next_[spare:, :] = jnp.zeros((1, z.cols), F32)


def is_outer(z):
    return lax.axis_index("rad") == z.rads - 1


def ends_kernel(z, recv, cond, steps, mate, next_, spread_a, spread_b):
    panel = lax.axis_index("panel")
    mate[...] = jnp.zeros_like(mate)
    next_[...] = jnp.zeros_like(next_)

    @pl.when(is_outer(z))
    def _():
        top, bottom = deposit_ends(z, recv, panel, spread_a, spread_b)
        weight = cond[0, 0] * wide(steps[:, 3:4], z.rows, z.cols)
        top = top * weight[:1]
        bottom = bottom * weight[z.rows - 1 :]
        even = even_tile()
        mate[...] = jnp.where(even, bottom, top)
        next_[:1, :] = jnp.where(even, top, bottom)


def ghost_kernel(z, early, recv, cond, *refs):
    if z.pair:
        cond2, mate_in, next_in, steps, couple, grow, gcol, gwt, out, added, spread_a, spread_b = refs
    else:
        mate_in, next_in, steps, couple, grow, gcol, gwt, out, added, spread_a, spread_b = refs
    panel, rad, tile = lax.axis_index("panel"), lax.axis_index("rad"), lax.axis_index("ang")
    other = 1 - panel
    outer = jnp.where(rad == z.rads - 1, 1.0, 0.0)
    above, below = around(z, mate_in[...], next_in[...])

    sets = [(other, rad), (panel, rad)]
    if z.pair:
        sets.append((other, 1 - rad))
        near = [1.0]
    else:
        sets += [(other, jnp.maximum(rad - 1, 0)), (other, jnp.minimum(rad + 1, z.rads - 1))]
        near = [jnp.where(rad > 0, 1.0, 0.0), jnp.where(rad < z.rads - 1, 1.0, 0.0)]
    strips = unpack_strips(z, recv, sets)
    dif, mix = weights_of(z, steps, couple, z.rows, z.cols)
    plane = iota((SUBL, z.edge), 0)
    by_plane = jnp.zeros((SUBL, z.edge), F32)
    for f in range(z.fields):
        by_plane = jnp.where(plane == f, wide(steps[:, f : f + 1], SUBL, z.edge), by_plane)
    rim, inside = strips[0]
    rim_s = edge_scaled(z, rim, by_plane)
    home_s = edge_scaled(z, strips[1][0], by_plane)
    layers_s = [edge_scaled(z, strips[2 + k][0], by_plane) for k in range(len(near))]
    lap = edge_scaled(z, inside, by_plane) - 6.0 * rim_s
    for k, one in enumerate(near):
        lap = lap + layers_s[k] * one
    spot = iota((SUBL, z.edge), 1) % z.total_rows
    lap = lap + jnp.where(spot == 0, 0.0, pltpu.roll(rim_s, 1, 1))
    lap = lap + jnp.where(spot == z.total_rows - 1, 0.0, pltpu.roll(rim_s, z.edge - 1, 1))
    thin = [[mix[e][f][:1, : z.edge] for f in range(z.fields)] for e in range(z.fields)]
    rows = [coupled(z, thin, lambda e: rim[e : e + 1], c) for c in range(z.fields)]
    mixed = jnp.concatenate(rows + [jnp.zeros((SUBL - z.fields, z.edge), F32)], axis=0)

    g_row = [line_of(grow, q) for q in range(z.stencil)]
    g_col = [line_of(gcol, q) for q in range(z.stencil)]
    g_wt = [line_of(gwt, q) for q in range(z.stencil)]
    targets = []
    for q in range(z.stencil):
        last_one = jnp.where(g_col[q] == z.cols - 1, z.total_rows + g_row[q], -1)
        targets.append(jnp.where(g_col[q] == 0, g_row[q], last_one))
    hits = onehot(jnp.concatenate(targets, axis=1), z.edge)
    values = jnp.concatenate([home_s * g_wt[q] for q in range(z.stencil)], axis=1)
    rim_ghost = joint_dot(values, hits, 3, NT_DIMS)
    sources = z.rads * z.tiles
    pulse = []
    for k in range(z.edge_rows):
        at = other * sources * z.block + z.feat_rows + k
        pulse.append(jnp.sum(recv[pl.ds(at, sources, stride=z.block), :], axis=0, keepdims=True))
    pulse = jnp.concatenate(pulse, axis=1) * outer
    rim_first = rim + lap + mixed + rim_ghost
    rim_first = rim_first + jnp.where(iota((SUBL, z.edge), 0) == 3, pulse, 0.0)
    rim_second = rim_first * rim[z.fields : z.fields + 1] * by_plane

    row0 = tile * z.rows
    aimed = [jnp.where(iota((z.rows, z.edge), 0) == g_row[q] - row0, g_wt[q], 0.0) for q in range(z.stencil)]
    loads = [rim_s, rim_second] + ([layers_s[0]] if z.pair else [])
    stacked = []
    for load in loads:
        for f in range(z.fields):
            stacked.append(jnp.concatenate([load[f : f + 1] * aimed[q] for q in range(z.stencil)], axis=1))
    for row in (row0 - 1, row0 + z.rows):
        stacked.append(
            jnp.concatenate([rim_s * jnp.where(g_row[q] == row, g_wt[q], 0.0) for q in range(z.stencil)], axis=1)
        )
    stacked = jnp.concatenate(stacked, axis=0)
    spots = jnp.concatenate(g_col, axis=1)
    columns = onehot(spots, z.cols)
    ghost = joint_dot(stacked, columns, 2, NT_DIMS)

    def ghost_of(step, f):
        at = (step * z.fields + f) * z.rows
        return ghost[at : at + z.rows]

    force = deposit(z, recv, panel, (0, 1), spread_a, spread_b)
    at = len(loads) * z.fields * z.rows
    ghost_above, ghost_below = ghost[at : at + SUBL], ghost[at + SUBL : at + 2 * SUBL]
    own_c = cond[0, 0]
    for f in range(z.fields):
        new = ghost_of(0, f) + brim(above[f : f + 1], below[f : f + 1], z.rows)
        added[f] = new + force[1] * outer if f == 3 else new
    for f in range(z.fields):
        s = added[f] * (own_c * dif[f])
        high = ghost_above[f : f + 1] * (above[z.fields :] * dif[f][:1])
        low = ghost_below[f : f + 1] * (below[z.fields :] * dif[f][:1])
        new = early[f] + added[f] - 6.0 * s + sideways(s) + upright(s, high, low)
        new = new + coupled(z, mix, lambda e: added[e], f) + ghost_of(1, f)
        if z.pair:
            part = ghost_of(2, f)
            if f == 3:
                part = part + force[1] * (1.0 - outer)
            new = new + part * (cond2[0, 0] * dif[f])
        if f == 3:
            new = new + force[0] * outer
        out[f] = new


def brim(high, low, rows):
    sub = iota((rows, high.shape[1]), 0)
    return jnp.where(sub == 0, high, 0.0) + jnp.where(sub == rows - 1, low, 0.0)


def last_kernel(z, late, *refs):
    if z.pair:
        cond2, mate_in, next_in, mate_end, next_end, steps, out = refs
    else:
        beside, mate_in, next_in, mate_end, next_end, steps, out = refs
    above, below = around(z, mate_in[...], next_in[: mate_in.shape[0], :])
    above_end, below_end = around(z, mate_end[...], next_end[:1, :])
    for f in range(z.fields):
        high, low = above[f : f + 1], below[f : f + 1]
        if f == 3:
            high, low = high + above_end, low + below_end
        if z.pair:
            far_c = cond2[0, 0] * wide(steps[:, f : f + 1], z.rows, z.cols)
            high = high + above[z.fields + f : z.fields + f + 1] * far_c[:1]
            low = low + below[z.fields + f : z.fields + f + 1] * far_c[z.rows - 1 :]
        new = late[f] + brim(high, low, z.rows)
        out[0, f, 0] = new if z.pair else new + beside[f]


def shifted(x, axis, step):
    count = lax.axis_size(axis)
    pairs = [(i, i + step) for i in range(count) if 0 <= i + step < count]
    return lax.ppermute(x, axis, pairs)


def both_sides(x, axis):
    return shifted(x, axis, 1) + shifted(x, axis, -1)


def beside_rows(z, mate, next_, across):
    pairs, links = [], []
    for panel in range(z.panels):
        for rad in range(z.rads):
            at = (panel * z.rads + rad) * z.tiles
            there = (panel ^ 1, rad) if across == "panel" else (panel, rad ^ 1)
            other = (there[0] * z.rads + there[1]) * z.tiles
            for i in range(z.tiles):
                pairs.append((at + i, at + (i ^ 1)))
                if 0 < i < z.tiles - 1:
                    links.append((at + i, at + (i + 1 if i % 2 else i - 1)))
                else:
                    links.append((at + i, other + i))
    axes = ("panel", "rad", "ang")
    return lax.ppermute(mate, axes, pairs), lax.ppermute(next_, axes, links)


def outer_rows(z, mate, next_):
    pairs, links = [], []
    for panel in range(z.panels):
        for rad in range(z.rads):
            at = (panel * z.rads + rad) * z.tiles
            for i in range(z.tiles):
                pairs.append((at + i, at + (i ^ 1)))
                if rad < z.rads - 1:
                    links.append((at + i, at + (i ^ 1)))
                elif 0 < i < z.tiles - 1:
                    links.append((at + i, at + (i + 1 if i % 2 else i - 1)))
                else:
                    links.append((at + i, ((panel ^ 1) * z.rads + rad) * z.tiles + i))
    axes = ("panel", "rad", "ang")
    return lax.ppermute(mate, axes, pairs), lax.ppermute(next_, axes, links)


def call(kernel, shapes, scratch, args, spaces=pltpu.VMEM, room=48, aliases=None, cost=0):
    return pl.pallas_call(
        kernel,
        out_shape=[jax.ShapeDtypeStruct(shape, F32) for shape in shapes],
        in_specs=[pl.BlockSpec(memory_space=spaces)] * len(args),
        out_specs=[pl.BlockSpec(memory_space=pltpu.VMEM)] * len(shapes),
        scratch_shapes=scratch,
        input_output_aliases=aliases or {},
        cost_estimate=pl.CostEstimate(flops=0, bytes_accessed=cost, transcendentals=0) if cost else None,
        compiler_params=pltpu.CompilerParams(vmem_limit_bytes=room << 20),
    )(*args)


def body(adj, cond, diffus, couple, ghost_row, ghost_col, ghost_wt, obs_dest, obs_cell, obs_wt, misfit):
    z = Sizes(adj, obs_cell, ghost_row)
    state = (z.fields, z.rows, z.cols)
    line, lines = (SUBL, z.cols), (SUBL * (2 if z.pair else 1), z.cols)
    if z.pair:
        swap = [(0, 1), (1, 0)]
        beside = [lax.ppermute(adj, "rad", swap), lax.ppermute(cond, "rad", swap)]
    else:
        coeff = diffus[:, None, None] * cond[0, 0][None]
        beside = [both_sides(coeff * adj[0, :, 0], "rad")]
    far = beside[1:]

    given = [adj, cond, diffus, obs_dest.reshape(1, z.count), obs_cell, obs_wt, misfit]
    held = [pltpu.SMEM(x.shape, x.dtype) if x is diffus else pltpu.VMEM(x.shape, x.dtype) for x in given]
    pay, *rows = call(
        functools.partial(pack_kernel, z),
        [(z.devices, z.block, LANES), line, line],
        held + [pltpu.SemaphoreType.DMA((len(given),))],
        given,
        spaces=pltpu.HBM,
        room=64,
    )
    recv = lax.all_to_all(pay, ("panel", "rad", "ang"), split_axis=0, concat_axis=0, tiled=True)
    recv = recv.reshape(z.devices * z.block, LANES)
    rows = list(beside_rows(z, *rows, "rad"))

    steps = diffus.reshape(1, z.fields)
    if z.pair:
        beside[:1] = call(functools.partial(far_kernel, z), [state], [], [beside[0]], cost=16 << 20)
    lone = call(
        functools.partial(lone_kernel, z),
        [state] * (2 if z.pair else 1),
        [],
        [adj, cond] + (beside[:1] if z.pair else []) + [steps, couple],
    )
    args = [cond, *lone] + beside + [steps, couple]
    early, mate, next_, *first = call(
        functools.partial(early_kernel, z),
        [state, lines, lines] + ([] if z.pair else [state]),
        [pltpu.VMEM(state, F32)] * (2 if z.pair else 0),
        args,
    )
    beyond_rows = z.fields * (2 if z.pair else 1)
    links = call(
        functools.partial(link_kernel, z),
        [(beyond_rows, z.cols), (beyond_rows + 1, z.cols)],
        [],
        [cond, steps] + rows + [mate, next_],
    )
    beyond = list(beside_rows(z, *links, "rad"))
    points = z.rads * z.tiles * z.npr * LANES
    ends = 2 * (-(-z.cols // LANES // 16) * 16)
    ends = call(
        functools.partial(ends_kernel, z),
        [(1, z.cols), (2, z.cols)],
        [pltpu.VMEM((2 * ends, points), BF16), pltpu.VMEM((LANES, points), BF16)],
        [recv, cond, steps],
    )
    beyond += outer_rows(z, *ends)
    args = [early, recv, cond] + far + rows + [steps, couple]
    late, *added = call(
        functools.partial(ghost_kernel, z),
        [state] if z.pair else [state, state],
        ([pltpu.VMEM(state, F32)] if z.pair else [])
        + [pltpu.VMEM((2 * TIMES * z.hi, points), BF16), pltpu.VMEM((LOW, points), BF16)],
        args + [ghost_row, ghost_col, ghost_wt],
    )
    if not z.pair:
        far = [both_sides(coeff * (first[0] + added[0]), "rad")]
    args = [late] + far + beyond + [steps]
    (out,) = call(functools.partial(last_kernel, z), [adj.shape], [], args)
    return out


def solution(mesh):
    placed = (
        P("panel", None, "rad", "ang", None),
        P("panel", "rad", "ang", None),
        P(),
        P(),
        P(),
        P(),
        P(),
        P("panel", "rad", "ang", None),
        P("panel", "rad", None, "ang"),
        P("panel", "rad", None, "ang"),
        P("panel", "rad", None, "ang"),
    )
    return jax.shard_map(
        body,
        mesh=mesh,
        in_specs=placed,
        out_specs=P("panel", None, "rad", "ang", None),
        check_vma=False,
    )
```

```python
import functools

import jax
import jax.numpy as jnp
from jax import lax
from jax.experimental import pallas as pl
from jax.experimental.pallas import tpu as pltpu
from jax.sharding import PartitionSpec as P

LANES = 128
SUBL = 8
POINTS = 4
TIMES = 2
LOW = 256
F32 = jnp.float32
BF16 = jnp.bfloat16
NT_DIMS = (((1,), (1,)), ((), ()))


def parts_of(x, count):
    parts = []
    for _ in range(count):
        part = x.astype(BF16)
        parts.append(part)
        x = x - part.astype(F32)
    return parts


def joint_dot(x, onehot, count, dims):
    rows = x.shape[0]
    parts = [part.astype(F32) for part in parts_of(x, count)]
    spare = -(rows * count) % 16
    if spare:
        parts.append(jnp.zeros((spare, x.shape[1]), F32))
    joined = jnp.concatenate(parts, axis=0).astype(BF16)
    out = lax.dot_general(joined, onehot, dims, preferred_element_type=F32)
    return sum(out[k * rows : (k + 1) * rows] for k in range(1, count)) + out[:rows]


def iota(shape, dim):
    return lax.broadcasted_iota(jnp.int32, shape, dim)


def tall(row, height):
    tile = jnp.broadcast_to(row, (16, row.shape[1])).astype(BF16)
    return jnp.concatenate([tile] * (height // 16), axis=0)


def matches(row, height):
    return iota((height, row.shape[1]), 0).astype(F32).astype(BF16) == tall(row.astype(F32), height)


def onehot(index, height):
    within = matches(jnp.maximum(index, 0) % LANES, LANES)
    nothing = jnp.zeros(within.shape, BF16)
    blocks = [jnp.where(within, tall((index // LANES == k).astype(F32), LANES), nothing) for k in range(height // LANES)]
    return jnp.concatenate(blocks, axis=0)


class Sizes:
    def __init__(self, adj, obs_cell, ghost_row):
        self.fields, self.rows, self.cols = adj.shape[1], adj.shape[3], adj.shape[4]
        self.panels = lax.axis_size("panel")
        self.rads = lax.axis_size("rad")
        self.tiles = lax.axis_size("ang")
        self.devices = self.panels * self.rads * self.tiles
        self.total_rows = self.tiles * self.rows
        self.edge = 2 * self.total_rows
        self.count = obs_cell.shape[-1]
        self.slots = 2 * self.count // self.tiles
        self.spr = min(POINTS, LANES // self.slots)
        self.npr = POINTS // self.spr
        self.feat_rows = 2 * self.npr + 1
        self.edge_rows = self.edge // LANES
        self.block = max(self.feat_rows + 1, self.edge_rows + 2)
        self.stencil = ghost_row.shape[1]
        self.hi = self.rows * self.cols // LOW
        self.pair = self.rads == 2


def rolled(x, shift, axis):
    size = x.shape[axis]
    shift = shift % size
    return x if shift == 0 else pltpu.roll(x, shift, axis)


def pack_kernel(z, *refs):
    count = 7
    given, (pay, mate, next_), held, sems = refs[:count], refs[count : count + 3], refs[count + 3 : -1], refs[-1]
    order = (3, 4, 5, 6, 2, 1, 0)
    copies = [pltpu.make_async_copy(given[n], held[n], sems.at[n]) for n in range(count)]
    for n in order:
        copies[n].start()
    adj, cond, diffus, dest, cell, wt, misfit = held
    for n in order[:4]:
        copies[n].wait()

    owner = dest[...]
    height = max(16, z.tiles)
    mine = (iota((height, z.count), 0) == owner).astype(F32)
    earlier = (iota((z.count, z.count), 0) < iota((z.count, z.count), 1)).astype(F32)
    ranks = jnp.dot(mine.astype(BF16), earlier.astype(BF16), preferred_element_type=F32)

    where = cell[0, 0]
    weight = wt[0, 0]
    mis = misfit[0, 0]
    row = ((where.astype(F32) + 0.5) * (1.0 / z.cols)).astype(jnp.int32)
    col = where - row * z.cols
    full_row = owner * z.rows + row
    edge_at = jnp.where(col == 0, full_row, jnp.where(col == z.cols - 1, z.total_rows + full_row, -1))
    hits = onehot(jnp.concatenate([edge_at[s : s + 1] for s in range(POINTS)], axis=1), z.edge)
    value = jnp.concatenate([mis[1:2] * weight[s : s + 1] for s in range(POINTS)], axis=1)
    edge_force = joint_dot(value, hits, 3, NT_DIMS)

    rank = jnp.sum(ranks * mine, axis=0, keepdims=True)
    place = owner * LANES + rank.astype(jnp.int32)
    spread = onehot(place, z.tiles * LANES)
    code = ((col // LOW) * z.rows + row) * LOW + col % LOW
    code = code.astype(F32)
    feats = []
    for g in range(z.spr):
        picked = [weight[h * z.spr + g : h * z.spr + g + 1] for h in range(z.npr)]
        picked += [code[h * z.spr + g : h * z.spr + g + 1] for h in range(z.npr)]
        picked.append(mis[g : g + 1] if g < TIMES else jnp.zeros((1, z.count), F32))
        feats += picked
    boxed = joint_dot(jnp.concatenate(feats, axis=0), spread, 3, NT_DIMS)
    slots = boxed[: z.feat_rows]
    for g in range(1, z.spr):
        slots = slots + rolled(boxed[g * z.feat_rows : (g + 1) * z.feat_rows], g * z.slots, 1)

    for n in order[4:]:
        copies[n].wait()

    lane = iota((z.rows, LANES), 1)
    sub = iota((z.rows, LANES), 0)
    strips = []
    for side in range(2):
        acc = jnp.zeros((z.rows, LANES), F32)
        for f in range(z.fields + 1):
            for inner in range(2):
                at = inner if side == 0 else z.cols - 1 - inner
                line = adj[0, f, 0, :, at : at + 1] if f < z.fields else cond[0, 0, :, at : at + 1]
                acc = jnp.where(lane == (f * 2 + inner) * z.rows + sub, line, acc)
        strips.append(jnp.sum(acc, axis=0, keepdims=True))

    acc = jnp.zeros((z.rows, LANES), F32)
    for f in range(z.fields):
        for side in range(2):
            at = side * (z.cols - 1)
            line = adj[0, f, 0, :, at : at + 1] * cond[0, 0, :, at : at + 1] * diffus[f]
            acc = jnp.where(lane == (f * 2 + side) * z.rows + sub, line, acc)
    edges = jnp.sum(acc, axis=0, keepdims=True)

    def filled(rows):
        used = sum(row.shape[0] for row in rows)
        return rows + ([jnp.zeros((z.block - used, LANES), F32)] if used < z.block else [])

    to_own, to_other = [], []
    for t in range(z.tiles):
        to_own += filled([slots[:, t * LANES : (t + 1) * LANES], edges])
        to_other += filled([edge_force[:, k * LANES : (k + 1) * LANES] for k in range(z.edge_rows)] + strips)
    to_own, to_other = jnp.concatenate(to_own, axis=0), jnp.concatenate(to_other, axis=0)
    height = z.tiles * z.block
    for panel in range(z.panels):
        part = jnp.where(lax.axis_index("panel") == panel, to_own, to_other)
        for rad in range(z.rads):
            at = (panel * z.rads + rad) * height
            pay[at : at + height, :] = part

    for f in range(z.fields):
        mate[f : f + 1, :], next_[f : f + 1, :] = facing(adj[0, f, 0] * (cond[0, 0] * diffus[f]))
    mate[z.fields :, :], next_[z.fields :, :] = facing(cond[0, 0])


def even_tile():
    return lax.axis_index("ang") % 2 == 0


def facing(s):
    top, bottom = s[:1], s[s.shape[0] - 1 :]
    even = even_tile()
    return jnp.where(even, bottom, top), jnp.where(even, top, bottom)


def around(z, mate, next_):
    even = even_tile()
    tile = lax.axis_index("ang")
    next_ = jnp.where((tile == 0) | (tile == z.tiles - 1), 0.0, next_)
    return jnp.where(even, next_, mate), jnp.where(even, mate, next_)


def wide(value, rows, cols):
    return jnp.concatenate([jnp.broadcast_to(value, (rows, LANES))] * (cols // LANES), axis=1)


def weights_of(z, steps, couple, rows, cols):
    dif = [wide(steps[:, f : f + 1], rows, cols) for f in range(z.fields)]
    mix = [[wide(couple[e : e + 1, c : c + 1], rows, cols) for c in range(z.fields)] for e in range(z.fields)]
    return dif, mix


def unpack_strips(z, recv, sets, own):
    def base(panel, rad):
        return (panel * z.rads + rad) * z.tiles * z.block

    height = 2 * z.tiles
    stacked = []
    for panel, rad in sets:
        for side in range(2):
            stacked.append(recv[pl.ds(base(panel, rad) + z.edge_rows + side, z.tiles, stride=z.block), :])
    stacked.append(recv[pl.ds(base(*own) + z.feat_rows, z.tiles, stride=z.block), :])
    stacked = jnp.concatenate(stacked, axis=0)
    width = 2 * SUBL * z.edge
    lane = iota((LANES, width), 1)
    slot = lane // z.edge
    inner, plane = slot // SUBL, slot % SUBL
    picks = (iota((LANES, width), 0) == (plane * 2 + inner) * z.rows + lane % z.rows).astype(F32)
    moved = joint_dot(stacked, picks.astype(BF16), 3, (((1,), (0,)), ((), ())))
    lane = iota((height, z.edge), 1)
    keep = lane // z.rows == iota((height, z.edge), 0)
    out = []
    for number in range(len(sets)):
        both = []
        for inner in range(2):
            rows = []
            for f in range(z.fields + 1):
                at = (inner * SUBL + f) * z.edge
                tile = moved[number * height : (number + 1) * height, at : at + z.edge]
                rows.append(jnp.sum(jnp.where(keep, tile, 0.0), axis=0, keepdims=True))
            both.append(jnp.concatenate(rows, axis=0))
        out.append(both)
    lane = iota((z.tiles, z.edge), 1)
    side = lane // z.total_rows
    keep = (lane % z.total_rows) // z.rows == iota((z.tiles, z.edge), 0)
    rows = []
    for f in range(z.fields):
        first, last = [
            moved[len(sets) * height :, (k * SUBL + f) * z.edge : (k * SUBL + f + 1) * z.edge] for k in range(2)
        ]
        tile = jnp.where(side == 0, first, last)
        rows.append(jnp.sum(jnp.where(keep, tile, 0.0), axis=0, keepdims=True))
    rows.append(jnp.zeros((SUBL - z.fields, z.edge), F32))
    return out, jnp.concatenate(rows, axis=0)


def edge_scaled(z, values, dif):
    return values * values[z.fields : z.fields + 1] * dif


def coupled(z, mix, state, c):
    total = None
    for e in range(z.fields):
        term = state(e) * mix[e][c]
        total = term if total is None else total + term
    return total


def line_of(ref, q):
    return jnp.concatenate([ref[side, q : q + 1, :] for side in range(2)], axis=1)


def observed(z, recv, panel):
    sources = z.rads * z.tiles
    base = panel * sources * z.block
    feat = [recv[pl.ds(base + k, sources, stride=z.block), :] for k in range(z.feat_rows)]
    lane = iota((sources, LANES), 1)
    misfits = []
    for t in range(TIMES):
        mis = jnp.where(lane // z.slots == t, feat[2 * z.npr], 0.0)
        full = None
        for g in range(z.spr):
            term = rolled(mis, (g - t) * z.slots, 1)
            full = term if full is None else full + term
        misfits.append(full)
    return feat[: z.npr], [code.astype(jnp.int32) for code in feat[z.npr : 2 * z.npr]], misfits


def dealt(z, values, highs, lows, height, spread_a, spread_b):
    width = spread_b.shape[0]
    sources = highs[0].shape[0]
    zero, one = jnp.zeros((height, LANES), BF16), jnp.ones((width, LANES), BF16)
    for h in range(z.npr):
        parts = []
        for value in values[h]:
            parts += [part.astype(F32) for part in parts_of(value, 2)]
        for n in range(sources):
            at = (n * z.npr + h) * LANES
            hit = matches(highs[h][n : n + 1], height)
            for k, part in enumerate(parts):
                spread_a[k * height : (k + 1) * height, at : at + LANES] = jnp.where(hit, tall(part[n : n + 1], height), zero)
            hit = matches(lows[h][n : n + 1], width)
            spread_b[:, at : at + LANES] = jnp.where(hit, one, jnp.zeros_like(one))
    grid = lax.dot_general(spread_a[...], spread_b[...], NT_DIMS, preferred_element_type=F32)
    return [
        grid[2 * k * height : (2 * k + 1) * height] + grid[(2 * k + 1) * height : (2 * k + 2) * height]
        for k in range(len(values[0]))
    ]


def deposit(z, recv, panel, times, spread_a, spread_b):
    weights, codes, misfits = observed(z, recv, panel)
    values = [[misfits[t] * weight for t in times] for weight in weights]
    highs = [code // LOW for code in codes]
    lows = [code % LOW for code in codes]
    out = []
    for both in dealt(z, values, highs, lows, z.hi, spread_a, spread_b):
        out.append(jnp.concatenate([both[k * z.rows : (k + 1) * z.rows] for k in range(z.cols // LOW)], axis=1))
    return out


def deposit_ends(z, recv, panel, spread_a, spread_b):
    weights, codes, misfits = observed(z, recv, panel)
    values = [[misfits[1] * weight] for weight in weights]
    chunks = -(-z.cols // LANES // 16) * 16
    highs, lows = [], []
    for code in codes:
        row = (code // LOW) % z.rows
        chunk = (code // LOW) // z.rows * (LOW // LANES) + (code % LOW) // LANES
        end = jnp.where(row == z.rows - 1, chunk + chunks, -1)
        highs.append(jnp.where(row == 0, chunk, end))
        lows.append(code % LANES)
    (both,) = dealt(z, values, highs, lows, 2 * chunks, spread_a, spread_b)
    ends = [[both[e * chunks + k : e * chunks + k + 1] for k in range(z.cols // LANES)] for e in range(2)]
    return [jnp.concatenate(end, axis=1) for end in ends]


def sideways(s):
    cols = s.shape[1]
    lane = iota(s.shape, 1)
    west = jnp.where(lane == 0, 0.0, pltpu.roll(s, 1, 1))
    east = jnp.where(lane == cols - 1, 0.0, pltpu.roll(s, cols - 1, 1))
    return west + east


def upright(s, above, below):
    rows = s.shape[0]
    sub = iota(s.shape, 0)
    north = jnp.where(sub == 0, above, pltpu.roll(s, 1, 0))
    south = jnp.where(sub == rows - 1, below, pltpu.roll(s, rows - 1, 0))
    return north + south


def far_kernel(z, adj2, out):
    out[...] = adj2[0, :, 0]


def lone_kernel(z, adj, cond, *refs):
    if z.pair:
        adj2, steps, couple, first, mixed = refs
    else:
        steps, couple, first = refs
    dif, mix = weights_of(z, steps, couple, z.rows, z.cols)
    for f in range(z.fields):
        s = adj[0, f, 0] * (cond[0, 0] * dif[f])
        new = adj[0, f, 0] - 6.0 * s + sideways(s) + upright(s, 0.0, 0.0)
        first[f] = new + coupled(z, mix, lambda e: adj[0, e, 0], f)
        if z.pair:
            mixed[f] = adj2[f] + s + coupled(z, mix, lambda e: adj2[e], f)


def early_kernel(z, cond, first, *refs):
    if z.pair:
        mixed, adj2, cond2, steps, couple, out, mate, next_, own, far = refs
    else:
        beside, steps, couple, out, mate, next_, own = refs
    dif, mix = weights_of(z, steps, couple, z.rows, z.cols)
    own_c = cond[0, 0]
    far_c = cond2[0, 0] if z.pair else None
    for f in range(z.fields):
        if z.pair:
            other = adj2[f] * (far_c * dif[f])
            new = first[f] + other
            far[f] = mixed[f] - 6.0 * other + sideways(other) + upright(other, 0.0, 0.0)
            at = SUBL + f
            mate[at : at + 1, :], next_[at : at + 1, :] = facing(other)
        else:
            new = first[f] + beside[f]
        own[f] = new
        mate[f : f + 1, :], next_[f : f + 1, :] = facing(new * (own_c * dif[f]))
    for half in range(2 if z.pair else 1):
        for ref in (mate, next_):
            ref[half * SUBL + z.fields : (half + 1) * SUBL, :] = jnp.zeros((SUBL - z.fields, z.cols), F32)
    for f in range(z.fields):
        s = own[f] * (own_c * dif[f])
        new = own[f] - 6.0 * s + sideways(s) + upright(s, 0.0, 0.0)
        new = new + coupled(z, mix, lambda e: own[e], f)
        if z.pair:
            new = new + far[f] * (far_c * dif[f])
        out[f] = new


def link_kernel(z, cond, steps, mate_row, next_row, mate_in, next_in, mate, next_):
    tile = lax.axis_index("ang")
    inner = jnp.where((tile == 0) | (tile == z.tiles - 1), 0.0, 1.0)
    cond_mate, cond_next = facing(cond[0, 0])
    for f in range(z.fields):
        dif = wide(steps[:, f : f + 1], 1, z.cols)
        mate[f : f + 1, :] = mate_in[f : f + 1, :] + mate_row[f : f + 1, :] * (cond_mate * dif)
        next_[f : f + 1, :] = next_in[f : f + 1, :] + next_row[f : f + 1, :] * (cond_next * dif * inner)
        if z.pair:
            mate[z.fields + f : z.fields + f + 1, :] = mate_in[SUBL + f : SUBL + f + 1, :]
            next_[z.fields + f : z.fields + f + 1, :] = next_in[SUBL + f : SUBL + f + 1, :]
    spare = next_.shape[0] - 1
    next_[spare:, :] = jnp.zeros((1, z.cols), F32)


def is_outer(z):
    return lax.axis_index("rad") == z.rads - 1


def ends_kernel(z, recv, cond, steps, mate, next_, spread_a, spread_b):
    panel = lax.axis_index("panel")
    mate[...] = jnp.zeros_like(mate)
    next_[...] = jnp.zeros_like(next_)

    @pl.when(is_outer(z))
    def _():
        top, bottom = deposit_ends(z, recv, panel, spread_a, spread_b)
        weight = cond[0, 0] * wide(steps[:, 3:4], z.rows, z.cols)
        top = top * weight[:1]
        bottom = bottom * weight[z.rows - 1 :]
        even = even_tile()
        mate[...] = jnp.where(even, bottom, top)
        next_[:1, :] = jnp.where(even, top, bottom)


def ghost_kernel(z, early, recv, cond, *refs):
    if z.pair:
        cond2, mate_in, next_in, steps, couple, grow, gcol, gwt, out, added, spread_a, spread_b = refs
    else:
        mate_in, next_in, steps, couple, grow, gcol, gwt, out, added, spread_a, spread_b = refs
    panel, rad, tile = lax.axis_index("panel"), lax.axis_index("rad"), lax.axis_index("ang")
    other = 1 - panel
    outer = jnp.where(rad == z.rads - 1, 1.0, 0.0)
    above, below = around(z, mate_in[...], next_in[...])

    sets = [(other, rad)]
    if z.pair:
        sets.append((other, 1 - rad))
        near = [1.0]
    else:
        sets += [(other, jnp.maximum(rad - 1, 0)), (other, jnp.minimum(rad + 1, z.rads - 1))]
        near = [jnp.where(rad > 0, 1.0, 0.0), jnp.where(rad < z.rads - 1, 1.0, 0.0)]
    strips, home_s = unpack_strips(z, recv, sets, (panel, rad))
    dif, mix = weights_of(z, steps, couple, z.rows, z.cols)
    plane = iota((SUBL, z.edge), 0)
    by_plane = jnp.zeros((SUBL, z.edge), F32)
    for f in range(z.fields):
        by_plane = jnp.where(plane == f, wide(steps[:, f : f + 1], SUBL, z.edge), by_plane)
    rim, inside = strips[0]
    rim_s = edge_scaled(z, rim, by_plane)
    layers_s = [edge_scaled(z, strips[1 + k][0], by_plane) for k in range(len(near))]
    lap = edge_scaled(z, inside, by_plane) - 6.0 * rim_s
    for k, one in enumerate(near):
        lap = lap + layers_s[k] * one
    spot = iota((SUBL, z.edge), 1) % z.total_rows
    lap = lap + jnp.where(spot == 0, 0.0, pltpu.roll(rim_s, 1, 1))
    lap = lap + jnp.where(spot == z.total_rows - 1, 0.0, pltpu.roll(rim_s, z.edge - 1, 1))
    thin = [[mix[e][f][:1, : z.edge] for f in range(z.fields)] for e in range(z.fields)]
    rows = [coupled(z, thin, lambda e: rim[e : e + 1], c) for c in range(z.fields)]
    mixed = jnp.concatenate(rows + [jnp.zeros((SUBL - z.fields, z.edge), F32)], axis=0)

    g_row = [line_of(grow, q) for q in range(z.stencil)]
    g_col = [line_of(gcol, q) for q in range(z.stencil)]
    g_wt = [line_of(gwt, q) for q in range(z.stencil)]
    targets = []
    for q in range(z.stencil):
        last_one = jnp.where(g_col[q] == z.cols - 1, z.total_rows + g_row[q], -1)
        targets.append(jnp.where(g_col[q] == 0, g_row[q], last_one))
    hits = onehot(jnp.concatenate(targets, axis=1), z.edge)
    values = jnp.concatenate([home_s * g_wt[q] for q in range(z.stencil)], axis=1)
    rim_ghost = joint_dot(values, hits, 3, NT_DIMS)
    sources = z.rads * z.tiles
    pulse = []
    for k in range(z.edge_rows):
        at = other * sources * z.block + k
        pulse.append(jnp.sum(recv[pl.ds(at, sources, stride=z.block), :], axis=0, keepdims=True))
    pulse = jnp.concatenate(pulse, axis=1) * outer
    rim_first = rim + lap + mixed + rim_ghost
    rim_first = rim_first + jnp.where(iota((SUBL, z.edge), 0) == 3, pulse, 0.0)
    rim_second = rim_first * rim[z.fields : z.fields + 1] * by_plane

    row0 = tile * z.rows
    aimed = [jnp.where(iota((z.rows, z.edge), 0) == g_row[q] - row0, g_wt[q], 0.0) for q in range(z.stencil)]
    loads = [rim_s, rim_second] + ([layers_s[0]] if z.pair else [])
    stacked = []
    for load in loads:
        for f in range(z.fields):
            stacked.append(jnp.concatenate([load[f : f + 1] * aimed[q] for q in range(z.stencil)], axis=1))
    for row in (row0 - 1, row0 + z.rows):
        stacked.append(
            jnp.concatenate([rim_s * jnp.where(g_row[q] == row, g_wt[q], 0.0) for q in range(z.stencil)], axis=1)
        )
    stacked = jnp.concatenate(stacked, axis=0)
    spots = jnp.concatenate(g_col, axis=1)
    columns = onehot(spots, z.cols)
    ghost = joint_dot(stacked, columns, 2, NT_DIMS)

    def ghost_of(step, f):
        at = (step * z.fields + f) * z.rows
        return ghost[at : at + z.rows]

    force = deposit(z, recv, panel, (0, 1), spread_a, spread_b)
    at = len(loads) * z.fields * z.rows
    ghost_above, ghost_below = ghost[at : at + SUBL], ghost[at + SUBL : at + 2 * SUBL]
    own_c = cond[0, 0]
    for f in range(z.fields):
        new = ghost_of(0, f) + brim(above[f : f + 1], below[f : f + 1], z.rows)
        added[f] = new + force[1] * outer if f == 3 else new
    for f in range(z.fields):
        s = added[f] * (own_c * dif[f])
        high = ghost_above[f : f + 1] * (above[z.fields :] * dif[f][:1])
        low = ghost_below[f : f + 1] * (below[z.fields :] * dif[f][:1])
        new = early[f] + added[f] - 6.0 * s + sideways(s) + upright(s, high, low)
        new = new + coupled(z, mix, lambda e: added[e], f) + ghost_of(1, f)
        if z.pair:
            part = ghost_of(2, f)
            if f == 3:
                part = part + force[1] * (1.0 - outer)
            new = new + part * (cond2[0, 0] * dif[f])
        if f == 3:
            new = new + force[0] * outer
        out[f] = new


def brim(high, low, rows):
    sub = iota((rows, high.shape[1]), 0)
    return jnp.where(sub == 0, high, 0.0) + jnp.where(sub == rows - 1, low, 0.0)


def last_kernel(z, late, *refs):
    if z.pair:
        cond2, mate_in, next_in, mate_end, next_end, steps, out = refs
    else:
        beside, mate_in, next_in, mate_end, next_end, steps, out = refs
    above, below = around(z, mate_in[...], next_in[: mate_in.shape[0], :])
    above_end, below_end = around(z, mate_end[...], next_end[:1, :])
    for f in range(z.fields):
        high, low = above[f : f + 1], below[f : f + 1]
        if f == 3:
            high, low = high + above_end, low + below_end
        if z.pair:
            far_c = cond2[0, 0] * wide(steps[:, f : f + 1], z.rows, z.cols)
            high = high + above[z.fields + f : z.fields + f + 1] * far_c[:1]
            low = low + below[z.fields + f : z.fields + f + 1] * far_c[z.rows - 1 :]
        new = late[f] + brim(high, low, z.rows)
        out[0, f, 0] = new if z.pair else new + beside[f]


def shifted(x, axis, step):
    count = lax.axis_size(axis)
    pairs = [(i, i + step) for i in range(count) if 0 <= i + step < count]
    return lax.ppermute(x, axis, pairs)


def both_sides(x, axis):
    return shifted(x, axis, 1) + shifted(x, axis, -1)


def beside_rows(z, mate, next_, across):
    pairs, links = [], []
    for panel in range(z.panels):
        for rad in range(z.rads):
            at = (panel * z.rads + rad) * z.tiles
            there = (panel ^ 1, rad) if across == "panel" else (panel, rad ^ 1)
            other = (there[0] * z.rads + there[1]) * z.tiles
            for i in range(z.tiles):
                pairs.append((at + i, at + (i ^ 1)))
                if 0 < i < z.tiles - 1:
                    links.append((at + i, at + (i + 1 if i % 2 else i - 1)))
                else:
                    links.append((at + i, other + i))
    axes = ("panel", "rad", "ang")
    return lax.ppermute(mate, axes, pairs), lax.ppermute(next_, axes, links)


def outer_rows(z, mate, next_):
    pairs, links = [], []
    for panel in range(z.panels):
        for rad in range(z.rads):
            at = (panel * z.rads + rad) * z.tiles
            for i in range(z.tiles):
                pairs.append((at + i, at + (i ^ 1)))
                if rad < z.rads - 1:
                    links.append((at + i, at + (i ^ 1)))
                elif 0 < i < z.tiles - 1:
                    links.append((at + i, at + (i + 1 if i % 2 else i - 1)))
                else:
                    links.append((at + i, ((panel ^ 1) * z.rads + rad) * z.tiles + i))
    axes = ("panel", "rad", "ang")
    return lax.ppermute(mate, axes, pairs), lax.ppermute(next_, axes, links)


def call(kernel, shapes, scratch, args, spaces=pltpu.VMEM, room=48, aliases=None, cost=0):
    return pl.pallas_call(
        kernel,
        out_shape=[jax.ShapeDtypeStruct(shape, F32) for shape in shapes],
        in_specs=[pl.BlockSpec(memory_space=spaces)] * len(args),
        out_specs=[pl.BlockSpec(memory_space=pltpu.VMEM)] * len(shapes),
        scratch_shapes=scratch,
        input_output_aliases=aliases or {},
        cost_estimate=pl.CostEstimate(flops=0, bytes_accessed=cost, transcendentals=0) if cost else None,
        compiler_params=pltpu.CompilerParams(vmem_limit_bytes=room << 20),
    )(*args)


def body(adj, cond, diffus, couple, ghost_row, ghost_col, ghost_wt, obs_dest, obs_cell, obs_wt, misfit):
    z = Sizes(adj, obs_cell, ghost_row)
    state = (z.fields, z.rows, z.cols)
    line, lines = (SUBL, z.cols), (SUBL * (2 if z.pair else 1), z.cols)
    if z.pair:
        swap = [(0, 1), (1, 0)]
        beside = [lax.ppermute(adj, "rad", swap), lax.ppermute(cond, "rad", swap)]
    else:
        coeff = diffus[:, None, None] * cond[0, 0][None]
        beside = [both_sides(coeff * adj[0, :, 0], "rad")]
    far = beside[1:]

    given = [adj, cond, diffus, obs_dest.reshape(1, z.count), obs_cell, obs_wt, misfit]
    held = [pltpu.SMEM(x.shape, x.dtype) if x is diffus else pltpu.VMEM(x.shape, x.dtype) for x in given]
    pay, *rows = call(
        functools.partial(pack_kernel, z),
        [(z.devices * z.block, LANES), line, line],
        held + [pltpu.SemaphoreType.DMA((len(given),))],
        given,
        spaces=pltpu.HBM,
        room=64,
    )
    pay = pay.reshape(z.devices, 1, z.block * LANES)
    recv = lax.all_to_all(pay, ("panel", "rad", "ang"), split_axis=0, concat_axis=0, tiled=True)
    recv = recv.reshape(z.devices * z.block, LANES)
    rows = list(beside_rows(z, *rows, "rad"))

    steps = diffus.reshape(1, z.fields)
    if z.pair:
        beside[:1] = call(functools.partial(far_kernel, z), [state], [], [beside[0]], cost=16 << 20)
    lone = call(
        functools.partial(lone_kernel, z),
        [state] * (2 if z.pair else 1),
        [],
        [adj, cond] + (beside[:1] if z.pair else []) + [steps, couple],
    )
    args = [cond, *lone] + beside + [steps, couple]
    early, mate, next_, *first = call(
        functools.partial(early_kernel, z),
        [state, lines, lines] + ([] if z.pair else [state]),
        [pltpu.VMEM(state, F32)] * (2 if z.pair else 0),
        args,
    )
    beyond_rows = z.fields * (2 if z.pair else 1)
    links = call(
        functools.partial(link_kernel, z),
        [(beyond_rows, z.cols), (beyond_rows + 1, z.cols)],
        [],
        [cond, steps] + rows + [mate, next_],
    )
    beyond = list(beside_rows(z, *links, "rad"))
    points = z.rads * z.tiles * z.npr * LANES
    ends = 2 * (-(-z.cols // LANES // 16) * 16)
    ends = call(
        functools.partial(ends_kernel, z),
        [(1, z.cols), (2, z.cols)],
        [pltpu.VMEM((2 * ends, points), BF16), pltpu.VMEM((LANES, points), BF16)],
        [recv, cond, steps],
    )
    beyond += outer_rows(z, *ends)
    args = [early, recv, cond] + far + rows + [steps, couple]
    late, *added = call(
        functools.partial(ghost_kernel, z),
        [state] if z.pair else [state, state],
        ([pltpu.VMEM(state, F32)] if z.pair else [])
        + [pltpu.VMEM((2 * TIMES * z.hi, points), BF16), pltpu.VMEM((LOW, points), BF16)],
        args + [ghost_row, ghost_col, ghost_wt],
    )
    if not z.pair:
        far = [both_sides(coeff * (first[0] + added[0]), "rad")]
    args = [late] + far + beyond + [steps]
    (out,) = call(functools.partial(last_kernel, z), [adj.shape], [], args)
    return out


def solution(mesh):
    placed = (
        P("panel", None, "rad", "ang", None),
        P("panel", "rad", "ang", None),
        P(),
        P(),
        P(),
        P(),
        P(),
        P("panel", "rad", "ang", None),
        P("panel", "rad", None, "ang"),
        P("panel", "rad", None, "ang"),
        P("panel", "rad", None, "ang"),
    )
    return jax.shard_map(
        body,
        mesh=mesh,
        in_specs=placed,
        out_specs=P("panel", None, "rad", "ang", None),
        check_vma=False,
    )
```

```python
import functools

import jax
import jax.numpy as jnp
from jax import lax
from jax.experimental import pallas as pl
from jax.experimental.pallas import tpu as pltpu
from jax.sharding import PartitionSpec as P

LANES = 128
SUBL = 8
POINTS = 4
TIMES = 2
LOW = 256
F32 = jnp.float32
BF16 = jnp.bfloat16
NT_DIMS = (((1,), (1,)), ((), ()))


def parts_of(x, count):
    parts = []
    for _ in range(count):
        part = x.astype(BF16)
        parts.append(part)
        x = x - part.astype(F32)
    return parts


def joint_dot(x, onehot, count, dims):
    rows = x.shape[0]
    parts = [part.astype(F32) for part in parts_of(x, count)]
    spare = -(rows * count) % 16
    if spare:
        parts.append(jnp.zeros((spare, x.shape[1]), F32))
    joined = jnp.concatenate(parts, axis=0).astype(BF16)
    out = lax.dot_general(joined, onehot, dims, preferred_element_type=F32)
    return sum(out[k * rows : (k + 1) * rows] for k in range(1, count)) + out[:rows]


def iota(shape, dim):
    return lax.broadcasted_iota(jnp.int32, shape, dim)


def tall(row, height):
    tile = jnp.broadcast_to(row, (16, row.shape[1])).astype(BF16)
    return jnp.concatenate([tile] * (height // 16), axis=0)


def numbers(height, width):
    return iota((height, width), 0).astype(F32).astype(BF16)


def matches(row, height, rows=None):
    rows = numbers(height, row.shape[1]) if rows is None else rows
    return rows == tall(row.astype(F32), height)


def onehot(index, height):
    within = matches(jnp.maximum(index, 0) % LANES, LANES)
    nothing = jnp.zeros(within.shape, BF16)
    blocks = [jnp.where(within, tall((index // LANES == k).astype(F32), LANES), nothing) for k in range(height // LANES)]
    return jnp.concatenate(blocks, axis=0)


class Sizes:
    def __init__(self, adj, obs_cell, ghost_row):
        self.fields, self.rows, self.cols = adj.shape[1], adj.shape[3], adj.shape[4]
        self.panels = lax.axis_size("panel")
        self.rads = lax.axis_size("rad")
        self.tiles = lax.axis_size("ang")
        self.devices = self.panels * self.rads * self.tiles
        self.total_rows = self.tiles * self.rows
        self.edge = 2 * self.total_rows
        self.count = obs_cell.shape[-1]
        self.slots = 2 * self.count // self.tiles
        self.spr = min(POINTS, LANES // self.slots)
        self.npr = POINTS // self.spr
        self.feat_rows = 2 * self.npr + 1
        self.edge_rows = self.edge // LANES
        self.block = max(self.feat_rows + 1, self.edge_rows + 2)
        self.stencil = ghost_row.shape[1]
        self.hi = self.rows * self.cols // LOW
        self.pair = self.rads == 2


def rolled(x, shift, axis):
    size = x.shape[axis]
    shift = shift % size
    return x if shift == 0 else pltpu.roll(x, shift, axis)


def pack_kernel(z, *refs):
    count = 7
    given, (pay, mate, next_), held, sems = refs[:count], refs[count : count + 3], refs[count + 3 : -1], refs[-1]
    order = (3, 4, 5, 6, 2, 1, 0)
    copies = [pltpu.make_async_copy(given[n], held[n], sems.at[n]) for n in range(count)]
    for n in order:
        copies[n].start()
    adj, cond, diffus, dest, cell, wt, misfit = held
    for n in order[:4]:
        copies[n].wait()

    owner = dest[...]
    height = max(16, z.tiles)
    mine = (iota((height, z.count), 0) == owner).astype(F32)
    earlier = (iota((z.count, z.count), 0) < iota((z.count, z.count), 1)).astype(F32)
    ranks = jnp.dot(mine.astype(BF16), earlier.astype(BF16), preferred_element_type=F32)

    where = cell[0, 0]
    weight = wt[0, 0]
    mis = misfit[0, 0]
    row = ((where.astype(F32) + 0.5) * (1.0 / z.cols)).astype(jnp.int32)
    col = where - row * z.cols
    full_row = owner * z.rows + row
    edge_at = jnp.where(col == 0, full_row, jnp.where(col == z.cols - 1, z.total_rows + full_row, -1))
    hits = onehot(jnp.concatenate([edge_at[s : s + 1] for s in range(POINTS)], axis=1), z.edge)
    value = jnp.concatenate([mis[1:2] * weight[s : s + 1] for s in range(POINTS)], axis=1)
    edge_force = joint_dot(value, hits, 3, NT_DIMS)

    rank = jnp.sum(ranks * mine, axis=0, keepdims=True)
    place = owner * LANES + rank.astype(jnp.int32)
    spread = onehot(place, z.tiles * LANES)
    code = ((col // LOW) * z.rows + row) * LOW + col % LOW
    code = code.astype(F32)
    feats = []
    for g in range(z.spr):
        picked = [weight[h * z.spr + g : h * z.spr + g + 1] for h in range(z.npr)]
        picked += [code[h * z.spr + g : h * z.spr + g + 1] for h in range(z.npr)]
        picked.append(mis[g : g + 1] if g < TIMES else jnp.zeros((1, z.count), F32))
        feats += picked
    boxed = joint_dot(jnp.concatenate(feats, axis=0), spread, 3, NT_DIMS)
    slots = boxed[: z.feat_rows]
    for g in range(1, z.spr):
        slots = slots + rolled(boxed[g * z.feat_rows : (g + 1) * z.feat_rows], g * z.slots, 1)

    for n in order[4:]:
        copies[n].wait()

    lane = iota((z.rows, LANES), 1)
    sub = iota((z.rows, LANES), 0)
    strips = []
    for side in range(2):
        acc = jnp.zeros((z.rows, LANES), F32)
        for f in range(z.fields + 1):
            for inner in range(2):
                at = inner if side == 0 else z.cols - 1 - inner
                line = adj[0, f, 0, :, at : at + 1] if f < z.fields else cond[0, 0, :, at : at + 1]
                acc = jnp.where(lane == (f * 2 + inner) * z.rows + sub, line, acc)
        strips.append(jnp.sum(acc, axis=0, keepdims=True))

    acc = jnp.zeros((z.rows, LANES), F32)
    for f in range(z.fields):
        for side in range(2):
            at = side * (z.cols - 1)
            line = adj[0, f, 0, :, at : at + 1] * cond[0, 0, :, at : at + 1] * diffus[f]
            acc = jnp.where(lane == (f * 2 + side) * z.rows + sub, line, acc)
    edges = jnp.sum(acc, axis=0, keepdims=True)

    def filled(rows):
        used = sum(row.shape[0] for row in rows)
        return rows + ([jnp.zeros((z.block - used, LANES), F32)] if used < z.block else [])

    to_own, to_other = [], []
    for t in range(z.tiles):
        to_own += filled([slots[:, t * LANES : (t + 1) * LANES], edges])
        to_other += filled([edge_force[:, k * LANES : (k + 1) * LANES] for k in range(z.edge_rows)] + strips)
    to_own, to_other = jnp.concatenate(to_own, axis=0), jnp.concatenate(to_other, axis=0)
    height = z.tiles * z.block
    for panel in range(z.panels):
        part = jnp.where(lax.axis_index("panel") == panel, to_own, to_other)
        for rad in range(z.rads):
            at = (panel * z.rads + rad) * height
            pay[at : at + height, :] = part

    for f in range(z.fields):
        mate[f : f + 1, :], next_[f : f + 1, :] = facing(adj[0, f, 0] * (cond[0, 0] * diffus[f]))
    mate[z.fields :, :], next_[z.fields :, :] = facing(cond[0, 0])


def even_tile():
    return lax.axis_index("ang") % 2 == 0


def facing(s):
    top, bottom = s[:1], s[s.shape[0] - 1 :]
    even = even_tile()
    return jnp.where(even, bottom, top), jnp.where(even, top, bottom)


def around(z, mate, next_):
    even = even_tile()
    tile = lax.axis_index("ang")
    next_ = jnp.where((tile == 0) | (tile == z.tiles - 1), 0.0, next_)
    return jnp.where(even, next_, mate), jnp.where(even, mate, next_)


def wide(value, rows, cols):
    return jnp.concatenate([jnp.broadcast_to(value, (rows, LANES))] * (cols // LANES), axis=1)


def weights_of(z, steps, couple, rows, cols):
    dif = [wide(steps[:, f : f + 1], rows, cols) for f in range(z.fields)]
    mix = [[wide(couple[e : e + 1, c : c + 1], rows, cols) for c in range(z.fields)] for e in range(z.fields)]
    return dif, mix


def unpack_strips(z, recv, sets, own):
    def base(panel, rad):
        return (panel * z.rads + rad) * z.tiles * z.block

    height = 2 * z.tiles
    stacked = []
    for panel, rad in sets:
        for side in range(2):
            stacked.append(recv[pl.ds(base(panel, rad) + z.edge_rows + side, z.tiles, stride=z.block), :])
    stacked.append(recv[pl.ds(base(*own) + z.feat_rows, z.tiles, stride=z.block), :])
    stacked = jnp.concatenate(stacked, axis=0)
    lane = iota((1, 2 * SUBL * z.edge), 1)
    slot = lane // z.edge
    inner, plane = slot // SUBL, slot % SUBL
    picks = onehot((plane * 2 + inner) * z.rows + lane % z.rows, LANES)
    moved = joint_dot(stacked, picks, 3, (((1,), (0,)), ((), ())))
    lane = iota((height, z.edge), 1)
    keep = lane // z.rows == iota((height, z.edge), 0)
    out = []
    for number in range(len(sets)):
        both = []
        for inner in range(2):
            rows = []
            for f in range(z.fields + 1):
                at = (inner * SUBL + f) * z.edge
                tile = moved[number * height : (number + 1) * height, at : at + z.edge]
                rows.append(jnp.sum(jnp.where(keep, tile, 0.0), axis=0, keepdims=True))
            both.append(jnp.concatenate(rows, axis=0))
        out.append(both)
    lane = iota((z.tiles, z.edge), 1)
    side = lane // z.total_rows
    keep = (lane % z.total_rows) // z.rows == iota((z.tiles, z.edge), 0)
    rows = []
    for f in range(z.fields):
        first, last = [
            moved[len(sets) * height :, (k * SUBL + f) * z.edge : (k * SUBL + f + 1) * z.edge] for k in range(2)
        ]
        tile = jnp.where(side == 0, first, last)
        rows.append(jnp.sum(jnp.where(keep, tile, 0.0), axis=0, keepdims=True))
    rows.append(jnp.zeros((SUBL - z.fields, z.edge), F32))
    return out, jnp.concatenate(rows, axis=0)


def edge_scaled(z, values, dif):
    return values * values[z.fields : z.fields + 1] * dif


def coupled(z, mix, state, c):
    total = None
    for e in range(z.fields):
        term = state(e) * mix[e][c]
        total = term if total is None else total + term
    return total


def line_of(ref, q):
    return jnp.concatenate([ref[side, q : q + 1, :] for side in range(2)], axis=1)


def observed(z, recv, panel):
    sources = z.rads * z.tiles
    base = panel * sources * z.block
    feat = [recv[pl.ds(base + k, sources, stride=z.block), :] for k in range(z.feat_rows)]
    lane = iota((sources, LANES), 1)
    misfits = []
    for t in range(TIMES):
        mis = jnp.where(lane // z.slots == t, feat[2 * z.npr], 0.0)
        full = None
        for g in range(z.spr):
            term = rolled(mis, (g - t) * z.slots, 1)
            full = term if full is None else full + term
        misfits.append(full)
    return feat[: z.npr], [code.astype(jnp.int32) for code in feat[z.npr : 2 * z.npr]], misfits


def dealt(z, values, highs, lows, height, spread_a, spread_b):
    width = spread_b.shape[0]
    sources = highs[0].shape[0]
    zero, none, one = jnp.zeros((height, LANES), BF16), jnp.zeros((width, LANES), BF16), jnp.ones((width, LANES), BF16)
    rows_high, rows_low = numbers(height, LANES), numbers(width, LANES)
    for h in range(z.npr):
        parts = []
        for value in values[h]:
            parts += [part.astype(F32) for part in parts_of(value, 2)]
        for n in range(sources):
            at = (n * z.npr + h) * LANES
            hit = matches(highs[h][n : n + 1], height, rows_high)
            for k, part in enumerate(parts):
                spread_a[k * height : (k + 1) * height, at : at + LANES] = jnp.where(hit, tall(part[n : n + 1], height), zero)
            hit = matches(lows[h][n : n + 1], width, rows_low)
            spread_b[:, at : at + LANES] = jnp.where(hit, one, none)
    grid = lax.dot_general(spread_a[...], spread_b[...], NT_DIMS, preferred_element_type=F32)
    return [
        grid[2 * k * height : (2 * k + 1) * height] + grid[(2 * k + 1) * height : (2 * k + 2) * height]
        for k in range(len(values[0]))
    ]


def deposit(z, recv, panel, times, spread_a, spread_b):
    weights, codes, misfits = observed(z, recv, panel)
    values = [[misfits[t] * weight for t in times] for weight in weights]
    highs = [code // LOW for code in codes]
    lows = [code % LOW for code in codes]
    out = []
    for both in dealt(z, values, highs, lows, z.hi, spread_a, spread_b):
        out.append(jnp.concatenate([both[k * z.rows : (k + 1) * z.rows] for k in range(z.cols // LOW)], axis=1))
    return out


def deposit_ends(z, recv, panel, spread_a, spread_b):
    weights, codes, misfits = observed(z, recv, panel)
    values = [[misfits[1] * weight] for weight in weights]
    chunks = -(-z.cols // LANES // 16) * 16
    highs, lows = [], []
    for code in codes:
        row = (code // LOW) % z.rows
        chunk = (code // LOW) // z.rows * (LOW // LANES) + (code % LOW) // LANES
        end = jnp.where(row == z.rows - 1, chunk + chunks, -1)
        highs.append(jnp.where(row == 0, chunk, end))
        lows.append(code % LANES)
    (both,) = dealt(z, values, highs, lows, 2 * chunks, spread_a, spread_b)
    ends = [[both[e * chunks + k : e * chunks + k + 1] for k in range(z.cols // LANES)] for e in range(2)]
    return [jnp.concatenate(end, axis=1) for end in ends]


def sideways(s):
    cols = s.shape[1]
    lane = iota(s.shape, 1)
    west = jnp.where(lane == 0, 0.0, pltpu.roll(s, 1, 1))
    east = jnp.where(lane == cols - 1, 0.0, pltpu.roll(s, cols - 1, 1))
    return west + east


def upright(s, above, below):
    rows = s.shape[0]
    sub = iota(s.shape, 0)
    north = jnp.where(sub == 0, above, pltpu.roll(s, 1, 0))
    south = jnp.where(sub == rows - 1, below, pltpu.roll(s, rows - 1, 0))
    return north + south


def far_kernel(z, adj2, out):
    out[...] = adj2[0, :, 0]


def lone_kernel(z, adj, cond, *refs):
    if z.pair:
        adj2, steps, couple, first, mixed = refs
    else:
        steps, couple, first = refs
    dif, mix = weights_of(z, steps, couple, z.rows, z.cols)
    for f in range(z.fields):
        s = adj[0, f, 0] * (cond[0, 0] * dif[f])
        new = adj[0, f, 0] - 6.0 * s + sideways(s) + upright(s, 0.0, 0.0)
        first[f] = new + coupled(z, mix, lambda e: adj[0, e, 0], f)
        if z.pair:
            mixed[f] = adj2[f] + s + coupled(z, mix, lambda e: adj2[e], f)


def early_kernel(z, cond, first, *refs):
    if z.pair:
        mixed, adj2, cond2, steps, couple, out, mate, next_, own, far = refs
    else:
        beside, steps, couple, out, mate, next_, own = refs
    dif, mix = weights_of(z, steps, couple, z.rows, z.cols)
    own_c = cond[0, 0]
    far_c = cond2[0, 0] if z.pair else None
    for f in range(z.fields):
        if z.pair:
            other = adj2[f] * (far_c * dif[f])
            new = first[f] + other
            far[f] = mixed[f] - 6.0 * other + sideways(other) + upright(other, 0.0, 0.0)
            at = SUBL + f
            mate[at : at + 1, :], next_[at : at + 1, :] = facing(other)
        else:
            new = first[f] + beside[f]
        own[f] = new
        mate[f : f + 1, :], next_[f : f + 1, :] = facing(new * (own_c * dif[f]))
    for half in range(2 if z.pair else 1):
        for ref in (mate, next_):
            ref[half * SUBL + z.fields : (half + 1) * SUBL, :] = jnp.zeros((SUBL - z.fields, z.cols), F32)
    for f in range(z.fields):
        s = own[f] * (own_c * dif[f])
        new = own[f] - 6.0 * s + sideways(s) + upright(s, 0.0, 0.0)
        new = new + coupled(z, mix, lambda e: own[e], f)
        if z.pair:
            new = new + far[f] * (far_c * dif[f])
        out[f] = new


def link_kernel(z, cond, steps, mate_row, next_row, mate_in, next_in, mate, next_):
    tile = lax.axis_index("ang")
    inner = jnp.where((tile == 0) | (tile == z.tiles - 1), 0.0, 1.0)
    cond_mate, cond_next = facing(cond[0, 0])
    for f in range(z.fields):
        dif = wide(steps[:, f : f + 1], 1, z.cols)
        mate[f : f + 1, :] = mate_in[f : f + 1, :] + mate_row[f : f + 1, :] * (cond_mate * dif)
        next_[f : f + 1, :] = next_in[f : f + 1, :] + next_row[f : f + 1, :] * (cond_next * dif * inner)
        if z.pair:
            mate[z.fields + f : z.fields + f + 1, :] = mate_in[SUBL + f : SUBL + f + 1, :]
            next_[z.fields + f : z.fields + f + 1, :] = next_in[SUBL + f : SUBL + f + 1, :]
    spare = next_.shape[0] - 1
    next_[spare:, :] = jnp.zeros((1, z.cols), F32)


def is_outer(z):
    return lax.axis_index("rad") == z.rads - 1


def ends_kernel(z, recv, cond, steps, mate, next_, spread_a, spread_b):
    panel = lax.axis_index("panel")
    mate[...] = jnp.zeros_like(mate)
    next_[...] = jnp.zeros_like(next_)

    @pl.when(is_outer(z))
    def _():
        top, bottom = deposit_ends(z, recv, panel, spread_a, spread_b)
        weight = cond[0, 0] * wide(steps[:, 3:4], z.rows, z.cols)
        top = top * weight[:1]
        bottom = bottom * weight[z.rows - 1 :]
        even = even_tile()
        mate[...] = jnp.where(even, bottom, top)
        next_[:1, :] = jnp.where(even, top, bottom)


def ghost_kernel(z, early, recv, cond, *refs):
    if z.pair:
        cond2, mate_in, next_in, steps, couple, grow, gcol, gwt, out, added, spread_a, spread_b = refs
    else:
        mate_in, next_in, steps, couple, grow, gcol, gwt, out, added, spread_a, spread_b = refs
    panel, rad, tile = lax.axis_index("panel"), lax.axis_index("rad"), lax.axis_index("ang")
    other = 1 - panel
    outer = jnp.where(rad == z.rads - 1, 1.0, 0.0)
    above, below = around(z, mate_in[...], next_in[...])

    sets = [(other, rad)]
    if z.pair:
        sets.append((other, 1 - rad))
        near = [1.0]
    else:
        sets += [(other, jnp.maximum(rad - 1, 0)), (other, jnp.minimum(rad + 1, z.rads - 1))]
        near = [jnp.where(rad > 0, 1.0, 0.0), jnp.where(rad < z.rads - 1, 1.0, 0.0)]
    strips, home_s = unpack_strips(z, recv, sets, (panel, rad))
    dif, mix = weights_of(z, steps, couple, z.rows, z.cols)
    plane = iota((SUBL, z.edge), 0)
    by_plane = jnp.zeros((SUBL, z.edge), F32)
    for f in range(z.fields):
        by_plane = jnp.where(plane == f, wide(steps[:, f : f + 1], SUBL, z.edge), by_plane)
    rim, inside = strips[0]
    rim_s = edge_scaled(z, rim, by_plane)
    layers_s = [edge_scaled(z, strips[1 + k][0], by_plane) for k in range(len(near))]
    lap = edge_scaled(z, inside, by_plane) - 6.0 * rim_s
    for k, one in enumerate(near):
        lap = lap + layers_s[k] * one
    spot = iota((SUBL, z.edge), 1) % z.total_rows
    lap = lap + jnp.where(spot == 0, 0.0, pltpu.roll(rim_s, 1, 1))
    lap = lap + jnp.where(spot == z.total_rows - 1, 0.0, pltpu.roll(rim_s, z.edge - 1, 1))
    thin = [[mix[e][f][:1, : z.edge] for f in range(z.fields)] for e in range(z.fields)]
    rows = [coupled(z, thin, lambda e: rim[e : e + 1], c) for c in range(z.fields)]
    mixed = jnp.concatenate(rows + [jnp.zeros((SUBL - z.fields, z.edge), F32)], axis=0)

    g_row = [line_of(grow, q) for q in range(z.stencil)]
    g_col = [line_of(gcol, q) for q in range(z.stencil)]
    g_wt = [line_of(gwt, q) for q in range(z.stencil)]
    targets = []
    for q in range(z.stencil):
        last_one = jnp.where(g_col[q] == z.cols - 1, z.total_rows + g_row[q], -1)
        targets.append(jnp.where(g_col[q] == 0, g_row[q], last_one))
    hits = onehot(jnp.concatenate(targets, axis=1), z.edge)
    values = jnp.concatenate([home_s * g_wt[q] for q in range(z.stencil)], axis=1)
    rim_ghost = joint_dot(values, hits, 3, NT_DIMS)
    sources = z.rads * z.tiles
    pulse = []
    for k in range(z.edge_rows):
        at = other * sources * z.block + k
        pulse.append(jnp.sum(recv[pl.ds(at, sources, stride=z.block), :], axis=0, keepdims=True))
    pulse = jnp.concatenate(pulse, axis=1) * outer
    rim_first = rim + lap + mixed + rim_ghost
    rim_first = rim_first + jnp.where(iota((SUBL, z.edge), 0) == 3, pulse, 0.0)
    rim_second = rim_first * rim[z.fields : z.fields + 1] * by_plane

    row0 = tile * z.rows
    aimed = [jnp.where(iota((z.rows, z.edge), 0) == g_row[q] - row0, g_wt[q], 0.0) for q in range(z.stencil)]
    loads = [rim_s, rim_second] + ([layers_s[0]] if z.pair else [])
    stacked = []
    for load in loads:
        for f in range(z.fields):
            stacked.append(jnp.concatenate([load[f : f + 1] * aimed[q] for q in range(z.stencil)], axis=1))
    for row in (row0 - 1, row0 + z.rows):
        stacked.append(
            jnp.concatenate([rim_s * jnp.where(g_row[q] == row, g_wt[q], 0.0) for q in range(z.stencil)], axis=1)
        )
    stacked = jnp.concatenate(stacked, axis=0)
    spots = jnp.concatenate(g_col, axis=1)
    columns = onehot(spots, z.cols)
    ghost = joint_dot(stacked, columns, 2, NT_DIMS)

    def ghost_of(step, f):
        at = (step * z.fields + f) * z.rows
        return ghost[at : at + z.rows]

    force = deposit(z, recv, panel, (0, 1), spread_a, spread_b)
    at = len(loads) * z.fields * z.rows
    ghost_above, ghost_below = ghost[at : at + SUBL], ghost[at + SUBL : at + 2 * SUBL]
    own_c = cond[0, 0]
    for f in range(z.fields):
        new = ghost_of(0, f) + brim(above[f : f + 1], below[f : f + 1], z.rows)
        added[f] = new + force[1] * outer if f == 3 else new
    for f in range(z.fields):
        s = added[f] * (own_c * dif[f])
        high = ghost_above[f : f + 1] * (above[z.fields :] * dif[f][:1])
        low = ghost_below[f : f + 1] * (below[z.fields :] * dif[f][:1])
        new = early[f] + added[f] - 6.0 * s + sideways(s) + upright(s, high, low)
        new = new + coupled(z, mix, lambda e: added[e], f) + ghost_of(1, f)
        if z.pair:
            part = ghost_of(2, f)
            if f == 3:
                part = part + force[1] * (1.0 - outer)
            new = new + part * (cond2[0, 0] * dif[f])
        if f == 3:
            new = new + force[0] * outer
        out[f] = new


def brim(high, low, rows):
    sub = iota((rows, high.shape[1]), 0)
    return jnp.where(sub == 0, high, 0.0) + jnp.where(sub == rows - 1, low, 0.0)


def last_kernel(z, late, *refs):
    if z.pair:
        cond2, mate_in, next_in, mate_end, next_end, steps, out = refs
    else:
        beside, mate_in, next_in, mate_end, next_end, steps, out = refs
    above, below = around(z, mate_in[...], next_in[: mate_in.shape[0], :])
    above_end, below_end = around(z, mate_end[...], next_end[:1, :])
    for f in range(z.fields):
        high, low = above[f : f + 1], below[f : f + 1]
        if f == 3:
            high, low = high + above_end, low + below_end
        if z.pair:
            far_c = cond2[0, 0] * wide(steps[:, f : f + 1], z.rows, z.cols)
            high = high + above[z.fields + f : z.fields + f + 1] * far_c[:1]
            low = low + below[z.fields + f : z.fields + f + 1] * far_c[z.rows - 1 :]
        new = late[f] + brim(high, low, z.rows)
        out[0, f, 0] = new if z.pair else new + beside[f]


def shifted(x, axis, step):
    count = lax.axis_size(axis)
    pairs = [(i, i + step) for i in range(count) if 0 <= i + step < count]
    return lax.ppermute(x, axis, pairs)


def both_sides(x, axis):
    return shifted(x, axis, 1) + shifted(x, axis, -1)


def beside_rows(z, mate, next_, across):
    pairs, links = [], []
    for panel in range(z.panels):
        for rad in range(z.rads):
            at = (panel * z.rads + rad) * z.tiles
            there = (panel ^ 1, rad) if across == "panel" else (panel, rad ^ 1)
            other = (there[0] * z.rads + there[1]) * z.tiles
            for i in range(z.tiles):
                pairs.append((at + i, at + (i ^ 1)))
                if 0 < i < z.tiles - 1:
                    links.append((at + i, at + (i + 1 if i % 2 else i - 1)))
                else:
                    links.append((at + i, other + i))
    axes = ("panel", "rad", "ang")
    return lax.ppermute(mate, axes, pairs), lax.ppermute(next_, axes, links)


def outer_rows(z, mate, next_):
    pairs, links = [], []
    for panel in range(z.panels):
        for rad in range(z.rads):
            at = (panel * z.rads + rad) * z.tiles
            for i in range(z.tiles):
                pairs.append((at + i, at + (i ^ 1)))
                if rad < z.rads - 1:
                    links.append((at + i, at + (i ^ 1)))
                elif 0 < i < z.tiles - 1:
                    links.append((at + i, at + (i + 1 if i % 2 else i - 1)))
                else:
                    links.append((at + i, ((panel ^ 1) * z.rads + rad) * z.tiles + i))
    axes = ("panel", "rad", "ang")
    return lax.ppermute(mate, axes, pairs), lax.ppermute(next_, axes, links)


def call(kernel, shapes, scratch, args, spaces=pltpu.VMEM, room=48, aliases=None, cost=0):
    return pl.pallas_call(
        kernel,
        out_shape=[jax.ShapeDtypeStruct(shape, F32) for shape in shapes],
        in_specs=[pl.BlockSpec(memory_space=spaces)] * len(args),
        out_specs=[pl.BlockSpec(memory_space=pltpu.VMEM)] * len(shapes),
        scratch_shapes=scratch,
        input_output_aliases=aliases or {},
        cost_estimate=pl.CostEstimate(flops=0, bytes_accessed=cost, transcendentals=0) if cost else None,
        compiler_params=pltpu.CompilerParams(vmem_limit_bytes=room << 20),
    )(*args)


def body(adj, cond, diffus, couple, ghost_row, ghost_col, ghost_wt, obs_dest, obs_cell, obs_wt, misfit):
    z = Sizes(adj, obs_cell, ghost_row)
    state = (z.fields, z.rows, z.cols)
    line, lines = (SUBL, z.cols), (SUBL * (2 if z.pair else 1), z.cols)
    if z.pair:
        swap = [(0, 1), (1, 0)]
        beside = [lax.ppermute(adj, "rad", swap), lax.ppermute(cond, "rad", swap)]
    else:
        coeff = diffus[:, None, None] * cond[0, 0][None]
        beside = [both_sides(coeff * adj[0, :, 0], "rad")]
    far = beside[1:]

    given = [adj, cond, diffus, obs_dest.reshape(1, z.count), obs_cell, obs_wt, misfit]
    held = [pltpu.SMEM(x.shape, x.dtype) if x is diffus else pltpu.VMEM(x.shape, x.dtype) for x in given]
    pay, *rows = call(
        functools.partial(pack_kernel, z),
        [(z.devices * z.block, LANES), line, line],
        held + [pltpu.SemaphoreType.DMA((len(given),))],
        given,
        spaces=pltpu.HBM,
        room=64,
    )
    pay = pay.reshape(z.devices, 1, z.block * LANES)
    recv = lax.all_to_all(pay, ("panel", "rad", "ang"), split_axis=0, concat_axis=0, tiled=True)
    recv = recv.reshape(z.devices * z.block, LANES)
    rows = list(beside_rows(z, *rows, "rad"))

    steps = diffus.reshape(1, z.fields)
    if z.pair:
        beside[:1] = call(functools.partial(far_kernel, z), [state], [], [beside[0]], cost=16 << 20)
    lone = call(
        functools.partial(lone_kernel, z),
        [state] * (2 if z.pair else 1),
        [],
        [adj, cond] + (beside[:1] if z.pair else []) + [steps, couple],
    )
    args = [cond, *lone] + beside + [steps, couple]
    early, mate, next_, *first = call(
        functools.partial(early_kernel, z),
        [state, lines, lines] + ([] if z.pair else [state]),
        [pltpu.VMEM(state, F32)] * (2 if z.pair else 0),
        args,
    )
    beyond_rows = z.fields * (2 if z.pair else 1)
    links = call(
        functools.partial(link_kernel, z),
        [(beyond_rows, z.cols), (beyond_rows + 1, z.cols)],
        [],
        [cond, steps] + rows + [mate, next_],
    )
    beyond = list(beside_rows(z, *links, "panel"))
    points = z.rads * z.tiles * z.npr * LANES
    ends = 2 * (-(-z.cols // LANES // 16) * 16)
    ends = call(
        functools.partial(ends_kernel, z),
        [(1, z.cols), (2, z.cols)],
        [pltpu.VMEM((2 * ends, points), BF16), pltpu.VMEM((LANES, points), BF16)],
        [recv, cond, steps],
    )
    beyond += outer_rows(z, *ends)
    args = [early, recv, cond] + far + rows + [steps, couple]
    late, *added = call(
        functools.partial(ghost_kernel, z),
        [state] if z.pair else [state, state],
        ([pltpu.VMEM(state, F32)] if z.pair else [])
        + [pltpu.VMEM((2 * TIMES * z.hi, points), BF16), pltpu.VMEM((LOW, points), BF16)],
        args + [ghost_row, ghost_col, ghost_wt],
    )
    if not z.pair:
        far = [both_sides(coeff * (first[0] + added[0]), "rad")]
    args = [late] + far + beyond + [steps]
    (out,) = call(functools.partial(last_kernel, z), [adj.shape], [], args)
    return out


def solution(mesh):
    placed = (
        P("panel", None, "rad", "ang", None),
        P("panel", "rad", "ang", None),
        P(),
        P(),
        P(),
        P(),
        P(),
        P("panel", "rad", "ang", None),
        P("panel", "rad", None, "ang"),
        P("panel", "rad", None, "ang"),
        P("panel", "rad", None, "ang"),
    )
    return jax.shard_map(
        body,
        mesh=mesh,
        in_specs=placed,
        out_specs=P("panel", None, "rad", "ang", None),
        check_vma=False,
    )
```
